512 devices in a mesh: ctx: 128 (over z_lo, y, x, core), tp: 4 (over z_hi).
Axes of the slice: x: 4, y: 8, z: 8 (z_hi: 4, z_lo: 2; z = z_hi * 2 + z_lo), core: 2. Of those that a mesh axis runs over, the one named last changes fastest.
Arguments:
- activations: bfloat16 [16384, 4096], P('ctx', 'tp'), may hold values from -6 to 6
- gradients: bfloat16 [16384, 4096], P('ctx', 'tp'), may hold values from -6 to 6
- basis_act: bfloat16 [4096, 2048], P('ctx', 'tp'), may hold values from -0.09375 to 0.09375
- basis_grad: bfloat16 [4096, 2048], P('ctx', 'tp'), may hold values from -0.09375 to 0.09375
- lengths: int32 [2], replicated, may hold values from 1024 to 8192, as said below
Outputs:
- eigenvalues: float32 [2048, 2048], P('ctx', 'tp')
The draws below stay inside these ranges and needn't reach their ends.
Inputs may be any that keep to these rules, and one draw needn't show every extreme that they name: `lengths`: one sequence uses all 8192 slots in every draw.
All inputs are finite; a program needn't handle non-finite values.
Results may differ from the reference program's by a relative error of at most 0.0041.
Values may be sent and summed in bfloat16 or wider, within the bound.
No kernel may reach another device: no remote copies, remote signals or barrier semaphores. Data moves between devices by JAX's collectives and lax.ppermute only.
A program may use at most 64 MiB of HBM per device.

```python
import jax
import jax.numpy as jnp

D = 4096
KA = 2048
KG = 2048
SEQS = 2
TOKENS = 16384
LEN = 8192


def draw_lengths(key, part):
    key = jax.random.fold_in(key, 7)
    key_len, key_pick = jax.random.split(key)
    shorter = jax.random.randint(key_len, (SEQS,), LEN // 8, LEN + 1)
    chosen = jax.random.randint(key_pick, (), 0, SEQS)
    return jnp.where(jnp.arange(SEQS) == chosen, LEN, shorter).astype(jnp.int32)


def block_levels(own_key, dims, cuts, low, top_value):
    factor_of = 1.0
    for dim, shards_of in cuts:
        draws = jax.random.uniform(jax.random.fold_in(jax.random.fold_in(own_key, 6), dim), (shards_of,), jnp.float32, low / len(cuts), top_value / len(cuts))
        factor_of = factor_of * jnp.repeat(jnp.exp(draws), dims[dim] // shards_of).reshape((-1,) + (1,) * (len(dims) - 1 - dim))
    return factor_of


def centred(key, extent, deviation, most, cuts=(), kind=jnp.bfloat16):
    level = block_levels(key, extent, cuts, -0.22, 0.18) if cuts else 1.0
    array = jax.random.normal(key, extent, jnp.float32) * deviation * level
    return jnp.minimum(jnp.maximum(array, -most), most).astype(kind)


def setup_inputs(seed: int = 0) -> dict:
    keys = jax.random.split(jax.random.key(seed), 6)
    return {
        "activations": centred(keys[0], (TOKENS, D), 1.0, 6.0, ((0, 128), (1, 4))),
        "gradients": centred(keys[1], (TOKENS, D), 1.0, 6.0, ((0, 128), (1, 4))),
        "basis_act": centred(keys[2], (D, KA), D ** -0.5, 0.09375, ((0, 128), (1, 4))),
        "basis_grad": centred(keys[3], (D, KG), D ** -0.5, 0.09375, ((0, 128), (1, 4))),
        "lengths": draw_lengths(jax.random.fold_in(keys[5], 71), 0),
    }


def reference(activations, gradients, basis_act, basis_grad, lengths):
    slots = jnp.arange(TOKENS, dtype=jnp.int32)
    seq_index = slots // LEN
    position = slots % LEN
    valid = position < lengths[seq_index]
    rot_act = jnp.dot(activations, basis_act, preferred_element_type=jnp.float32)
    rot_act = jnp.where(valid[:, None], rot_act, jnp.float32(0.0)).astype(jnp.bfloat16)
    rot_grad = jnp.dot(gradients, basis_grad, preferred_element_type=jnp.float32).astype(jnp.bfloat16)
    total = jnp.zeros((KG, KA), jnp.float32)
    for step in range(SEQS):
        grad_rows = rot_grad[step * LEN:(step + 1) * LEN]
        act_rows = rot_act[step * LEN:(step + 1) * LEN]
        rotated = jnp.dot(grad_rows.T, act_rows, preferred_element_type=jnp.float32)
        total = total + rotated * rotated / lengths[step].astype(jnp.float32)
    return total / jnp.float32(SEQS)
```

```python
import jax
import jax.numpy as jnp
from jax import lax
from jax.sharding import Mesh
from jax.sharding import PartitionSpec as P

SEQS = 2
F32 = jnp.float32
BF16 = jnp.bfloat16


def gather(value, axes, count):
    copies = jnp.broadcast_to(value[None], (count, *value.shape))
    return lax.all_to_all(copies, axes, 0, 0, tiled=True)


def on_device(activations, gradients, basis_act, basis_grad, lengths):
    n_zl, n_y, n_x, n_c, n_zh = (lax.axis_size(a) for a in ("zl", "y", "x", "c", "zh"))
    n_xc, y_lo = n_x * n_c, n_y // 2
    toks, feats = activations.shape
    rows, cols = basis_act.shape
    part = cols // n_xc

    tokens = lax.all_gather(
        jnp.concatenate([activations, gradients], axis=1), ("x", "c"), axis=0, tiled=True
    )

    piece_act = basis_act.reshape(rows, n_c, n_x, part).transpose(2, 1, 0, 3)
    lines = cols // (y_lo * n_xc)
    piece_grad = basis_grad.reshape(rows, y_lo, n_x, n_c, lines).transpose(2, 3, 0, 1, 4)
    pieces = jnp.concatenate([piece_act, piece_grad.reshape(n_x, n_c, rows, part)], axis=3)
    swap = []
    for q in range(n_zh):
        for y in range(y_lo):
            for zh in range(n_zh):
                swap.append((((q * y_lo) + y) * n_zh + zh, ((zh * y_lo) + y) * n_zh + q))
    pieces = lax.ppermute(pieces, ("zl", "y", "zh"), swap)
    pieces = jnp.broadcast_to(
        pieces.reshape(1, n_xc, rows, 2 * part), (n_zl * n_y, n_xc, rows, 2 * part)
    ).reshape(n_zl * n_y * n_xc, rows, 2 * part)
    basis = lax.all_to_all(pieces, ("zl", "y", "x", "c"), 0, 0, tiled=True)
    basis = basis.reshape(n_zh, y_lo * n_xc * rows, 2 * part)

    act = jnp.einsum("kfj,tf->kjt", basis, tokens[:, :feats], preferred_element_type=F32)
    grad = jnp.einsum("kfj,tf->kjt", basis, tokens[:, feats:], preferred_element_type=F32)
    partial = jnp.concatenate([act[:, :part], grad[:, part:]], axis=1)
    partial = lax.all_to_all(partial, "zh", 0, 0, tiled=True)
    rotated = jnp.sum(partial, axis=0)
    group = toks * n_xc
    position = lax.axis_index("y") * group + jnp.arange(group, dtype=jnp.int32)
    length = jnp.where(lax.axis_index("zl") == 0, lengths[0], lengths[1])
    valid = position < length
    rot_act = jnp.where(valid[None, :], rotated[:part], F32(0.0)).astype(BF16)
    rot_grad = rotated[part:].astype(BF16)

    wide_grad = lax.all_gather(rot_grad, "zh", axis=0, tiled=True)
    wide_act = lax.all_gather(rot_act, "x", axis=0, tiled=True)
    wide_act = gather(wide_act, "c", n_c).reshape(cols, group)
    share = lax.dot_general(
        wide_grad, wide_act, (((1,), (1,)), ((), ())), preferred_element_type=F32
    )
    share = share.astype(BF16).reshape(n_zl * n_y, -1, cols)
    received = lax.all_to_all(share, ("zl", "y"), 0, 0, tiled=True)
    received = received.astype(F32).reshape(SEQS, n_y, -1, cols)
    per_seq = jnp.sum(received, axis=1)
    scale = lengths.astype(F32)[:, None, None]
    return jnp.sum(per_seq * per_seq / scale, axis=0) / F32(SEQS)


def solution(mesh):
    split = Mesh(mesh.devices.reshape(2, 8, 4, 2, 4), ("zl", "y", "x", "c", "zh"))
    spec = P(("zl", "y", "x", "c"), "zh")
    return jax.shard_map(
        on_device, mesh=split, in_specs=(spec, spec, spec, spec, P()), out_specs=spec, check_vma=False
    )
```

```python
import jax
import jax.numpy as jnp
from jax import lax
from jax.sharding import Mesh
from jax.sharding import PartitionSpec as P

SEQS = 2
F32 = jnp.float32
BF16 = jnp.bfloat16
F16 = jnp.float16
TILE = 16
TOP = 15


def on_device(activations, gradients, basis_act, basis_grad, lengths):
    n_zl, n_y, n_x, n_c, n_zh = (lax.axis_size(a) for a in ("zl", "y", "x", "c", "zh"))
    n_xc, y_lo = n_x * n_c, n_y // 2
    toks, feats = activations.shape
    rows, cols = basis_act.shape
    part = cols // n_xc

    tokens = lax.all_gather(
        jnp.concatenate([activations, gradients], axis=1), ("x", "c"), axis=0, tiled=True
    )

    piece_act = basis_act.reshape(rows, n_x, n_c, part).transpose(1, 2, 0, 3)
    lines = cols // (y_lo * n_xc)
    piece_grad = basis_grad.reshape(rows, y_lo, n_x, n_c, lines).transpose(2, 3, 0, 1, 4)
    pieces = jnp.concatenate([piece_act, piece_grad.reshape(n_x, n_c, rows, part)], axis=3)
    swap = []
    for q in range(n_zh):
        for y in range(y_lo):
            for zh in range(n_zh):
                swap.append((((q * y_lo) + y) * n_zh + zh, ((zh * y_lo) + y) * n_zh + q))
    pieces = lax.ppermute(pieces, ("zl", "y", "zh"), swap)
    pieces = jnp.broadcast_to(
        pieces.reshape(1, n_xc, rows, 2 * part), (n_zl * n_y, n_xc, rows, 2 * part)
    ).reshape(n_zl * n_y * n_xc, rows, 2 * part)
    basis = lax.all_to_all(pieces, ("zl", "y", "x", "c"), 0, 0, tiled=True)
    basis = basis.reshape(n_zh, y_lo * n_xc * rows, 2 * part)

    act = jnp.einsum("kfj,tf->kjt", basis, tokens[:, :feats], preferred_element_type=F32)
    grad = jnp.einsum("kfj,tf->kjt", basis, tokens[:, feats:], preferred_element_type=F32)
    group = toks * n_xc
    act, grad = act[:, :part], grad[:, part:]
    largest = jnp.maximum(jnp.max(jnp.abs(act)), jnp.max(jnp.abs(grad)))
    level = jnp.clip(jnp.ceil(jnp.log2(jnp.maximum(largest, F32(1e-30)))), -100.0, 100.0)
    factor = jnp.exp2(F32(TOP) - level)
    partial = jnp.concatenate(
        [
            (act * factor).astype(F16),
            (grad * factor).astype(F16),
            jnp.full((n_zh, TILE, group), level, F32).astype(F16),
        ],
        axis=1,
    )
    partial = lax.all_to_all(partial, "zh", 0, 0, tiled=True).astype(F32)
    factors = jnp.exp2(partial[:, -TILE:, :] - F32(TOP))[:, :1, :1]
    rotated = jnp.sum(partial[:, :-TILE] * factors, axis=0)
    position = lax.axis_index("y") * group + jnp.arange(group, dtype=jnp.int32)
    length = jnp.where(lax.axis_index("zl") == 0, lengths[0], lengths[1])
    valid = position < length
    rot_act = jnp.where(valid[None, :], rotated[:part], F32(0.0)).astype(BF16)
    rot_grad = rotated[part:].astype(BF16)

    wide_grad = lax.all_gather(rot_grad, "zh", axis=0, tiled=True)
    wide_act = lax.all_gather(rot_act, ("x", "c"), axis=0, tiled=True)
    share = lax.dot_general(
        wide_grad, wide_act, (((1,), (1,)), ((), ())), preferred_element_type=F32
    )
    share = share.astype(BF16).reshape(n_zl * n_y, -1, cols)
    received = lax.all_to_all(share, ("zl", "y"), 0, 0, tiled=True)
    received = received.astype(F32).reshape(SEQS, n_y, -1, cols)
    per_seq = jnp.sum(received, axis=1)
    scale = lengths.astype(F32)[:, None, None]
    return jnp.sum(per_seq * per_seq / scale, axis=0) / F32(SEQS)


def solution(mesh):
    split = Mesh(mesh.devices.reshape(2, 8, 4, 2, 4), ("zl", "y", "x", "c", "zh"))
    spec = P(("zl", "y", "x", "c"), "zh")
    return jax.shard_map(
        on_device, mesh=split, in_specs=(spec, spec, spec, spec, P()), out_specs=spec, check_vma=False
    )
```

```python
import jax
import jax.numpy as jnp
from jax import lax
from jax.sharding import Mesh
from jax.sharding import PartitionSpec as P

SEQS = 2
F32 = jnp.float32
BF16 = jnp.bfloat16
F16 = jnp.float16
TILE = 16
TOP = 15


def exchange(value, axis, partner):
    return lax.ppermute(value, axis, [(i, partner(i)) for i in range(lax.axis_size(axis))])


def swap_if(condition, value, axis):
    low, high = jnp.split(value, 2, axis=axis)
    return jnp.where(condition, jnp.concatenate([high, low], axis=axis), value)


def on_device(activations, gradients, basis_act, basis_grad, lengths):
    n_zl, n_y, n_x, n_c, n_zh = (lax.axis_size(a) for a in ("zl", "y", "x", "c", "zh"))
    zl, y, x, c = (lax.axis_index(a) for a in ("zl", "y", "x", "c"))
    n_xc, y_lo = n_x * n_c, n_y // 2
    toks, feats = activations.shape
    rows, cols = basis_act.shape
    part = cols // n_xc
    group = toks * n_xc

    piece_act = basis_act.reshape(rows, n_c, n_x, part).transpose(2, 1, 0, 3)
    lines = cols // (y_lo * n_xc)
    piece_grad = basis_grad.reshape(rows, y_lo, n_x, n_c, lines).transpose(2, 3, 0, 1, 4)
    pieces = jnp.concatenate([piece_act, piece_grad.reshape(n_x, n_c, rows, part)], axis=3)
    swap = []
    for q in range(n_zh):
        for low in range(y_lo):
            for zh in range(n_zh):
                swap.append((((q * y_lo) + low) * n_zh + zh, ((zh * y_lo) + low) * n_zh + q))
    pieces = lax.ppermute(pieces, ("zl", "y", "zh"), swap)

    own = jnp.stack([activations, gradients])
    pair = jnp.stack([own, exchange(own, "x", lambda i: i ^ 1)])
    quad = jnp.concatenate([pair, exchange(pair, "x", lambda i: n_x - 1 - i)])
    other = exchange(quad, "c", lambda i: 1 - i)

    pieces = jnp.broadcast_to(
        pieces.reshape(1, n_xc, rows, 2 * part), (n_y, n_xc, rows, 2 * part)
    ).reshape(n_y * n_xc, rows, 2 * part)
    basis = lax.all_to_all(pieces, ("y", "x", "c"), 0, 0, tiled=True)
    basis = basis.reshape(n_y // y_lo, y_lo * n_xc * rows, 2 * part)
    far_basis = exchange(basis, "zl", lambda i: 1 - i)

    def rotate(which, first, last):
        def product(columns, blocks):
            out = jnp.einsum(
                "kfj,stf->kjst", columns, blocks[:, which], preferred_element_type=F32
            )
            return out[:, first:last].reshape(-1, last - first, group // n_c)

        halves = [
            jnp.concatenate([product(b, quad), product(b, other)], axis=2)
            for b in (basis, far_basis)
        ]
        return swap_if(zl == 1, jnp.concatenate(halves, axis=0), 0)

    act = rotate(0, 0, part)
    grad = rotate(1, part, 2 * part)
    largest = jnp.maximum(jnp.max(jnp.abs(act)), jnp.max(jnp.abs(grad)))
    level = jnp.clip(jnp.ceil(jnp.log2(jnp.maximum(largest, F32(1e-30)))), -100.0, 100.0)
    factor = jnp.exp2(F32(TOP) - level)
    level = jnp.full((n_zh, TILE, group), level, F32).astype(F16)
    act = jnp.concatenate([(act * factor).astype(F16), level], axis=1)
    grad = (grad * factor).astype(F16)
    act = lax.all_to_all(act, "zh", 0, 0, tiled=True)
    act, grad = lax.optimization_barrier((act, grad))
    grad = lax.all_to_all(grad, "zh", 0, 0, tiled=True).astype(F32)
    act = act.astype(F32)
    factors = jnp.exp2(act[:, -TILE:, :] - F32(TOP))[:, :1, :1]

    def in_order(value):
        blocks = jnp.split(value, n_xc, axis=1)
        blocks = [blocks[i] for i in (0, 1, 3, 2, 4, 5, 7, 6)]
        for condition, step in ((c == 1, n_x), (x >= 2, 2), (x % 2 == 1, 1)):
            blocks = [jnp.where(condition, blocks[i ^ step], blocks[i]) for i in range(n_xc)]
        return jnp.concatenate(blocks, axis=1)

    rot_act = in_order(jnp.sum(act[:, :-TILE] * factors, axis=0))
    rot_grad = in_order(jnp.sum(grad * factors, axis=0)).astype(BF16)
    block = jnp.arange(group, dtype=jnp.int32) // toks
    block = (block % n_x) * n_c + block // n_x
    position = y * group + block * toks + jnp.arange(group, dtype=jnp.int32) % toks
    length = jnp.where(zl == 0, lengths[0], lengths[1])
    valid = position < length
    rot_act = jnp.where(valid[None, :], rot_act, F32(0.0)).astype(BF16)

    wide_act = lax.all_gather(rot_act, "x", axis=0, tiled=True)
    wide_act = lax.all_to_all(
        jnp.broadcast_to(wide_act[None], (n_c, *wide_act.shape)), "c", 0, 0, tiled=True
    ).reshape(cols, group)
    wide_grad = lax.all_gather(rot_grad, "zh", axis=0, tiled=True)
    share = lax.dot_general(
        wide_grad, wide_act, (((1,), (1,)), ((), ())), preferred_element_type=F32
    )
    share = share.astype(BF16).reshape(n_zl * n_y, -1, cols)
    received = lax.all_to_all(share, ("zl", "y"), 0, 0, tiled=True)
    received = received.astype(F32).reshape(SEQS, n_y, -1, cols)
    per_seq = jnp.sum(received, axis=1)
    scale = lengths.astype(F32)[:, None, None]
    return jnp.sum(per_seq * per_seq / scale, axis=0) / F32(SEQS)


def solution(mesh):
    split = Mesh(mesh.devices.reshape(2, 8, 4, 2, 4), ("zl", "y", "x", "c", "zh"))
    spec = P(("zl", "y", "x", "c"), "zh")
    return jax.shard_map(
        on_device, mesh=split, in_specs=(spec, spec, spec, spec, P()), out_specs=spec, check_vma=False
    )
```

```python
import jax
import jax.numpy as jnp
from jax import lax
from jax.experimental import pallas as pl
from jax.experimental.pallas import tpu as pltpu
from jax.sharding import Mesh
from jax.sharding import PartitionSpec as P

SEQS = 2
F32 = jnp.float32
BF16 = jnp.bfloat16
F16 = jnp.float16
TILE = 16
TOP = 15
XORS = (0, 1, 3, 2)


def exchange(value, axis, partner):
    return lax.ppermute(value, axis, [(i, partner(i)) for i in range(lax.axis_size(axis))])


def rotate_kernel(place, basis, far_basis, pair, far, core_pair, core_far, act, grad, most, turned):
    n_zl, n_k = 2, basis.shape[0]
    part, toks = basis.shape[2] // 2, pair.shape[2]
    x, c, zl = place[0], place[1], place[2]
    for k in range(n_zl * n_k):
        block = (basis if k < n_k else far_basis)[k % n_k].T
        turned[0, pl.ds(k * part, part)] = block[:part]
        turned[1, pl.ds(k * part, part)] = block[part:]
    largest = jnp.zeros((n_zl * n_k * part, toks), F32)
    for slot, xor in enumerate(XORS):
        mine, other = ((pair, core_pair), (far, core_far))[slot // 2]
        first = (x ^ xor) * 2
        for which, out_ref in enumerate((act, grad)):
            rows = jnp.concatenate([mine[slot % 2, which], other[slot % 2, which]], axis=0)
            out = lax.dot_general(
                turned[which], rows, (((1,), (1,)), ((), ())), preferred_element_type=F32
            )
            for half, core in enumerate((c, 1 - c)):
                value = out[:, half * toks : (half + 1) * toks]
                largest = jnp.maximum(largest, jnp.abs(value))
                lanes = pl.ds(pl.multiple_of((first + core) * toks, toks), toks)
                for k in range(n_zl * n_k):
                    column = (zl ^ (k // n_k)) * n_k + k % n_k
                    out_ref[column, :, lanes] = value[k * part : (k + 1) * part]
    most[...] = jnp.max(largest.reshape(-1, 8, toks), axis=0)


def rotate(place, basis, far_basis, *tokens):
    n_k, feats, wide = basis.shape
    toks = tokens[0].shape[2]
    n_k, part, group = 2 * n_k, wide // 2, 8 * toks
    out = jax.ShapeDtypeStruct((n_k, part, group), F32)
    vmem = pl.BlockSpec(memory_space=pltpu.VMEM)
    return pl.pallas_call(
        rotate_kernel,
        out_shape=(out, out, jax.ShapeDtypeStruct((8, toks), F32)),
        in_specs=[pl.BlockSpec(memory_space=pltpu.SMEM)] + [vmem] * 6,
        out_specs=(vmem, vmem, vmem),
        scratch_shapes=[pltpu.VMEM((2, n_k * part, feats), BF16)],
        compiler_params=pltpu.CompilerParams(vmem_limit_bytes=32 * 2**20),
        cost_estimate=pl.CostEstimate(
            flops=2 * n_k * wide * feats * group, bytes_accessed=8 * 2**20, transcendentals=0
        ),
        name="rotate",
    )(place, basis, far_basis, *tokens)


def on_device(activations, gradients, basis_act, basis_grad, lengths):
    n_zl, n_y, n_x, n_c, n_zh = (lax.axis_size(a) for a in ("zl", "y", "x", "c", "zh"))
    zl, y, x, c = (lax.axis_index(a) for a in ("zl", "y", "x", "c"))
    n_xc, y_lo = n_x * n_c, n_y // 2
    toks, feats = activations.shape
    rows, cols = basis_act.shape
    part = cols // n_xc
    group = toks * n_xc

    piece_act = basis_act.reshape(rows, n_c, n_x, part).transpose(2, 1, 0, 3)
    lines = cols // (y_lo * n_xc)
    piece_grad = basis_grad.reshape(rows, y_lo, n_x, n_c, lines).transpose(2, 3, 0, 1, 4)
    pieces = jnp.concatenate([piece_act, piece_grad.reshape(n_x, n_c, rows, part)], axis=3)
    own = jnp.stack([activations, gradients])
    pieces, own = lax.optimization_barrier((pieces.reshape(n_xc, rows, 2 * part), own))
    swap = []
    for q in range(n_zh):
        for low in range(y_lo):
            for zh in range(n_zh):
                swap.append((((q * y_lo) + low) * n_zh + zh, ((zh * y_lo) + low) * n_zh + q))
    pieces = lax.ppermute(pieces, ("zl", "y", "zh"), swap)

    near = exchange(own, "x", lambda i: i ^ 1)
    near, pieces = lax.optimization_barrier((near, pieces))
    pair = jnp.stack([own, near])
    far = exchange(pair, "x", lambda i: n_x - 1 - i)
    core_pair = exchange(pair, "c", lambda i: 1 - i)
    pieces = jnp.broadcast_to(pieces[None], (n_y, n_xc, rows, 2 * part))
    basis = lax.all_to_all(pieces.reshape(-1, rows, 2 * part), ("y", "x", "c"), 0, 0, tiled=True)
    basis = basis.reshape(n_y // y_lo, y_lo * n_xc * rows, 2 * part)
    basis, far = lax.optimization_barrier((basis, far))
    far_basis = exchange(basis, "zl", lambda i: 1 - i)
    core_far = exchange(far, "c", lambda i: 1 - i)

    place = jnp.stack([x, c, zl]).astype(jnp.int32)
    act, grad, most = rotate(place, basis, far_basis, pair, far, core_pair, core_far)
    largest = jnp.max(most)
    level = jnp.clip(jnp.ceil(jnp.log2(jnp.maximum(largest, F32(1e-30)))), -100.0, 100.0)
    factor = jnp.exp2(F32(TOP) - level)
    level = jnp.full((n_zh, TILE, group), level, F32).astype(F16)
    act = jnp.concatenate([(act * factor).astype(F16), level], axis=1)
    grad = (grad * factor).astype(F16)
    act = lax.all_to_all(act, "zh", 0, 0, tiled=True)
    act, grad = lax.optimization_barrier((act, grad))
    grad = lax.all_to_all(grad, "zh", 0, 0, tiled=True)
    act = act.astype(F32)
    factors = jnp.exp2(act[:, -TILE:, :] - F32(TOP))[:, :1, :1]
    rot_act = jnp.sum(act[:, :-TILE] * factors, axis=0)
    position = y * group + jnp.arange(group, dtype=jnp.int32)
    length = jnp.where(zl == 0, lengths[0], lengths[1])
    valid = position < length
    rot_act = jnp.where(valid[None, :], rot_act, F32(0.0)).astype(BF16)
    wide_act = lax.all_gather(rot_act, "x", axis=0, tiled=True)
    wide_act, grad = lax.optimization_barrier((wide_act, grad))
    far_act = exchange(wide_act, "c", lambda i: 1 - i)
    rot_grad = jnp.sum(grad.astype(F32) * factors, axis=0).astype(BF16)
    wide_grad = lax.all_gather(rot_grad, "zh", axis=0, tiled=True)

    def product(columns):
        return lax.dot_general(
            wide_grad, columns, (((1,), (1,)), ((), ())), preferred_element_type=F32
        ).astype(BF16)

    near_share, far_share = product(wide_act), product(far_act)
    share = jnp.concatenate(
        [jnp.where(c == 0, near_share, far_share), jnp.where(c == 0, far_share, near_share)],
        axis=1,
    )
    received = lax.all_to_all(
        share.reshape(n_zl * n_y, -1, cols), ("zl", "y"), 0, 0, tiled=True
    )
    received = received.astype(F32).reshape(SEQS, n_y, -1, cols)
    per_seq = jnp.sum(received, axis=1)
    scale = lengths.astype(F32)[:, None, None]
    return jnp.sum(per_seq * per_seq / scale, axis=0) / F32(SEQS)


def solution(mesh):
    split = Mesh(mesh.devices.reshape(2, 8, 4, 2, 4), ("zl", "y", "x", "c", "zh"))
    spec = P(("zl", "y", "x", "c"), "zh")
    return jax.shard_map(
        on_device, mesh=split, in_specs=(spec, spec, spec, spec, P()), out_specs=spec, check_vma=False
    )
```

```python
import jax
import jax.numpy as jnp
from jax import lax
from jax.experimental import pallas as pl
from jax.experimental.pallas import tpu as pltpu
from jax.sharding import Mesh
from jax.sharding import PartitionSpec as P

SEQS = 2
F32 = jnp.float32
BF16 = jnp.bfloat16
F16 = jnp.float16
TILE = 16
TOP = 15
VMEM = pl.BlockSpec(memory_space=pltpu.VMEM)
SMEM = pl.BlockSpec(memory_space=pltpu.SMEM)


def shift(value, axis, step):
    n = lax.axis_size(axis)
    return lax.ppermute(value, axis, [(i, (i + step) % n) for i in range(n)])


def spread(value, outer, n_x, inner, run):
    width = value.shape[1]
    source = lax.broadcasted_iota(jnp.int32, (width, width), 0)
    target = lax.broadcasted_iota(jnp.int32, (width, width), 1)
    at_run, at_inner = source % run, source // run % inner
    at_x, at_outer = source // (run * inner) % n_x, source // (run * inner * n_x)
    moved = ((at_x * inner + at_inner) * outer + at_outer) * run + at_run
    ones = (moved == target).astype(F32).astype(BF16)
    return jnp.dot(value, ones, preferred_element_type=F32).astype(BF16)


def prepare_kernel(y_lo, n_c, act, grad, basis_act, basis_grad, tokens, bases):
    n_x, _, toks, width = tokens.shape
    rows = basis_act.shape[0]
    both = jnp.concatenate([act[...], grad[...]], axis=0)
    both = spread(both, y_lo, n_x, n_c, width // (y_lo * n_c))
    for x in range(n_x):
        for which in range(2):
            tokens[x, which] = both[which * toks : (which + 1) * toks, x * width : (x + 1) * width]
    bases[0] = basis_act[...]
    bases[1] = spread(basis_grad[...], y_lo, n_x, 1, basis_grad.shape[1] // (y_lo * n_x))


def prepare(y_lo, n_x, n_c, act, grad, basis_act, basis_grad):
    toks, feats = act.shape
    return pl.pallas_call(
        lambda *refs: prepare_kernel(y_lo, n_c, *refs),
        out_shape=(
            jax.ShapeDtypeStruct((n_x, 2, toks, feats // n_x), BF16),
            jax.ShapeDtypeStruct((2, *basis_act.shape), BF16),
        ),
        in_specs=[VMEM] * 4,
        out_specs=(VMEM, VMEM),
        compiler_params=pltpu.CompilerParams(vmem_limit_bytes=32 * 2**20),
        cost_estimate=pl.CostEstimate(
            flops=4 * toks * feats * feats, bytes_accessed=2**20, transcendentals=0
        ),
        name="prepare",
    )(act, grad, basis_act, basis_grad)


def rotate_kernel(place, mine, up, down, far_act, far_grad, basis, core_basis, out):
    n_x, _, toks, width = mine.shape
    rows, cols = basis.shape[2], basis.shape[3]
    n_zh = 4
    per, half = basis.shape[0] // n_zh, width // 2
    zh, c = place[0], place[1]
    near, far = (pl.ds(pl.multiple_of(core * half, half), half) for core in (c, 1 - c))
    sums = []
    for which in range(2):
        total = None
        for step, block in enumerate((mine, down, None, up)):
            owner = pl.ds(((zh + step) % n_zh) * per, per)
            left = []
            for lanes in (near, far):
                if block is None:
                    piece = (far_act, far_grad)[which][:, :, lanes]
                else:
                    piece = block[:, which, :, lanes]
                left.append(piece.reshape(n_x * toks, half))
            right = [b[owner, which].reshape(per * rows, cols) for b in (basis, core_basis)]
            product = jnp.dot(
                jnp.concatenate(left, axis=1),
                jnp.concatenate(right, axis=0),
                preferred_element_type=F32,
            )
            total = product if total is None else total + product
        sums.append(total)
    largest = jnp.max(jnp.maximum(jnp.abs(sums[0]), jnp.abs(sums[1])), axis=0, keepdims=True)
    largest = jnp.max(largest, axis=1, keepdims=True)
    level = jnp.clip(jnp.ceil(jnp.log2(jnp.maximum(largest, 1e-30))), -100.0, 100.0)
    factor = jnp.exp2(F32(TOP) - level)
    group, part = n_x * toks, cols // n_x
    for x in range(n_x):
        for which in range(2):
            value = sums[which][:, x * part : (x + 1) * part] * factor
            out[x, pl.ds(which * group, group)] = value
        out[x, pl.ds(2 * group, TILE)] = jnp.broadcast_to(level, (TILE, part))


def rotate(place, *arrays):
    n_x, _, toks, width = arrays[0].shape
    cols = arrays[-1].shape[3]
    return pl.pallas_call(
        rotate_kernel,
        out_shape=jax.ShapeDtypeStruct((n_x, 2 * n_x * toks + TILE, cols // n_x), F32),
        in_specs=[SMEM] + [VMEM] * len(arrays),
        out_specs=VMEM,
        compiler_params=pltpu.CompilerParams(vmem_limit_bytes=40 * 2**20),
        cost_estimate=pl.CostEstimate(
            flops=16 * n_x * toks * width * cols, bytes_accessed=8 * 2**20, transcendentals=0
        ),
        name="rotate",
    )(place, *arrays)


def on_device(activations, gradients, basis_act, basis_grad, lengths):
    n_zl, n_y, n_x, n_c, n_zh = (lax.axis_size(a) for a in ("zl", "y", "x", "c", "zh"))
    zl, y, c, zh = (lax.axis_index(a) for a in ("zl", "y", "c", "zh"))
    toks = activations.shape[0]
    rows, cols = basis_act.shape
    part, group = cols // n_x, n_x * toks

    tokens, bases = prepare(n_y // 2, n_x, n_c, activations, gradients, basis_act, basis_grad)
    mine = lax.all_to_all(tokens, "x", 0, 0, tiled=True)
    mine, bases = lax.optimization_barrier((mine, bases))
    up, down = shift(mine, "zh", 1), shift(mine, "zh", -1)
    far_act, far_grad = shift(up[:, 0], "zh", 1), shift(down[:, 1], "zh", -1)

    copies = jnp.broadcast_to(bases[None], (n_zl * n_y, *bases.shape))
    basis = lax.all_to_all(copies, ("zl", "y"), 0, 0, tiled=True)
    core_basis = shift(basis, "c", 1)

    place = jnp.stack([zh, c]).astype(jnp.int32)
    partial = rotate(place, mine, up, down, far_act, far_grad, basis, core_basis)
    partial = lax.all_to_all(partial.astype(F16), "x", 0, 0, tiled=True).astype(F32)
    factors = jnp.exp2(partial[:, 2 * group :, :] - F32(TOP))[:, :1, :1]
    rotated = jnp.sum(partial[:, : 2 * group] * factors, axis=0)
    index = jnp.arange(group, dtype=jnp.int32)
    position = ((y * n_x + index // toks) * n_c + c) * toks + index % toks
    length = jnp.where(zl == 0, lengths[0], lengths[1])
    valid = position < length
    rot_act = jnp.where(valid[:, None], rotated[:group], F32(0.0)).astype(BF16)
    rot_grad = rotated[group:].astype(BF16)

    wide_act = lax.all_to_all(
        jnp.broadcast_to(rot_act[None], (n_x, group, part)), "x", 0, 0, tiled=True
    )
    wide_grad = lax.all_gather(rot_grad, "zh", axis=0)
    share = jnp.einsum("ktg,xta->kgxa", wide_grad, wide_act, preferred_element_type=F32)
    share = share.astype(BF16).reshape(n_zl * n_y * n_c, -1, cols)
    received = lax.all_to_all(share, ("zl", "y", "c"), 0, 0, tiled=True)
    received = received.astype(F32).reshape(SEQS, n_y * n_c, -1, cols)
    per_seq = jnp.sum(received, axis=1)
    scale = lengths.astype(F32)[:, None, None]
    return jnp.sum(per_seq * per_seq / scale, axis=0) / F32(SEQS)


def solution(mesh):
    split = Mesh(mesh.devices.reshape(2, 8, 4, 2, 4), ("zl", "y", "x", "c", "zh"))
    spec = P(("zl", "y", "x", "c"), "zh")
    return jax.shard_map(
        on_device, mesh=split, in_specs=(spec, spec, spec, spec, P()), out_specs=spec, check_vma=False
    )
```

```python
import jax
import jax.numpy as jnp
from jax import lax
from jax.experimental import pallas as pl
from jax.experimental.pallas import tpu as pltpu
from jax.sharding import Mesh
from jax.sharding import PartitionSpec as P

SEQS = 2
F32 = jnp.float32
BF16 = jnp.bfloat16
F16 = jnp.float16
TILE = 16
ROWS = 32
XORS = (0, 1, 3, 2)
TOP = 15
VMEM = pl.BlockSpec(memory_space=pltpu.VMEM)
SMEM = pl.BlockSpec(memory_space=pltpu.SMEM)


def send(value, axis, target):
    return lax.ppermute(value, axis, [(i, target(i)) for i in range(lax.axis_size(axis))])


def prepare_kernel(act_hbm, grad_hbm, act_out, grad_out, held, sems):
    copies = [
        pltpu.make_async_copy(ref, held.at[i], sems.at[i]) for i, ref in enumerate((act_hbm, grad_hbm))
    ]
    for copy in copies:
        copy.start()
    n_x, _, part = act_out.shape
    cols = held.shape[2]
    lines = part // n_x
    source = lax.broadcasted_iota(jnp.int32, (cols, cols), 0)
    target = lax.broadcasted_iota(jnp.int32, (cols, cols), 1)
    upper = source // lines
    moved = (upper % n_x * n_x + upper // n_x) * lines + source % lines
    ones = (moved == target).astype(F32).astype(BF16)
    copies[0].wait()
    for x in range(n_x):
        act_out[x] = held[0, :, x * part : (x + 1) * part]
    copies[1].wait()
    grad = jnp.dot(held[1], ones, preferred_element_type=F32).astype(BF16)
    for x in range(n_x):
        grad_out[x] = grad[:, x * part : (x + 1) * part]


def prepare(n_x, act, grad):
    rows, cols = act.shape
    hbm = pl.BlockSpec(memory_space=pl.ANY)
    out = jax.ShapeDtypeStruct((n_x, rows, cols // n_x), BF16)
    return pl.pallas_call(
        prepare_kernel,
        out_shape=(out, out),
        in_specs=[hbm, hbm],
        out_specs=(VMEM, VMEM),
        scratch_shapes=[pltpu.VMEM((2, rows, cols), BF16), pltpu.SemaphoreType.DMA((2,))],
        compiler_params=pltpu.CompilerParams(vmem_limit_bytes=32 * 2**20),
        cost_estimate=pl.CostEstimate(
            flops=2 * rows * cols * cols, bytes_accessed=2**17, transcendentals=0
        ),
        name="prepare",
    )(act, grad)


def rotate_kernel(which, place, pair, far, basis, core_basis, out, whole):
    n_k, _, part = basis.shape
    toks = pair.shape[2]
    group = 2 * pair.shape[0] * toks
    rows = ROWS
    x, c, zh = place[0], place[1], place[2]
    for k in range(n_k):
        for i in range(basis.shape[1] // rows):
            for ref, core in ((basis, c), (core_basis, 1 - c)):
                at = pl.ds(pl.multiple_of((2 * i + core) * rows, rows), rows)
                whole[at, pl.ds(k * part, part)] = ref[k, pl.ds(i * rows, rows)]
    largest = jnp.zeros((toks, n_k * part), F32)
    for slot, xor in enumerate(XORS):
        tokens = (pair, far)[slot // 2][slot % 2, which]
        value = jnp.dot(tokens, whole[...], preferred_element_type=F32)
        largest = jnp.maximum(largest, jnp.abs(value))
        at = pl.ds(pl.multiple_of((x ^ xor) * toks, toks), toks)
        for k in range(n_k):
            out[(k - zh) % n_k if which == 0 else k, at] = value[:, k * part : (k + 1) * part]
    largest = jnp.max(jnp.max(largest, axis=0, keepdims=True), axis=1, keepdims=True)
    level = jnp.clip(jnp.ceil(jnp.log2(jnp.maximum(largest, 1e-30))), -100.0, 100.0)
    factor = jnp.exp2(TOP - level)
    for k in range(n_k):
        out[k, pl.ds(0, group)] = out[k, pl.ds(0, group)] * factor
        out[k, pl.ds(group, TILE)] = jnp.broadcast_to(level, (TILE, part))


def rotate(which, place, pair, far, basis, core_basis):
    n_k, depth, part = basis.shape
    group = 4 * pair.shape[2]
    return pl.pallas_call(
        lambda *refs: rotate_kernel(which, *refs),
        out_shape=jax.ShapeDtypeStruct((n_k, group + TILE, part), F32),
        in_specs=[SMEM] + [VMEM] * 4,
        out_specs=VMEM,
        scratch_shapes=[pltpu.VMEM((2 * depth, n_k * part), BF16)],
        compiler_params=pltpu.CompilerParams(vmem_limit_bytes=32 * 2**20),
        cost_estimate=pl.CostEstimate(
            flops=4 * depth * n_k * part * group, bytes_accessed=4 * 2**20, transcendentals=0
        ),
        name="rotate",
    )(place, pair, far, basis, core_basis)


def on_device(activations, gradients, basis_act, basis_grad, lengths):
    n_zl, n_y, n_x, n_c, n_zh = (lax.axis_size(a) for a in ("zl", "y", "x", "c", "zh"))
    zl, y, x, c, zh = (lax.axis_index(a) for a in ("zl", "y", "x", "c", "zh"))
    y_lo = n_y // 2
    toks = activations.shape[0]
    rows, cols = basis_act.shape
    part, group = cols // n_x, n_x * toks

    pieces = jnp.stack(prepare(n_x, basis_act, basis_grad))
    swap = []
    for q in range(n_zh):
        for low in range(y_lo):
            for h in range(n_zh):
                swap.append((((q * y_lo) + low) * n_zh + h, ((h * y_lo) + low) * n_zh + q))
    pieces = lax.ppermute(pieces, ("zl", "y", "zh"), swap)

    own = jnp.stack([activations, gradients])
    near = send(own, "x", lambda i: i ^ 1)
    near, pieces = lax.optimization_barrier((near, pieces))
    pair = jnp.stack([own, near])
    far = send(pair, "x", lambda i: n_x - 1 - i)

    def spread(value):
        value = jnp.broadcast_to(value[None], (n_zl * n_y, *value.shape))
        value = value.reshape(-1, rows, part)
        value = lax.all_to_all(value, ("zl", "y", "x"), 0, 0, tiled=True)
        return value.reshape(n_zh, -1, part)

    def total(parts):
        sums = 0.0
        for value in parts:
            value = value.astype(F32)
            sums += value[:group] * jnp.exp2(value[group : group + 1, :1] - TOP)
        return sums

    place = jnp.stack([x, c, zh]).astype(jnp.int32)
    basis = spread(pieces[0])
    basis, far, pieces = lax.optimization_barrier((basis, far, pieces))
    core_basis = send(basis, "c", lambda i: 1 - i)
    basis_2 = spread(pieces[1])

    act = rotate(0, place, pair, far, basis, core_basis)
    parts = [act[0]]
    for step in range(1, n_zh):
        parts.append(send(act[step].astype(F16), "zh", lambda i: (i + step) % n_zh))
    index = jnp.arange(group, dtype=jnp.int32)
    position = ((y * n_x + index // toks) * n_c + c) * toks + index % toks
    valid = position < jnp.where(zl == 0, lengths[0], lengths[1])
    rot_act = jnp.where(valid[:, None], total(parts), F32(0.0)).astype(BF16)
    basis_2, rot_act = lax.optimization_barrier((basis_2, rot_act))
    core_basis_2 = send(basis_2, "c", lambda i: 1 - i)
    wide_act = lax.all_gather(rot_act, "x", axis=0)

    grad = rotate(1, place, pair, far, basis_2, core_basis_2)
    grad = lax.all_to_all(grad.astype(F16), "zh", 0, 0, tiled=True)
    rot_grad = total([grad[k] for k in range(n_zh)]).astype(BF16)
    wide_grad = lax.all_gather(rot_grad, "zh", axis=0)

    share = jnp.einsum("ktg,xta->kgxa", wide_grad, wide_act, preferred_element_type=F32)
    share = share.astype(BF16).reshape(n_zl * n_y * n_c, -1, cols)
    received = lax.all_to_all(share, ("zl", "y", "c"), 0, 0, tiled=True)
    received = received.astype(F32).reshape(SEQS, n_y * n_c, -1, cols)
    per_seq = jnp.sum(received, axis=1)
    scale = lengths.astype(F32)[:, None, None]
    return jnp.sum(per_seq * per_seq / scale, axis=0) / F32(SEQS)


def solution(mesh):
    split = Mesh(mesh.devices.reshape(2, 8, 4, 2, 4), ("zl", "y", "x", "c", "zh"))
    spec = P(("zl", "y", "x", "c"), "zh")
    return jax.shard_map(
        on_device, mesh=split, in_specs=(spec, spec, spec, spec, P()), out_specs=spec, check_vma=False
    )
```

```python
import jax
import jax.numpy as jnp
from jax import lax
from jax.experimental import pallas as pl
from jax.experimental.pallas import tpu as pltpu
from jax.sharding import Mesh
from jax.sharding import PartitionSpec as P

SEQS = 2
F32 = jnp.float32
BF16 = jnp.bfloat16
F16 = jnp.float16
TILE = 16
TOP = 15
VMEM = pl.BlockSpec(memory_space=pltpu.VMEM)
SMEM = pl.BlockSpec(memory_space=pltpu.SMEM)


def shift(value, axis, step):
    n = lax.axis_size(axis)
    return lax.ppermute(value, axis, [(i, (i + step) % n) for i in range(n)])


def spread(value, outer, n_x, inner, run):
    width = value.shape[1]
    source = lax.broadcasted_iota(jnp.int32, (width, width), 0)
    target = lax.broadcasted_iota(jnp.int32, (width, width), 1)
    at_run, at_inner = source % run, source // run % inner
    at_x, at_outer = source // (run * inner) % n_x, source // (run * inner * n_x)
    moved = ((at_x * inner + at_inner) * outer + at_outer) * run + at_run
    ones = (moved == target).astype(F32).astype(BF16)
    return jnp.dot(value, ones, preferred_element_type=F32).astype(BF16)


def prepare_kernel(y_lo, n_c, *refs):
    inputs, (tokens, bases), held, sems = refs[:4], refs[4:6], refs[6:10], refs[10]
    sorted_tokens, out_sems = refs[11:]
    copies = [
        pltpu.make_async_copy(ref, kept, sems.at[i]) for i, (ref, kept) in enumerate(zip(inputs, held))
    ]
    for copy in copies:
        copy.start()
    n_x, n_zh, _, toks, width = tokens.shape
    run = width // (y_lo * n_c)
    for copy in copies:
        copy.wait()
    for which in range(2):
        moved = spread(held[which][...], y_lo, n_x, n_c, run)
        for x in range(n_x):
            sorted_tokens[x, which] = moved[:, x * width : (x + 1) * width]
    copies = [
        pltpu.make_async_copy(sorted_tokens.at[x], tokens.at[x, zh], out_sems.at[x, zh])
        for x in range(n_x)
        for zh in range(n_zh)
    ]
    for copy in copies:
        copy.start()
    bases[0] = held[2][...]
    bases[1] = spread(held[3][...], y_lo, n_x, 1, bases.shape[2] // (y_lo * n_x))
    for copy in copies:
        copy.wait()


def prepare(y_lo, n_x, n_c, n_zh, *arrays):
    toks, feats = arrays[0].shape
    return pl.pallas_call(
        lambda *refs: prepare_kernel(y_lo, n_c, *refs),
        out_shape=(
            jax.ShapeDtypeStruct((n_x, n_zh, 2, toks, feats // n_x), BF16),
            jax.ShapeDtypeStruct((2, *arrays[2].shape), BF16),
        ),
        in_specs=[pl.BlockSpec(memory_space=pl.ANY)] * 4,
        out_specs=(pl.BlockSpec(memory_space=pl.ANY), VMEM),
        scratch_shapes=[
            *[pltpu.VMEM(a.shape, BF16) for a in arrays],
            pltpu.SemaphoreType.DMA((4,)),
            pltpu.VMEM((n_x, 2, toks, feats // n_x), BF16),
            pltpu.SemaphoreType.DMA((n_x, n_zh)),
        ],
        compiler_params=pltpu.CompilerParams(vmem_limit_bytes=60 * 2**20),
        cost_estimate=pl.CostEstimate(
            flops=4 * toks * feats * feats, bytes_accessed=2**20, transcendentals=0
        ),
        name="prepare",
    )(*arrays)


def rotate_kernel(place, tokens, basis, far_basis, core_basis, core_far_basis, out):
    n_x, n_zh, _, toks, width = tokens.shape
    n_y, _, rows, cols = basis.shape
    per, half = n_y * 2 // n_zh, width // 2
    zl, c = place[0], place[1]
    near, far = (pl.ds(pl.multiple_of(core * half, half), half) for core in (c, 1 - c))
    sums = []
    for which in range(2):
        total = None
        for side, bases in ((zl, (basis, core_basis)), (1 - zl, (far_basis, core_far_basis))):
            for upper in range(n_y // per):
                owner = side * (n_y // per) + upper
                left = [
                    tokens[:, owner, which, :, lanes].reshape(n_x * toks, half)
                    for lanes in (near, far)
                ]
                right = [
                    ref[upper * per : (upper + 1) * per, which].reshape(per * rows, cols)
                    for ref in bases
                ]
                product = jnp.dot(
                    jnp.concatenate(left, axis=1),
                    jnp.concatenate(right, axis=0),
                    preferred_element_type=F32,
                )
                total = product if total is None else total + product
        sums.append(total)
    largest = jnp.max(jnp.maximum(jnp.abs(sums[0]), jnp.abs(sums[1])), axis=0, keepdims=True)
    largest = jnp.max(largest, axis=1, keepdims=True)
    level = jnp.clip(jnp.ceil(jnp.log2(jnp.maximum(largest, 1e-30))), -100.0, 100.0)
    factor = jnp.exp2(F32(TOP) - level)
    group, part = n_x * toks, cols // n_x
    for x in range(n_x):
        for which in range(2):
            value = sums[which][:, x * part : (x + 1) * part] * factor
            out[x, pl.ds(which * group, group)] = value
        out[x, pl.ds(2 * group, TILE)] = jnp.broadcast_to(level, (TILE, part))


def rotate(place, *arrays):
    n_x, n_zh, _, toks, width = arrays[0].shape
    cols = arrays[-1].shape[3]
    return pl.pallas_call(
        rotate_kernel,
        out_shape=jax.ShapeDtypeStruct((n_x, 2 * n_x * toks + TILE, cols // n_x), F32),
        in_specs=[SMEM] + [VMEM] * len(arrays),
        out_specs=VMEM,
        compiler_params=pltpu.CompilerParams(vmem_limit_bytes=40 * 2**20),
        cost_estimate=pl.CostEstimate(
            flops=4 * n_x * n_zh * toks * width * cols, bytes_accessed=8 * 2**20, transcendentals=0
        ),
        name="rotate",
    )(place, *arrays)


def on_device(activations, gradients, basis_act, basis_grad, lengths):
    n_zl, n_y, n_x, n_c, n_zh = (lax.axis_size(a) for a in ("zl", "y", "x", "c", "zh"))
    zl, y, c = (lax.axis_index(a) for a in ("zl", "y", "c"))
    toks = activations.shape[0]
    cols = basis_act.shape[1]
    part, group = cols // n_x, n_x * toks

    tokens, bases = prepare(n_y // 2, n_x, n_c, n_zh, activations, gradients, basis_act, basis_grad)
    tokens = lax.all_to_all(
        tokens.reshape(n_x * n_zh, *tokens.shape[2:]), ("x", "zh"), 0, 0, tiled=True
    ).reshape(tokens.shape)

    basis = lax.all_gather(bases, "y", axis=0)
    far_basis = shift(basis, "zl", 1)
    core_basis = shift(basis, "c", 1)
    core_far_basis = shift(far_basis, "c", 1)

    place = jnp.stack([zl, c]).astype(jnp.int32)
    partial = rotate(place, tokens, basis, far_basis, core_basis, core_far_basis)
    partial = lax.all_to_all(partial.astype(F16), "x", 0, 0, tiled=True).astype(F32)
    factors = jnp.exp2(partial[:, None, 2 * group :] - F32(TOP))
    partial = partial[:, : 2 * group].reshape(n_x, 2 * group // TILE, TILE, part)
    rotated = jnp.sum(partial * factors, axis=0).reshape(2 * group, part)
    index = jnp.arange(group, dtype=jnp.int32)
    position = ((y * n_x + index // toks) * n_c + c) * toks + index % toks
    length = jnp.where(zl == 0, lengths[0], lengths[1])
    valid = position < length
    rot_act = jnp.where(valid[:, None], rotated[:group], F32(0.0)).astype(BF16)
    rot_grad = rotated[group:].astype(BF16)

    wide_act = lax.all_to_all(
        jnp.broadcast_to(rot_act[None], (n_x, group, part)), "x", 0, 0, tiled=True
    )
    wide_grad = lax.all_gather(rot_grad, "zh", axis=0)
    share = jnp.einsum("ktg,xta->kgxa", wide_grad, wide_act, preferred_element_type=F32)
    share = share.astype(BF16).reshape(n_zl * n_y * n_c, -1, cols)
    received = lax.all_to_all(share, ("zl", "y", "c"), 0, 0, tiled=True)
    received = received.astype(F32).reshape(SEQS, n_y * n_c, -1, cols)
    per_seq = jnp.sum(received, axis=1)
    scale = lengths.astype(F32)[:, None, None]
    return jnp.sum(per_seq * per_seq / scale, axis=0) / F32(SEQS)


def solution(mesh):
    split = Mesh(mesh.devices.reshape(2, 8, 4, 2, 4), ("zl", "y", "x", "c", "zh"))
    spec = P(("zl", "y", "x", "c"), "zh")
    return jax.shard_map(
        on_device, mesh=split, in_specs=(spec, spec, spec, spec, P()), out_specs=spec, check_vma=False
    )
```

```python
import jax
import jax.numpy as jnp
from jax import lax
from jax.experimental import pallas as pl
from jax.experimental.pallas import tpu as pltpu
from jax.sharding import Mesh
from jax.sharding import PartitionSpec as P

SEQS = 2
F32 = jnp.float32
BF16 = jnp.bfloat16
F16 = jnp.float16
TILE = 16
TOP = 15
VMEM = pl.BlockSpec(memory_space=pltpu.VMEM)
SMEM = pl.BlockSpec(memory_space=pltpu.SMEM)


def shift(value, axis, step):
    n = lax.axis_size(axis)
    return lax.ppermute(value, axis, [(i, (i + step) % n) for i in range(n)])


def sorting(width, outer, n_x, inner):
    run = width // (outer * n_x * inner)
    source = lax.broadcasted_iota(jnp.int32, (width, width), 0)
    target = lax.broadcasted_iota(jnp.int32, (width, width), 1)
    at_run, at_inner = source % run, source // run % inner
    at_x, at_outer = source // (run * inner) % n_x, source // (run * inner * n_x)
    moved = ((at_x * inner + at_inner) * outer + at_outer) * run + at_run
    return (moved == target).astype(F32).astype(BF16)


def spread(value, ones):
    return jnp.dot(value, ones, preferred_element_type=F32).astype(BF16)


def prepare_kernel(y_lo, n_c, *refs):
    inputs, (tokens, bases), held, sems = refs[:4], refs[4:6], refs[6:10], refs[10]
    sorted_tokens, out_sems = refs[11:]
    copies = [
        pltpu.make_async_copy(ref, kept, sems.at[i]) for i, (ref, kept) in enumerate(zip(inputs, held))
    ]
    for copy in copies:
        copy.start()
    n_x, n_zh, _, toks, width = tokens.shape
    cols = bases.shape[2]
    by_x = sorting(n_x * width, y_lo, n_x, n_c)
    by_owner = sorting(cols, y_lo, n_x, n_c)
    for copy in copies:
        copy.wait()
    both = jnp.concatenate([held[0][...], held[1][...]], axis=0)
    sent = []
    for x in range(n_x):
        moved = spread(both, by_x[:, x * width : (x + 1) * width])
        for which in range(2):
            sorted_tokens[x, which] = moved[which * toks : (which + 1) * toks]
        for zh in range(n_zh):
            sent.append(
                pltpu.make_async_copy(sorted_tokens.at[x], tokens.at[x, zh], out_sems.at[x, zh])
            )
            sent[-1].start()
    bases[0] = held[2][...]
    bases[1] = spread(held[3][...], by_owner)
    for copy in sent:
        copy.wait()


def prepare(y_lo, n_x, n_c, n_zh, *arrays):
    toks, feats = arrays[0].shape
    return pl.pallas_call(
        lambda *refs: prepare_kernel(y_lo, n_c, *refs),
        out_shape=(
            jax.ShapeDtypeStruct((n_x, n_zh, 2, toks, feats // n_x), BF16),
            jax.ShapeDtypeStruct((2, *arrays[2].shape), BF16),
        ),
        in_specs=[pl.BlockSpec(memory_space=pl.ANY)] * 4,
        out_specs=(pl.BlockSpec(memory_space=pl.ANY), VMEM),
        scratch_shapes=[
            *[pltpu.VMEM(a.shape, BF16) for a in arrays],
            pltpu.SemaphoreType.DMA((4,)),
            pltpu.VMEM((n_x, 2, toks, feats // n_x), BF16),
            pltpu.SemaphoreType.DMA((n_x, n_zh)),
        ],
        compiler_params=pltpu.CompilerParams(vmem_limit_bytes=60 * 2**20),
        cost_estimate=pl.CostEstimate(
            flops=4 * toks * feats * feats, bytes_accessed=2**20, transcendentals=0
        ),
        name="prepare",
    )(*arrays)


def rotate_kernel(place, tokens, basis, far_basis, core_basis, core_far_basis, out):
    n_x, n_zh, _, toks, width = tokens.shape
    n_y, _, rows, cols = basis.shape
    per, half = n_y * 2 // n_zh, width // 2
    zl, c = place[0], place[1]
    near, far = (pl.ds(pl.multiple_of(core * half, half), half) for core in (c, 1 - c))
    sums = []
    for which in range(2):
        total = None
        for side, bases in ((zl, (basis, core_basis)), (1 - zl, (far_basis, core_far_basis))):
            for upper in range(n_y // per):
                owner = side * (n_y // per) + upper
                left = [
                    tokens[:, owner, which, :, lanes].reshape(n_x * toks, half)
                    for lanes in (near, far)
                ]
                right = [
                    ref[upper * per : (upper + 1) * per, which].reshape(per * rows, cols)
                    for ref in bases
                ]
                product = jnp.dot(
                    jnp.concatenate(left, axis=1),
                    jnp.concatenate(right, axis=0),
                    preferred_element_type=F32,
                )
                total = product if total is None else total + product
        sums.append(total)
    largest = jnp.max(jnp.maximum(jnp.abs(sums[0]), jnp.abs(sums[1])), axis=0, keepdims=True)
    largest = jnp.max(largest, axis=1, keepdims=True)
    level = jnp.clip(jnp.ceil(jnp.log2(jnp.maximum(largest, 1e-30))), -100.0, 100.0)
    factor = jnp.exp2(F32(TOP) - level)
    group, part = n_x * toks, cols // n_x
    for x in range(n_x):
        for which in range(2):
            value = sums[which][:, x * part : (x + 1) * part] * factor
            out[x, pl.ds(which * group, group)] = value
        out[x, pl.ds(2 * group, TILE)] = jnp.broadcast_to(level, (TILE, part))


def rotate(place, *arrays):
    n_x, n_zh, _, toks, width = arrays[0].shape
    cols = arrays[-1].shape[3]
    return pl.pallas_call(
        rotate_kernel,
        out_shape=jax.ShapeDtypeStruct((n_x, 2 * n_x * toks + TILE, cols // n_x), F32),
        in_specs=[SMEM] + [VMEM] * len(arrays),
        out_specs=VMEM,
        compiler_params=pltpu.CompilerParams(vmem_limit_bytes=40 * 2**20),
        cost_estimate=pl.CostEstimate(
            flops=4 * n_x * n_zh * toks * width * cols, bytes_accessed=8 * 2**20, transcendentals=0
        ),
        name="rotate",
    )(place, *arrays)


def share_kernel(grad, act, out):
    n_k, _, part = grad.shape
    n_x, n_c = act.shape[:2]
    half = part // n_c
    turned = [grad[k].T for k in range(n_k)]
    total = None
    for core in range(n_c):
        left = jnp.concatenate([t[core * half : (core + 1) * half] for t in turned], axis=0)
        right = jnp.concatenate([act[x, core] for x in range(n_x)], axis=1)
        product = jnp.dot(left, right, preferred_element_type=F32)
        total = product if total is None else total + product
    out[...] = total.astype(BF16)


def share_of(grad, act):
    n_k, group, part = grad.shape
    n_x, n_c = act.shape[:2]
    rows, cols = n_k * part // n_c, n_x * part
    return pl.pallas_call(
        share_kernel,
        out_shape=jax.ShapeDtypeStruct((rows, cols), BF16),
        in_specs=[VMEM, VMEM],
        out_specs=VMEM,
        compiler_params=pltpu.CompilerParams(vmem_limit_bytes=32 * 2**20),
        cost_estimate=pl.CostEstimate(
            flops=2 * n_c * rows * cols * group, bytes_accessed=2 * 2**20, transcendentals=0
        ),
        name="share",
    )(grad, act)


def on_device(activations, gradients, basis_act, basis_grad, lengths):
    n_zl, n_y, n_x, n_c, n_zh = (lax.axis_size(a) for a in ("zl", "y", "x", "c", "zh"))
    zl, y, c = (lax.axis_index(a) for a in ("zl", "y", "c"))
    toks = activations.shape[0]
    cols = basis_act.shape[1]
    part, group = cols // n_x, n_x * toks

    tokens, bases = prepare(n_y // 2, n_x, n_c, n_zh, activations, gradients, basis_act, basis_grad)
    far_bases = shift(bases, "zl", 1)
    tokens = lax.all_to_all(
        tokens.reshape(n_x * n_zh, *tokens.shape[2:]), ("x", "zh"), 0, 0, tiled=True
    ).reshape(tokens.shape)

    basis = lax.all_gather(bases, "y", axis=0)
    core_basis = shift(basis, "c", 1)
    far_basis = lax.all_gather(far_bases, "y", axis=0)
    core_far_basis = shift(far_basis, "c", 1)

    place = jnp.stack([zl, c]).astype(jnp.int32)
    partial = rotate(place, tokens, basis, far_basis, core_basis, core_far_basis)
    partial = lax.all_to_all(partial.astype(F16), "x", 0, 0, tiled=True).astype(F32)
    factors = jnp.exp2(partial[:, None, 2 * group :] - F32(TOP))
    partial = partial[:, : 2 * group].reshape(n_x, 2 * group // TILE, TILE, part)
    rotated = jnp.sum(partial * factors, axis=0).reshape(2 * group, part)
    index = jnp.arange(group, dtype=jnp.int32)
    position = ((y * n_x + index // toks) * n_c + c) * toks + index % toks
    length = jnp.where(zl == 0, lengths[0], lengths[1])
    valid = position < length
    rot_act = jnp.where(valid[:, None], rotated[:group], F32(0.0)).astype(BF16)
    mine = jnp.stack([rot_act, rotated[group:].astype(BF16)])
    other = shift(mine, "c", 1)

    lane = jnp.arange(part, dtype=jnp.int32)
    rot_grad = jnp.where(lane // (part // n_c) == c, mine[1], jnp.roll(other[1], part // n_c, axis=1))
    both_act = jnp.where(c == 0, jnp.stack([mine[0], other[0]]), jnp.stack([other[0], mine[0]]))
    wide_act = lax.all_to_all(
        jnp.broadcast_to(both_act[None], (n_x, *both_act.shape)), "x", 0, 0, tiled=True
    )
    wide_grad = lax.all_gather(rot_grad, "zh", axis=0)
    share = share_of(wide_grad, wide_act).reshape(n_zl * n_y, -1, cols)
    received = lax.all_to_all(share, ("zl", "y"), 0, 0, tiled=True)
    received = received.astype(F32).reshape(SEQS, n_y, -1, cols)
    per_seq = jnp.sum(received, axis=1)
    scale = lengths.astype(F32)[:, None, None]
    return jnp.sum(per_seq * per_seq / scale, axis=0) / F32(SEQS)


def solution(mesh):
    split = Mesh(mesh.devices.reshape(2, 8, 4, 2, 4), ("zl", "y", "x", "c", "zh"))
    spec = P(("zl", "y", "x", "c"), "zh")
    return jax.shard_map(
        on_device, mesh=split, in_specs=(spec, spec, spec, spec, P()), out_specs=spec, check_vma=False
    )
```

```python
import jax
import jax.numpy as jnp
from jax import lax
from jax.experimental import pallas as pl
from jax.experimental.pallas import tpu as pltpu
from jax.sharding import Mesh
from jax.sharding import PartitionSpec as P

SEQS = 2
F32 = jnp.float32
BF16 = jnp.bfloat16
F16 = jnp.float16
TILE = 16
TOP = 15
VMEM = pl.BlockSpec(memory_space=pltpu.VMEM)
SMEM = pl.BlockSpec(memory_space=pltpu.SMEM)


def shift(value, axis, step):
    n = lax.axis_size(axis)
    return lax.ppermute(value, axis, [(i, (i + step) % n) for i in range(n)])


def sorting(width, outer, n_x, inner):
    run = width // (outer * n_x * inner)
    source = lax.broadcasted_iota(jnp.int32, (width, width), 0)
    target = lax.broadcasted_iota(jnp.int32, (width, width), 1)
    at_run, at_inner = source % run, source // run % inner
    at_x, at_outer = source // (run * inner) % n_x, source // (run * inner * n_x)
    moved = ((at_x * inner + at_inner) * outer + at_outer) * run + at_run
    return (moved == target).astype(F32).astype(BF16)


def spread(value, ones):
    return jnp.dot(value, ones, preferred_element_type=F32).astype(BF16)


def prepare_kernel(y_lo, n_c, *refs):
    inputs, (tokens, bases), held, sems = refs[:4], refs[4:6], refs[6:10], refs[10]
    sorted_tokens, out_sems = refs[11:]
    copies = [
        pltpu.make_async_copy(ref, kept, sems.at[i]) for i, (ref, kept) in enumerate(zip(inputs, held))
    ]
    for copy in copies:
        copy.start()
    n_x, n_zh, _, toks, width = tokens.shape
    cols = bases.shape[2]
    by_x = sorting(n_x * width, y_lo, n_x, n_c)
    by_owner = sorting(cols, y_lo, n_x, n_c)
    for copy in copies:
        copy.wait()
    both = jnp.concatenate([held[0][...], held[1][...]], axis=0)
    sent = []
    for x in range(n_x):
        moved = spread(both, by_x[:, x * width : (x + 1) * width])
        for which in range(2):
            sorted_tokens[x, which] = moved[which * toks : (which + 1) * toks]
        for zh in range(n_zh):
            sent.append(
                pltpu.make_async_copy(sorted_tokens.at[x], tokens.at[x, zh], out_sems.at[x, zh])
            )
            sent[-1].start()
    bases[0] = held[2][...]
    bases[1] = spread(held[3][...], by_owner)
    for copy in sent:
        copy.wait()


def prepare(y_lo, n_x, n_c, n_zh, *arrays):
    toks, feats = arrays[0].shape
    return pl.pallas_call(
        lambda *refs: prepare_kernel(y_lo, n_c, *refs),
        out_shape=(
            jax.ShapeDtypeStruct((n_x, n_zh, 2, toks, feats // n_x), BF16),
            jax.ShapeDtypeStruct((2, *arrays[2].shape), BF16),
        ),
        in_specs=[pl.BlockSpec(memory_space=pl.ANY)] * 4,
        out_specs=(pl.BlockSpec(memory_space=pl.ANY), VMEM),
        scratch_shapes=[
            *[pltpu.VMEM(a.shape, BF16) for a in arrays],
            pltpu.SemaphoreType.DMA((4,)),
            pltpu.VMEM((n_x, 2, toks, feats // n_x), BF16),
            pltpu.SemaphoreType.DMA((n_x, n_zh)),
        ],
        compiler_params=pltpu.CompilerParams(vmem_limit_bytes=60 * 2**20),
        cost_estimate=pl.CostEstimate(
            flops=4 * toks * feats * feats, bytes_accessed=2**20, transcendentals=0
        ),
        name="prepare",
    )(*arrays)


def rotate_kernel(which, place, tokens, basis, core_basis, far_basis, core_far_basis, out):
    n_x, n_zh, _, toks, width = tokens.shape
    _, n_y, rows, cols = basis.shape
    per, half = n_y * 2 // n_zh, width // 2
    zl, c = place[0], place[1]
    near, far = (pl.ds(pl.multiple_of(core * half, half), half) for core in (c, 1 - c))
    total = None
    sides = (
        (zl, (basis.at[which], core_basis.at[which])),
        (1 - zl, (far_basis, core_far_basis)),
    )
    for side, bases in sides:
        for upper in range(n_y // per):
            owner = side * (n_y // per) + upper
            left = [
                tokens[:, owner, which, :, lanes].reshape(n_x * toks, half) for lanes in (near, far)
            ]
            right = [
                ref[upper * per : (upper + 1) * per].reshape(per * rows, cols) for ref in bases
            ]
            product = jnp.dot(
                jnp.concatenate(left, axis=1),
                jnp.concatenate(right, axis=0),
                preferred_element_type=F32,
            )
            total = product if total is None else total + product
    largest = jnp.max(jnp.max(jnp.abs(total), axis=0, keepdims=True), axis=1, keepdims=True)
    level = jnp.clip(jnp.ceil(jnp.log2(jnp.maximum(largest, 1e-30))), -100.0, 100.0)
    total = total * jnp.exp2(F32(TOP) - level)
    group, part = n_x * toks, cols // n_x
    for i in range(out.shape[0]):
        if which == 0:
            value = total[:, i * part : (i + 1) * part]
        else:
            value = total[:, i * part // 2 : (i + 1) * part // 2]
            value = jnp.concatenate([value[: group // 2], value[group // 2 :]], axis=1)
        out[i, pl.ds(0, value.shape[0])] = value
        out[i, pl.ds(value.shape[0], TILE)] = jnp.broadcast_to(level, (TILE, part))


def rotate(which, place, *arrays):
    n_x, n_zh, _, toks, width = arrays[0].shape
    cols = arrays[-1].shape[2]
    pieces = n_x * (1 + which)
    depth = n_x * toks // (1 + which) + TILE
    return pl.pallas_call(
        lambda *refs: rotate_kernel(which, *refs),
        out_shape=jax.ShapeDtypeStruct((pieces, depth, cols // n_x), F32),
        in_specs=[SMEM] + [VMEM] * len(arrays),
        out_specs=VMEM,
        compiler_params=pltpu.CompilerParams(vmem_limit_bytes=40 * 2**20),
        cost_estimate=pl.CostEstimate(
            flops=2 * n_x * n_zh * toks * width * cols, bytes_accessed=4 * 2**20, transcendentals=0
        ),
        name="rotate",
    )(place, *arrays)


def share_kernel(grad, act, out):
    n_k, n_c, depth, part = grad.shape
    n_x, half = act.shape[0], part // 2
    total = None
    for core in range(n_c):
        turned = [grad[k, core].T for k in range(n_k)]
        for side in range(2):
            left = jnp.concatenate([t[side * half : (side + 1) * half] for t in turned], axis=0)
            tokens = slice(side * depth, (side + 1) * depth)
            right = jnp.concatenate([act[x, core, tokens] for x in range(n_x)], axis=1)
            product = jnp.dot(left, right, preferred_element_type=F32)
            total = product if total is None else total + product
    out[...] = total.astype(BF16)


def share_of(grad, act):
    n_k, n_c, depth, part = grad.shape
    rows, cols = n_k * part // 2, act.shape[0] * part
    return pl.pallas_call(
        share_kernel,
        out_shape=jax.ShapeDtypeStruct((rows, cols), BF16),
        in_specs=[VMEM, VMEM],
        out_specs=VMEM,
        compiler_params=pltpu.CompilerParams(vmem_limit_bytes=32 * 2**20),
        cost_estimate=pl.CostEstimate(
            flops=4 * n_c * rows * cols * depth, bytes_accessed=2 * 2**20, transcendentals=0
        ),
        name="share",
    )(grad, act)


def total_of(partial, axes, n_x):
    partial = lax.all_to_all(partial.astype(F16), axes, 0, 0, tiled=True).astype(F32)
    factors = jnp.exp2(partial[:, None, -TILE:] - F32(TOP))
    partial = partial[:, :-TILE].reshape(len(partial), -1, TILE, partial.shape[2]) * factors
    partial = partial.reshape(n_x, -1, *partial.shape[1:])
    return jnp.sum(partial, axis=0).reshape(partial.shape[1], -1, partial.shape[4])


def on_device(activations, gradients, basis_act, basis_grad, lengths):
    n_zl, n_y, n_x, n_c, n_zh = (lax.axis_size(a) for a in ("zl", "y", "x", "c", "zh"))
    zl, y, c = (lax.axis_index(a) for a in ("zl", "y", "c"))
    toks = activations.shape[0]
    cols = basis_act.shape[1]
    group = n_x * toks

    tokens, bases = prepare(n_y // 2, n_x, n_c, n_zh, activations, gradients, basis_act, basis_grad)
    tokens = lax.all_to_all(
        tokens.reshape(n_x * n_zh, *tokens.shape[2:]), ("x", "zh"), 0, 0, tiled=True
    ).reshape(tokens.shape)

    basis = lax.all_gather(bases, "y", axis=1)
    core_basis = shift(basis, "c", 1)
    far_act = shift(basis[0], "zl", 1)
    far_grad = shift(basis[1], "zl", 1)
    core_far_act, core_far_grad = shift(far_act, "c", 1), shift(far_grad, "c", 1)

    place = jnp.stack([zl, c]).astype(jnp.int32)
    act = rotate(0, place, tokens, basis, core_basis, far_act, core_far_act)
    rot_act = total_of(act, "x", n_x)[0]
    grad = rotate(1, place, tokens, basis, core_basis, far_grad, core_far_grad)
    rot_grad = total_of(grad, ("x", "c"), n_x).astype(BF16)
    index = jnp.arange(group, dtype=jnp.int32)
    position = ((y * n_x + index // toks) * n_c + c) * toks + index % toks
    length = jnp.where(zl == 0, lengths[0], lengths[1])
    valid = position < length
    rot_act = jnp.where(valid[:, None], rot_act, F32(0.0)).astype(BF16)
    other_act = shift(rot_act, "c", 1)

    both_act = jnp.where(
        c == 0, jnp.stack([rot_act, other_act]), jnp.stack([other_act, rot_act])
    )
    wide_act = lax.all_to_all(
        jnp.broadcast_to(both_act[None], (n_x, *both_act.shape)), "x", 0, 0, tiled=True
    )
    wide_grad = lax.all_gather(rot_grad, "zh", axis=0)
    share = share_of(wide_grad, wide_act).reshape(n_zl * n_y, -1, cols)
    received = lax.all_to_all(share, ("zl", "y"), 0, 0, tiled=True)
    received = received.astype(F32).reshape(SEQS, n_y, -1, cols)
    per_seq = jnp.sum(received, axis=1)
    scale = lengths.astype(F32)[:, None, None]
    return jnp.sum(per_seq * per_seq / scale, axis=0) / F32(SEQS)


def solution(mesh):
    split = Mesh(mesh.devices.reshape(2, 8, 4, 2, 4), ("zl", "y", "x", "c", "zh"))
    spec = P(("zl", "y", "x", "c"), "zh")
    return jax.shard_map(
        on_device, mesh=split, in_specs=(spec, spec, spec, spec, P()), out_specs=spec, check_vma=False
    )
```

```python
import jax
import jax.numpy as jnp
from jax import lax
from jax.experimental import pallas as pl
from jax.experimental.pallas import tpu as pltpu
from jax.sharding import Mesh
from jax.sharding import PartitionSpec as P

SEQS = 2
F32 = jnp.float32
BF16 = jnp.bfloat16
F16 = jnp.float16
TILE = 16
TOP = 15
VMEM = pl.BlockSpec(memory_space=pltpu.VMEM)
SMEM = pl.BlockSpec(memory_space=pltpu.SMEM)


def shift(value, axis, step):
    n = lax.axis_size(axis)
    return lax.ppermute(value, axis, [(i, (i + step) % n) for i in range(n)])


def sorting(width, outer, n_x, inner):
    run = width // (outer * n_x * inner)
    source = lax.broadcasted_iota(jnp.int32, (width, width), 0)
    target = lax.broadcasted_iota(jnp.int32, (width, width), 1)
    at_run, at_inner = source % run, source // run % inner
    at_x, at_outer = source // (run * inner) % n_x, source // (run * inner * n_x)
    moved = ((at_x * inner + at_inner) * outer + at_outer) * run + at_run
    return (moved == target).astype(F32).astype(BF16)


def spread(value, ones):
    return jnp.dot(value, ones, preferred_element_type=F32).astype(BF16)


def bases_kernel(y_lo, n_x, n_c, act, grad, out, held, sems):
    copies = [
        pltpu.make_async_copy(ref, held.at[i], sems.at[i]) for i, ref in enumerate((act, grad))
    ]
    for copy in copies:
        copy.start()
    by_owner = sorting(held.shape[2], y_lo, n_x, n_c)
    for copy in copies:
        copy.wait()
    out[0] = held[0]
    out[1] = spread(held[1], by_owner)


def arrange_bases(y_lo, n_x, n_c, act, grad):
    return pl.pallas_call(
        lambda *refs: bases_kernel(y_lo, n_x, n_c, *refs),
        out_shape=jax.ShapeDtypeStruct((2, *act.shape), BF16),
        in_specs=[pl.BlockSpec(memory_space=pl.ANY)] * 2,
        out_specs=VMEM,
        scratch_shapes=[pltpu.VMEM((2, *act.shape), BF16), pltpu.SemaphoreType.DMA((2,))],
        compiler_params=pltpu.CompilerParams(vmem_limit_bytes=60 * 2**20),
        cost_estimate=pl.CostEstimate(
            flops=2 * act.shape[0] * act.shape[1] ** 2, bytes_accessed=2**17, transcendentals=0
        ),
        name="arrange_bases",
    )(act, grad)


def tokens_kernel(y_lo, n_c, act, grad, tokens, held, in_sems, moved, out_sems):
    copies = [
        pltpu.make_async_copy(ref, held.at[i], in_sems.at[i]) for i, ref in enumerate((act, grad))
    ]
    for copy in copies:
        copy.start()
    n_x, n_zh, _, toks, width = tokens.shape
    by_x = sorting(n_x * width, y_lo, n_x, n_c)
    for copy in copies:
        copy.wait()
    both = held[...].reshape(2 * toks, n_x * width)
    sent = []
    for x in range(n_x):
        part = spread(both, by_x[:, x * width : (x + 1) * width])
        moved[x] = part.reshape(2, toks, width)
        for zh in range(n_zh):
            sent.append(pltpu.make_async_copy(moved.at[x], tokens.at[x, zh], out_sems.at[x, zh]))
            sent[-1].start()
    for copy in sent:
        copy.wait()


def arrange_tokens(y_lo, n_x, n_c, n_zh, act, grad):
    toks, feats = act.shape
    return pl.pallas_call(
        lambda *refs: tokens_kernel(y_lo, n_c, *refs),
        out_shape=jax.ShapeDtypeStruct((n_x, n_zh, 2, toks, feats // n_x), BF16),
        in_specs=[pl.BlockSpec(memory_space=pl.ANY)] * 2,
        out_specs=pl.BlockSpec(memory_space=pl.ANY),
        scratch_shapes=[
            pltpu.VMEM((2, toks, feats), BF16),
            pltpu.SemaphoreType.DMA((2,)),
            pltpu.VMEM((n_x, 2, toks, feats // n_x), BF16),
            pltpu.SemaphoreType.DMA((n_x, n_zh)),
        ],
        compiler_params=pltpu.CompilerParams(vmem_limit_bytes=60 * 2**20),
        cost_estimate=pl.CostEstimate(
            flops=4 * toks * feats * feats, bytes_accessed=2**20, transcendentals=0
        ),
        name="arrange_tokens",
    )(act, grad)


def rotate_kernel(which, place, lengths, tokens, low, high, core_low, core_high, out, whole):
    n_x, n_zh, _, toks, width = tokens.shape
    rows, cols = low.shape[4], low.shape[5]
    group, part = n_x * toks, cols // n_x
    zl, y, c = place[0], place[1], place[2]
    for one, pair in enumerate(((low, core_low), (high, core_high))):
        for two in range(2):
            for four in range(2):
                from_y = y ^ (four * 4 + two * 2 + one)
                for far in range(2):
                    owner = (zl ^ far) * 2 + from_y // 4
                    for ref, core in zip(pair, (c, 1 - c)):
                        at = pl.multiple_of((core * 4 + from_y % 4) * rows, rows)
                        whole[owner, pl.ds(at, rows)] = ref[two, four, far, which]
    total = None
    for owner in range(n_zh):
        left = tokens[:, owner, which].reshape(group, width)
        product = jnp.dot(left, whole[owner], preferred_element_type=F32)
        total = product if total is None else total + product
    if which == 0:
        index = lax.broadcasted_iota(jnp.int32, (group, 1), 0)
        position = ((y * n_x + index // toks) * 2 + c) * toks + index % toks
        total = jnp.where(position < lengths[zl], total, 0.0)
    largest = jnp.max(jnp.max(jnp.abs(total), axis=0, keepdims=True), axis=1, keepdims=True)
    level = jnp.clip(jnp.ceil(jnp.log2(jnp.maximum(largest, 1e-30))), -100.0, 100.0)
    total = total * jnp.exp2(F32(TOP) - level)
    for i in range(out.shape[0]):
        if which == 0:
            value = total[:, i * part : (i + 1) * part]
        else:
            value = total[:, i * part // 2 : (i + 1) * part // 2]
            value = jnp.concatenate([value[: group // 2], value[group // 2 :]], axis=1)
        out[i, pl.ds(0, value.shape[0])] = value
        out[i, pl.ds(value.shape[0], TILE)] = jnp.broadcast_to(level, (TILE, part))


def rotate(which, place, lengths, *arrays):
    n_x, n_zh, _, toks, width = arrays[0].shape
    cols = arrays[1].shape[5]
    pieces = n_x * (1 + which)
    depth = n_x * toks // (1 + which) + TILE
    return pl.pallas_call(
        lambda *refs: rotate_kernel(which, *refs),
        out_shape=jax.ShapeDtypeStruct((pieces, depth, cols // n_x), F32),
        in_specs=[SMEM] * 2 + [VMEM] * len(arrays),
        out_specs=VMEM,
        scratch_shapes=[pltpu.VMEM((n_zh, width, cols), BF16)],
        compiler_params=pltpu.CompilerParams(vmem_limit_bytes=40 * 2**20),
        cost_estimate=pl.CostEstimate(
            flops=2 * n_x * n_zh * toks * width * cols, bytes_accessed=4 * 2**20, transcendentals=0
        ),
        name="rotate",
    )(place, lengths, *arrays)


def share_kernel(grad, act, out):
    n_k, n_c, depth, part = grad.shape
    n_x, half = act.shape[0], part // 2
    total = None
    for core in range(n_c):
        turned = [grad[k, core].T for k in range(n_k)]
        for side in range(2):
            left = jnp.concatenate([t[side * half : (side + 1) * half] for t in turned], axis=0)
            tokens = slice(side * depth, (side + 1) * depth)
            right = jnp.concatenate([act[x, core, tokens] for x in range(n_x)], axis=1)
            product = jnp.dot(left, right, preferred_element_type=F32)
            total = product if total is None else total + product
    out[...] = total.astype(BF16)


def share_of(grad, act):
    n_k, n_c, depth, part = grad.shape
    rows, cols = n_k * part // 2, act.shape[0] * part
    return pl.pallas_call(
        share_kernel,
        out_shape=jax.ShapeDtypeStruct((rows, cols), BF16),
        in_specs=[VMEM, VMEM],
        out_specs=VMEM,
        compiler_params=pltpu.CompilerParams(vmem_limit_bytes=32 * 2**20),
        cost_estimate=pl.CostEstimate(
            flops=4 * n_c * rows * cols * depth, bytes_accessed=2 * 2**20, transcendentals=0
        ),
        name="share",
    )(grad, act)


def total_of(partial, axes, n_x):
    partial = lax.all_to_all(partial.astype(F16), axes, 0, 0, tiled=True).astype(F32)
    factors = jnp.exp2(partial[:, None, -TILE:] - F32(TOP))
    partial = partial[:, :-TILE].reshape(len(partial), -1, TILE, partial.shape[2]) * factors
    partial = partial.reshape(n_x, -1, *partial.shape[1:])
    return jnp.sum(partial, axis=0).reshape(partial.shape[1], -1, partial.shape[4])


def on_device(activations, gradients, basis_act, basis_grad, lengths):
    n_zl, n_y, n_x, n_c, n_zh = (lax.axis_size(a) for a in ("zl", "y", "x", "c", "zh"))
    zl, y, c = (lax.axis_index(a) for a in ("zl", "y", "c"))
    cols = basis_act.shape[1]

    def partner(value, step):
        return lax.ppermute(value, "y", [(i, i ^ step) for i in range(n_y)])

    bases = arrange_bases(n_y // 2, n_x, n_c, basis_act, basis_grad)
    tokens = arrange_tokens(n_y // 2, n_x, n_c, n_zh, activations, gradients)
    far_bases, tokens = lax.optimization_barrier((shift(bases, "zl", 1), tokens))
    low = jnp.stack([bases, far_bases])
    low = jnp.stack([low, partner(low, 4)])
    low = jnp.stack([low, partner(low, 2)])
    high = partner(low, 1)
    core_low, core_high = shift(low, "c", 1), shift(high, "c", 1)

    tokens = lax.all_to_all(
        tokens.reshape(n_x * n_zh, *tokens.shape[2:]), ("x", "zh"), 0, 0, tiled=True
    ).reshape(tokens.shape)

    place = jnp.stack([zl, y, c]).astype(jnp.int32)
    arrays = (lengths, tokens, low, high, core_low, core_high)
    rot_act = total_of(rotate(0, place, *arrays), "x", n_x)[0].astype(BF16)
    grad = rotate(1, place, *arrays)
    rot_grad = total_of(grad, ("x", "c"), n_x).astype(BF16)
    other_act = shift(rot_act, "c", 1)

    both_act = jnp.where(
        c == 0, jnp.stack([rot_act, other_act]), jnp.stack([other_act, rot_act])
    )
    wide_act = lax.all_to_all(
        jnp.broadcast_to(both_act[None], (n_x, *both_act.shape)), "x", 0, 0, tiled=True
    )
    wide_grad = lax.all_gather(rot_grad, "zh", axis=0)
    share = share_of(wide_grad, wide_act).reshape(n_zl * n_y, -1, cols)
    received = lax.all_to_all(share, ("zl", "y"), 0, 0, tiled=True)
    received = received.astype(F32).reshape(SEQS, n_y, -1, cols)
    per_seq = jnp.sum(received, axis=1)
    scale = lengths.astype(F32)[:, None, None]
    return jnp.sum(per_seq * per_seq / scale, axis=0) / F32(SEQS)


def solution(mesh):
    split = Mesh(mesh.devices.reshape(2, 8, 4, 2, 4), ("zl", "y", "x", "c", "zh"))
    spec = P(("zl", "y", "x", "c"), "zh")
    return jax.shard_map(
        on_device, mesh=split, in_specs=(spec, spec, spec, spec, P()), out_specs=spec, check_vma=False
    )
```

```python
import jax
import jax.numpy as jnp
from jax import lax
from jax.experimental import pallas as pl
from jax.experimental.pallas import tpu as pltpu
from jax.sharding import Mesh
from jax.sharding import PartitionSpec as P

SEQS = 2
F32 = jnp.float32
BF16 = jnp.bfloat16
F16 = jnp.float16
TILE = 16
TOP = 15
VMEM = pl.BlockSpec(memory_space=pltpu.VMEM)
SMEM = pl.BlockSpec(memory_space=pltpu.SMEM)


def shift(value, axis, step):
    n = lax.axis_size(axis)
    return lax.ppermute(value, axis, [(i, (i + step) % n) for i in range(n)])


def sorting(width, outer, n_x, inner):
    run = width // (outer * n_x * inner)
    source = lax.broadcasted_iota(jnp.int32, (width, width), 0)
    target = lax.broadcasted_iota(jnp.int32, (width, width), 1)
    at_run, at_inner = source % run, source // run % inner
    at_x, at_outer = source // (run * inner) % n_x, source // (run * inner * n_x)
    moved = ((at_x * inner + at_inner) * outer + at_outer) * run + at_run
    return (moved == target).astype(F32).astype(BF16)


def spread(value, ones):
    return jnp.dot(value, ones, preferred_element_type=F32).astype(BF16)


def bases_kernel(y_lo, n_x, n_c, act, grad, out, held, sems):
    copies = [
        pltpu.make_async_copy(ref, held.at[i], sems.at[i]) for i, ref in enumerate((act, grad))
    ]
    for copy in copies:
        copy.start()
    by_owner = sorting(held.shape[2], y_lo, n_x, n_c)
    for copy in copies:
        copy.wait()
    out[0] = held[0]
    out[1] = spread(held[1], by_owner)


def arrange_bases(y_lo, n_x, n_c, act, grad):
    return pl.pallas_call(
        lambda *refs: bases_kernel(y_lo, n_x, n_c, *refs),
        out_shape=jax.ShapeDtypeStruct((2, *act.shape), BF16),
        in_specs=[pl.BlockSpec(memory_space=pl.ANY)] * 2,
        out_specs=VMEM,
        scratch_shapes=[pltpu.VMEM((2, *act.shape), BF16), pltpu.SemaphoreType.DMA((2,))],
        compiler_params=pltpu.CompilerParams(vmem_limit_bytes=60 * 2**20),
        cost_estimate=pl.CostEstimate(
            flops=2 * act.shape[0] * act.shape[1] ** 2, bytes_accessed=2**17, transcendentals=0
        ),
        name="arrange_bases",
    )(act, grad)


def tokens_kernel(y_lo, n_c, act, grad, tokens, held, in_sems, moved, out_sems):
    copies = [
        pltpu.make_async_copy(ref, held.at[i], in_sems.at[i]) for i, ref in enumerate((act, grad))
    ]
    for copy in copies:
        copy.start()
    n_x, n_zh, _, toks, width = tokens.shape
    by_x = sorting(n_x * width, y_lo, n_x, n_c)
    for copy in copies:
        copy.wait()
    both = held[...].reshape(2 * toks, n_x * width)
    sent = []
    for x in range(n_x):
        part = spread(both, by_x[:, x * width : (x + 1) * width])
        moved[x] = part.reshape(2, toks, width)
        for zh in range(n_zh):
            sent.append(pltpu.make_async_copy(moved.at[x], tokens.at[x, zh], out_sems.at[x, zh]))
            sent[-1].start()
    for copy in sent:
        copy.wait()


def arrange_tokens(y_lo, n_x, n_c, n_zh, act, grad):
    toks, feats = act.shape
    return pl.pallas_call(
        lambda *refs: tokens_kernel(y_lo, n_c, *refs),
        out_shape=jax.ShapeDtypeStruct((n_x, n_zh, 2, toks, feats // n_x), BF16),
        in_specs=[pl.BlockSpec(memory_space=pl.ANY)] * 2,
        out_specs=pl.BlockSpec(memory_space=pl.ANY),
        scratch_shapes=[
            pltpu.VMEM((2, toks, feats), BF16),
            pltpu.SemaphoreType.DMA((2,)),
            pltpu.VMEM((n_x, 2, toks, feats // n_x), BF16),
            pltpu.SemaphoreType.DMA((n_x, n_zh)),
        ],
        compiler_params=pltpu.CompilerParams(vmem_limit_bytes=60 * 2**20),
        cost_estimate=pl.CostEstimate(
            flops=4 * toks * feats * feats, bytes_accessed=2**20, transcendentals=0
        ),
        name="arrange_tokens",
    )(act, grad)


def rotate_kernel(place, lengths, tokens, low, high, core_low, core_high, out, whole):
    n_x, n_zh, _, toks, width = tokens.shape
    rows, cols = low.shape[4], low.shape[5]
    group, part = n_x * toks, cols // n_x
    zl, y, c = place[0], place[1], place[2]
    sums = []
    for which in range(2):
        for one, pair in enumerate(((low, core_low), (high, core_high))):
            for two in range(2):
                for four in range(2):
                    from_y = y ^ (four * 4 + two * 2 + one)
                    for far in range(2):
                        owner = (zl ^ far) * 2 + from_y // 4
                        for ref, core in zip(pair, (c, 1 - c)):
                            at = pl.multiple_of((core * 4 + from_y % 4) * rows, rows)
                            whole[which, owner, pl.ds(at, rows)] = ref[two, four, far, which]
        total = None
        for owner in range(n_zh):
            left = tokens[:, owner, which].reshape(group, width)
            product = jnp.dot(left, whole[which, owner], preferred_element_type=F32)
            total = product if total is None else total + product
        sums.append(total)
    index = lax.broadcasted_iota(jnp.int32, (group, 1), 0)
    position = ((y * n_x + index // toks) * 2 + c) * toks + index % toks
    sums[0] = jnp.where(position < lengths[zl], sums[0], 0.0)
    largest = jnp.max(jnp.maximum(jnp.abs(sums[0]), jnp.abs(sums[1])), axis=0, keepdims=True)
    largest = jnp.max(largest, axis=1, keepdims=True)
    level = jnp.clip(jnp.ceil(jnp.log2(jnp.maximum(largest, 1e-30))), -100.0, 100.0)
    act, grad = (total * jnp.exp2(F32(TOP) - level) for total in sums)
    half = group // 2
    for x in range(n_x):
        for core in range(2):
            piece = 2 * x + core
            out[piece, pl.ds(0, half)] = act[core * half : (core + 1) * half, x * part : (x + 1) * part]
            value = grad[:, piece * part // 2 : (piece + 1) * part // 2]
            out[piece, pl.ds(half, half)] = jnp.concatenate([value[:half], value[half:]], axis=1)
            out[piece, pl.ds(group, TILE)] = jnp.broadcast_to(level, (TILE, part))


def rotate(place, lengths, *arrays):
    n_x, n_zh, _, toks, width = arrays[0].shape
    cols = arrays[1].shape[5]
    return pl.pallas_call(
        rotate_kernel,
        out_shape=jax.ShapeDtypeStruct((2 * n_x, n_x * toks + TILE, cols // n_x), F32),
        in_specs=[SMEM] * 2 + [VMEM] * len(arrays),
        out_specs=VMEM,
        scratch_shapes=[pltpu.VMEM((2, n_zh, width, cols), BF16)],
        compiler_params=pltpu.CompilerParams(vmem_limit_bytes=40 * 2**20),
        cost_estimate=pl.CostEstimate(
            flops=4 * n_x * n_zh * toks * width * cols, bytes_accessed=8 * 2**20, transcendentals=0
        ),
        name="rotate",
    )(place, lengths, *arrays)


def share_kernel(grad, act, out):
    n_k, n_c, depth, part = grad.shape
    n_x, half = act.shape[0], part // 2
    total = None
    for core in range(n_c):
        turned = [grad[k, core].T for k in range(n_k)]
        for side in range(2):
            left = jnp.concatenate([t[side * half : (side + 1) * half] for t in turned], axis=0)
            right = jnp.concatenate([act[x, side, core] for x in range(n_x)], axis=1)
            product = jnp.dot(left, right, preferred_element_type=F32)
            total = product if total is None else total + product
    out[...] = total.astype(BF16)


def share_of(grad, act):
    n_k, n_c, depth, part = grad.shape
    rows, cols = n_k * part // 2, act.shape[0] * part
    return pl.pallas_call(
        share_kernel,
        out_shape=jax.ShapeDtypeStruct((rows, cols), BF16),
        in_specs=[VMEM, VMEM],
        out_specs=VMEM,
        compiler_params=pltpu.CompilerParams(vmem_limit_bytes=32 * 2**20),
        cost_estimate=pl.CostEstimate(
            flops=4 * n_c * rows * cols * depth, bytes_accessed=2 * 2**20, transcendentals=0
        ),
        name="share",
    )(grad, act)


def on_device(activations, gradients, basis_act, basis_grad, lengths):
    n_zl, n_y, n_x, n_c, n_zh = (lax.axis_size(a) for a in ("zl", "y", "x", "c", "zh"))
    zl, y, c = (lax.axis_index(a) for a in ("zl", "y", "c"))
    cols, group = basis_act.shape[1], n_x * activations.shape[0]

    def partner(value, step):
        return lax.ppermute(value, "y", [(i, i ^ step) for i in range(n_y)])

    bases = arrange_bases(n_y // 2, n_x, n_c, basis_act, basis_grad)
    tokens = arrange_tokens(n_y // 2, n_x, n_c, n_zh, activations, gradients)
    far_bases, tokens = lax.optimization_barrier((shift(bases, "zl", 1), tokens))
    low = jnp.stack([bases, far_bases])
    low = jnp.stack([low, partner(low, 4)])
    low = jnp.stack([low, partner(low, 2)])
    high = partner(low, 1)
    core_low, core_high = shift(low, "c", 1), shift(high, "c", 1)

    tokens = lax.all_to_all(
        tokens.reshape(n_x * n_zh, *tokens.shape[2:]), ("x", "zh"), 0, 0, tiled=True
    ).reshape(tokens.shape)

    place = jnp.stack([zl, y, c]).astype(jnp.int32)
    arrays = (lengths, tokens, low, high, core_low, core_high)
    partial = rotate(place, *arrays).astype(F16)
    partial = lax.all_to_all(partial, ("x", "c"), 0, 0, tiled=True)
    factors = jnp.exp2(partial[:, None, -TILE:].astype(F32) - F32(TOP))
    partial = partial[:, :-TILE].reshape(n_x * n_c, -1, TILE, partial.shape[2]).astype(F32)
    partial = (partial * factors).reshape(n_x, n_c, *partial.shape[1:])
    rotated = jnp.sum(partial, axis=0).astype(BF16).reshape(n_c, group, -1)
    rot_act, rot_grad = rotated[:, : group // 2], rotated[:, group // 2 :]

    wide_act = lax.all_to_all(
        jnp.broadcast_to(rot_act[None], (n_x * n_c, *rot_act.shape)), ("x", "c"), 0, 0, tiled=True
    ).reshape(n_x, n_c, *rot_act.shape)
    wide_grad = lax.all_gather(rot_grad, "zh", axis=0)
    share = share_of(wide_grad, wide_act).reshape(n_zl * n_y, -1, cols)
    received = lax.all_to_all(share, ("zl", "y"), 0, 0, tiled=True)
    received = received.astype(F32).reshape(SEQS, n_y, -1, cols)
    per_seq = jnp.sum(received, axis=1)
    scale = lengths.astype(F32)[:, None, None]
    return jnp.sum(per_seq * per_seq / scale, axis=0) / F32(SEQS)


def solution(mesh):
    split = Mesh(mesh.devices.reshape(2, 8, 4, 2, 4), ("zl", "y", "x", "c", "zh"))
    spec = P(("zl", "y", "x", "c"), "zh")
    return jax.shard_map(
        on_device, mesh=split, in_specs=(spec, spec, spec, spec, P()), out_specs=spec, check_vma=False
    )
```

```python
import jax
import jax.numpy as jnp
from jax import lax
from jax.experimental import pallas as pl
from jax.experimental.pallas import tpu as pltpu
from jax.sharding import Mesh
from jax.sharding import PartitionSpec as P

SEQS = 2
F32 = jnp.float32
BF16 = jnp.bfloat16
F16 = jnp.float16
TILE = 16
TOP = 15
VMEM = pl.BlockSpec(memory_space=pltpu.VMEM)
SMEM = pl.BlockSpec(memory_space=pltpu.SMEM)


def shift(value, axis, step):
    n = lax.axis_size(axis)
    return lax.ppermute(value, axis, [(i, (i + step) % n) for i in range(n)])


def sorting(width, outer, n_x, inner):
    run = width // (outer * n_x * inner)
    source = lax.broadcasted_iota(jnp.int32, (width, width), 0)
    target = lax.broadcasted_iota(jnp.int32, (width, width), 1)
    at_run, at_inner = source % run, source // run % inner
    at_x, at_outer = source // (run * inner) % n_x, source // (run * inner * n_x)
    moved = ((at_x * inner + at_inner) * outer + at_outer) * run + at_run
    return (moved == target).astype(F32).astype(BF16)


def spread(value, ones):
    return jnp.dot(value, ones, preferred_element_type=F32).astype(BF16)


def bases_kernel(y_lo, n_x, n_c, act, grad, out, held, sems):
    copies = [
        pltpu.make_async_copy(ref, held.at[i], sems.at[i]) for i, ref in enumerate((act, grad))
    ]
    for copy in copies:
        copy.start()
    by_owner = sorting(held.shape[2], y_lo, n_x, n_c)
    for copy in copies:
        copy.wait()
    out[0] = held[0]
    out[1] = spread(held[1], by_owner)


def arrange_bases(y_lo, n_x, n_c, act, grad):
    return pl.pallas_call(
        lambda *refs: bases_kernel(y_lo, n_x, n_c, *refs),
        out_shape=jax.ShapeDtypeStruct((2, *act.shape), BF16),
        in_specs=[pl.BlockSpec(memory_space=pl.ANY)] * 2,
        out_specs=VMEM,
        scratch_shapes=[pltpu.VMEM((2, *act.shape), BF16), pltpu.SemaphoreType.DMA((2,))],
        compiler_params=pltpu.CompilerParams(vmem_limit_bytes=60 * 2**20),
        cost_estimate=pl.CostEstimate(
            flops=2 * act.shape[0] * act.shape[1] ** 2, bytes_accessed=2**17, transcendentals=0
        ),
        name="arrange_bases",
    )(act, grad)


def tokens_kernel(y_lo, n_c, act, grad, tokens, held, in_sems, moved, out_sems):
    copies = [
        pltpu.make_async_copy(ref, held.at[i], in_sems.at[i]) for i, ref in enumerate((act, grad))
    ]
    for copy in copies:
        copy.start()
    n_x, n_zh, _, toks, width = tokens.shape
    by_x = sorting(n_x * width, y_lo, n_x, n_c)
    for copy in copies:
        copy.wait()
    both = held[...].reshape(2 * toks, n_x * width)
    sent = []
    for x in range(n_x):
        part = spread(both, by_x[:, x * width : (x + 1) * width])
        moved[x] = part.reshape(2, toks, width)
        for zh in range(n_zh):
            sent.append(pltpu.make_async_copy(moved.at[x], tokens.at[x, zh], out_sems.at[x, zh]))
            sent[-1].start()
    for copy in sent:
        copy.wait()


def arrange_tokens(y_lo, n_x, n_c, n_zh, act, grad):
    toks, feats = act.shape
    return pl.pallas_call(
        lambda *refs: tokens_kernel(y_lo, n_c, *refs),
        out_shape=jax.ShapeDtypeStruct((n_x, n_zh, 2, toks, feats // n_x), BF16),
        in_specs=[pl.BlockSpec(memory_space=pl.ANY)] * 2,
        out_specs=pl.BlockSpec(memory_space=pl.ANY),
        scratch_shapes=[
            pltpu.VMEM((2, toks, feats), BF16),
            pltpu.SemaphoreType.DMA((2,)),
            pltpu.VMEM((n_x, 2, toks, feats // n_x), BF16),
            pltpu.SemaphoreType.DMA((n_x, n_zh)),
        ],
        compiler_params=pltpu.CompilerParams(vmem_limit_bytes=60 * 2**20),
        cost_estimate=pl.CostEstimate(
            flops=4 * toks * feats * feats, bytes_accessed=2**20, transcendentals=0
        ),
        name="arrange_tokens",
    )(act, grad)


def rotate_kernel(place, lengths, tokens, low, high, core_low, core_high, out, whole):
    n_x, n_zh, _, toks, width = tokens.shape
    rows, cols = low.shape[4], low.shape[5]
    group, part = n_x * toks, cols // n_x
    zl, y, c = place[0], place[1], place[2]
    sums = []
    for which in range(2):
        for one, pair in enumerate(((low, core_low), (high, core_high))):
            for two in range(2):
                for four in range(2):
                    from_y = y ^ (four * 4 + two * 2 + one)
                    for far in range(2):
                        owner = (zl ^ far) * 2 + from_y // 4
                        for ref, core in zip(pair, (c, 1 - c)):
                            at = pl.multiple_of((core * 4 + from_y % 4) * rows, rows)
                            whole[which, owner, pl.ds(at, rows)] = ref[two, four, far, which]
        total = None
        for owner in range(n_zh):
            left = tokens[:, owner, which].reshape(group, width)
            product = jnp.dot(left, whole[which, owner], preferred_element_type=F32)
            total = product if total is None else total + product
        sums.append(total)
    index = lax.broadcasted_iota(jnp.int32, (group, 1), 0)
    position = ((y * n_x + index // toks) * 2 + c) * toks + index % toks
    sums[0] = jnp.where(position < lengths[zl], sums[0], 0.0)
    largest = jnp.max(jnp.maximum(jnp.abs(sums[0]), jnp.abs(sums[1])), axis=0, keepdims=True)
    largest = jnp.max(largest, axis=1, keepdims=True)
    level = jnp.clip(jnp.ceil(jnp.log2(jnp.maximum(largest, 1e-30))), -100.0, 100.0)
    act, grad = (total * jnp.exp2(F32(TOP) - level) for total in sums)
    half = group // 2
    for x in range(n_x):
        for core in range(2):
            piece = 2 * x + core
            out[piece, pl.ds(0, half)] = act[core * half : (core + 1) * half, x * part : (x + 1) * part]
            value = grad[:, piece * part // 2 : (piece + 1) * part // 2]
            out[piece, pl.ds(half, half)] = jnp.concatenate([value[:half], value[half:]], axis=1)
            out[piece, pl.ds(group, TILE)] = jnp.broadcast_to(level, (TILE, part))


def rotate(place, lengths, *arrays):
    n_x, n_zh, _, toks, width = arrays[0].shape
    cols = arrays[1].shape[5]
    return pl.pallas_call(
        rotate_kernel,
        out_shape=jax.ShapeDtypeStruct((2 * n_x, n_x * toks + TILE, cols // n_x), F32),
        in_specs=[SMEM] * 2 + [VMEM] * len(arrays),
        out_specs=VMEM,
        scratch_shapes=[pltpu.VMEM((2, n_zh, width, cols), BF16)],
        compiler_params=pltpu.CompilerParams(vmem_limit_bytes=40 * 2**20),
        cost_estimate=pl.CostEstimate(
            flops=4 * n_x * n_zh * toks * width * cols, bytes_accessed=8 * 2**20, transcendentals=0
        ),
        name="rotate",
    )(place, lengths, *arrays)


def share_kernel(place, grad, act, core_act, out):
    n_k, n_c, depth, part = grad.shape
    n_x, half = act.shape[0], part // 2
    c = place[2]
    total = None
    for core in range(n_c):
        turned = [grad[k, core].T for k in range(n_k)]
        low = jnp.concatenate([t[:half] for t in turned], axis=0)
        high = jnp.concatenate([t[half:] for t in turned], axis=0)
        sides = ((jnp.where(c == 0, low, high), act), (jnp.where(c == 0, high, low), core_act))
        for left, tokens in sides:
            right = jnp.concatenate([tokens[x, core] for x in range(n_x)], axis=1)
            product = jnp.dot(left, right, preferred_element_type=F32)
            total = product if total is None else total + product
    out[...] = total.astype(BF16)


def share_of(place, grad, act, core_act):
    n_k, n_c, depth, part = grad.shape
    rows, cols = n_k * part // 2, act.shape[0] * part
    return pl.pallas_call(
        share_kernel,
        out_shape=jax.ShapeDtypeStruct((rows, cols), BF16),
        in_specs=[SMEM] + [VMEM] * 3,
        out_specs=VMEM,
        compiler_params=pltpu.CompilerParams(vmem_limit_bytes=32 * 2**20),
        cost_estimate=pl.CostEstimate(
            flops=4 * n_c * rows * cols * depth, bytes_accessed=2 * 2**20, transcendentals=0
        ),
        name="share",
    )(place, grad, act, core_act)


def on_device(activations, gradients, basis_act, basis_grad, lengths):
    n_zl, n_y, n_x, n_c, n_zh = (lax.axis_size(a) for a in ("zl", "y", "x", "c", "zh"))
    zl, y, c = (lax.axis_index(a) for a in ("zl", "y", "c"))
    cols, group = basis_act.shape[1], n_x * activations.shape[0]

    def partner(value, step):
        return lax.ppermute(value, "y", [(i, i ^ step) for i in range(n_y)])

    bases = arrange_bases(n_y // 2, n_x, n_c, basis_act, basis_grad)
    tokens = arrange_tokens(n_y // 2, n_x, n_c, n_zh, activations, gradients)
    far_bases, tokens = lax.optimization_barrier((shift(bases, "zl", 1), tokens))
    low = jnp.stack([bases, far_bases])
    low = jnp.stack([low, partner(low, 4)])
    low = jnp.stack([low, partner(low, 2)])
    high = partner(low, 1)
    core_low, core_high = shift(low, "c", 1), shift(high, "c", 1)

    tokens = lax.all_to_all(
        tokens.reshape(n_x * n_zh, *tokens.shape[2:]), ("x", "zh"), 0, 0, tiled=True
    ).reshape(tokens.shape)

    place = jnp.stack([zl, y, c]).astype(jnp.int32)
    arrays = (lengths, tokens, low, high, core_low, core_high)
    partial = rotate(place, *arrays).astype(F16)
    partial = lax.all_to_all(partial, ("x", "c"), 0, 0, tiled=True)
    factors = jnp.exp2(partial[:, None, -TILE:].astype(F32) - F32(TOP))
    partial = partial[:, :-TILE].reshape(n_x * n_c, -1, TILE, partial.shape[2]).astype(F32)
    partial = (partial * factors).reshape(n_x, n_c, *partial.shape[1:])
    rotated = jnp.sum(partial, axis=0).astype(BF16).reshape(n_c, group, -1)
    rot_act, rot_grad = rotated[:, : group // 2], rotated[:, group // 2 :]

    wide_grad = lax.all_to_all(
        jnp.broadcast_to(rot_grad[None], (n_zh, *rot_grad.shape)), "zh", 0, 0, tiled=True
    )
    wide_act = lax.all_gather(rot_act, "x", axis=0)
    core_act = shift(wide_act, "c", 1)
    share = share_of(place, wide_grad, wide_act, core_act).reshape(n_zl * n_y, -1, cols)
    received = lax.all_to_all(share, ("zl", "y"), 0, 0, tiled=True)
    received = received.astype(F32).reshape(SEQS, n_y, -1, cols)
    per_seq = jnp.sum(received, axis=1)
    scale = lengths.astype(F32)[:, None, None]
    return jnp.sum(per_seq * per_seq / scale, axis=0) / F32(SEQS)


def solution(mesh):
    split = Mesh(mesh.devices.reshape(2, 8, 4, 2, 4), ("zl", "y", "x", "c", "zh"))
    spec = P(("zl", "y", "x", "c"), "zh")
    return jax.shard_map(
        on_device, mesh=split, in_specs=(spec, spec, spec, spec, P()), out_specs=spec, check_vma=False
    )
```

```python
import jax
import jax.numpy as jnp
from jax import lax
from jax.experimental import pallas as pl
from jax.experimental.pallas import tpu as pltpu
from jax.sharding import Mesh
from jax.sharding import PartitionSpec as P

SEQS = 2
F32 = jnp.float32
BF16 = jnp.bfloat16
F16 = jnp.float16
TILE = 16
TOP = 15
VMEM = pl.BlockSpec(memory_space=pltpu.VMEM)
SMEM = pl.BlockSpec(memory_space=pltpu.SMEM)


def sorting(width, outer, n_x, inner):
    run = width // (outer * n_x * inner)
    source = lax.broadcasted_iota(jnp.int32, (width, width), 0)
    target = lax.broadcasted_iota(jnp.int32, (width, width), 1)
    at_run, at_inner = source % run, source // run % inner
    at_x, at_outer = source // (run * inner) % n_x, source // (run * inner * n_x)
    moved = ((at_x * inner + at_inner) * outer + at_outer) * run + at_run
    return (moved == target).astype(F32).astype(BF16)


def spread(value, ones):
    return jnp.dot(value, ones, preferred_element_type=F32).astype(BF16)


def bases_kernel(y_lo, n_x, n_c, act, grad, out, held, sems):
    copies = [
        pltpu.make_async_copy(ref, held.at[i], sems.at[i]) for i, ref in enumerate((act, grad))
    ]
    for copy in copies:
        copy.start()
    by_owner = sorting(held.shape[2], y_lo, n_x, n_c)
    for copy in copies:
        copy.wait()
    out[0] = held[0]
    out[1] = spread(held[1], by_owner)


def arrange_bases(y_lo, n_x, n_c, act, grad):
    return pl.pallas_call(
        lambda *refs: bases_kernel(y_lo, n_x, n_c, *refs),
        out_shape=jax.ShapeDtypeStruct((2, *act.shape), BF16),
        in_specs=[pl.BlockSpec(memory_space=pl.ANY)] * 2,
        out_specs=VMEM,
        scratch_shapes=[pltpu.VMEM((2, *act.shape), BF16), pltpu.SemaphoreType.DMA((2,))],
        compiler_params=pltpu.CompilerParams(vmem_limit_bytes=60 * 2**20),
        cost_estimate=pl.CostEstimate(
            flops=2 * act.shape[0] * act.shape[1] ** 2, bytes_accessed=2**17, transcendentals=0
        ),
        name="arrange_bases",
    )(act, grad)


def tokens_kernel(y_lo, n_c, act, grad, act_out, grad_out, held, in_sems, moved, out_sems):
    copies = [
        pltpu.make_async_copy(ref, held.at[i], in_sems.at[i]) for i, ref in enumerate((act, grad))
    ]
    for copy in copies:
        copy.start()
    n_x, n_zh, toks, width = act_out.shape
    by_x = sorting(n_x * width, y_lo, n_x, n_c)
    sent = []
    for which, out in enumerate((act_out, grad_out)):
        copies[which].wait()
        part = spread(held[which], by_x)
        for x in range(n_x):
            moved[which, x] = part[:, x * width : (x + 1) * width]
            for zh in range(n_zh):
                sent.append(
                    pltpu.make_async_copy(
                        moved.at[which, x], out.at[x, zh], out_sems.at[which, x, zh]
                    )
                )
                sent[-1].start()
    for copy in sent:
        copy.wait()


def arrange_tokens(y_lo, n_x, n_c, n_zh, act, grad):
    toks, feats = act.shape
    out = jax.ShapeDtypeStruct((n_x, n_zh, toks, feats // n_x), BF16)
    hbm = pl.BlockSpec(memory_space=pl.ANY)
    return pl.pallas_call(
        lambda *refs: tokens_kernel(y_lo, n_c, *refs),
        out_shape=(out, out),
        in_specs=[hbm, hbm],
        out_specs=(hbm, hbm),
        scratch_shapes=[
            pltpu.VMEM((2, toks, feats), BF16),
            pltpu.SemaphoreType.DMA((2,)),
            pltpu.VMEM((2, n_x, toks, feats // n_x), BF16),
            pltpu.SemaphoreType.DMA((2, n_x, n_zh)),
        ],
        compiler_params=pltpu.CompilerParams(vmem_limit_bytes=60 * 2**20),
        cost_estimate=pl.CostEstimate(
            flops=4 * toks * feats * feats, bytes_accessed=2**20, transcendentals=0
        ),
        name="arrange_tokens",
    )(act, grad)


def rotate_kernel(which, place, lengths, tokens, low, high, core_low, core_high, out, whole):
    n_x, n_zh, toks, width = tokens.shape
    rows, cols = low.shape[4], low.shape[5]
    group, part = n_x * toks, cols // n_x
    zl, y, c, own_x = (place[i] for i in range(4))
    for one, pair in enumerate(((low, core_low), (high, core_high))):
        for two in range(2):
            for four in range(2):
                from_y = y ^ (four * 4 + two * 2 + one)
                for far in range(2):
                    owner = (zl ^ far) * 2 + from_y // 4
                    for ref, core in zip(pair, (c, 1 - c)):
                        at = pl.multiple_of((core * 4 + from_y % 4) * rows, rows)
                        whole[owner, pl.ds(at, rows)] = ref[two, four, far, which]
    total = None
    for owner in range(n_zh):
        left = tokens[:, owner].reshape(group, width)
        product = jnp.dot(left, whole[owner], preferred_element_type=F32)
        total = product if total is None else total + product
    if which == 0:
        index = lax.broadcasted_iota(jnp.int32, (group, 1), 0)
        position = ((y * n_x + index // toks) * 2 + c) * toks + index % toks
        total = jnp.where(position < lengths[zl], total, 0.0)
    largest = jnp.max(jnp.max(jnp.abs(total), axis=0, keepdims=True), axis=1, keepdims=True)
    level = jnp.clip(jnp.ceil(jnp.log2(jnp.maximum(largest, 1e-30))), -100.0, 100.0)
    total = total * jnp.exp2(F32(TOP) - level)
    for i in range(out.shape[0]):
        if which == 0:
            to = own_x ^ i
            value = total[:, i * part : (i + 1) * part]
        else:
            value = total[:, i * part // 2 : (i + 1) * part // 2]
            to = i
            value = jnp.concatenate([value[: group // 2], value[group // 2 :]], axis=1)
        out[to, pl.ds(0, value.shape[0])] = value
        out[to, pl.ds(value.shape[0], TILE)] = jnp.broadcast_to(level, (TILE, part))


def rotate(which, place, lengths, *arrays):
    n_x, n_zh, toks, width = arrays[0].shape
    cols = arrays[1].shape[5]
    pieces = n_x * (1 + which)
    depth = n_x * toks // (1 + which) + TILE
    return pl.pallas_call(
        lambda *refs: rotate_kernel(which, *refs),
        out_shape=jax.ShapeDtypeStruct((pieces, depth, cols // n_x), F32),
        in_specs=[SMEM] * 2 + [VMEM] * len(arrays),
        out_specs=VMEM,
        scratch_shapes=[pltpu.VMEM((n_zh, width, cols), BF16)],
        compiler_params=pltpu.CompilerParams(vmem_limit_bytes=40 * 2**20),
        cost_estimate=pl.CostEstimate(
            flops=2 * n_x * n_zh * toks * width * cols, bytes_accessed=4 * 2**20, transcendentals=0
        ),
        name="rotate",
    )(place, lengths, *arrays)


def share_kernel(place, grad, act, core_act, out):
    n_k, _, depth, part = grad.shape
    n_x, half = act.shape[0], part // 2
    c = place[2]
    total = None
    for core, tokens in ((c, act), (1 - c, core_act)):
        turned = [grad[k, core].T for k in range(n_k)]
        for side in range(2):
            left = jnp.concatenate([t[side * half : (side + 1) * half] for t in turned], axis=0)
            right = jnp.concatenate(
                [tokens[x, side * depth : (side + 1) * depth] for x in range(n_x)], axis=1
            )
            product = jnp.dot(left, right, preferred_element_type=F32)
            total = product if total is None else total + product
    out[...] = total.astype(BF16)


def share_of(place, grad, act, core_act):
    n_k, n_c, depth, part = grad.shape
    rows, cols = n_k * part // 2, act.shape[0] * part
    return pl.pallas_call(
        share_kernel,
        out_shape=jax.ShapeDtypeStruct((rows, cols), BF16),
        in_specs=[SMEM] + [VMEM] * 3,
        out_specs=VMEM,
        compiler_params=pltpu.CompilerParams(vmem_limit_bytes=32 * 2**20),
        cost_estimate=pl.CostEstimate(
            flops=4 * n_c * rows * cols * depth, bytes_accessed=2 * 2**20, transcendentals=0
        ),
        name="share",
    )(place, grad, act, core_act)


def on_device(activations, gradients, basis_act, basis_grad, lengths):
    n_zl, n_y, n_x, n_c, n_zh = (lax.axis_size(a) for a in ("zl", "y", "x", "c", "zh"))
    zl, y, x, c = (lax.axis_index(a) for a in ("zl", "y", "x", "c"))
    cols, group = basis_act.shape[1], n_x * activations.shape[0]

    def partner(value, axis, step):
        return lax.ppermute(value, axis, [(i, i ^ step) for i in range(lax.axis_size(axis))])

    bases = arrange_bases(n_y // 2, n_x, n_c, basis_act, basis_grad)
    act, grad = arrange_tokens(n_y // 2, n_x, n_c, n_zh, activations, gradients)
    far_bases, act = lax.optimization_barrier((partner(bases, "zl", 1), act))
    low = jnp.stack([bases, far_bases])
    low = jnp.stack([low, partner(low, "y", 4)])
    low = jnp.stack([low, partner(low, "y", 2)])
    high = partner(low, "y", 1)
    arrays = (low, high, partner(low, "c", 1), partner(high, "c", 1))

    def to_owners(tokens):
        flat = tokens.reshape(n_x * n_zh, *tokens.shape[2:])
        return lax.all_to_all(flat, ("x", "zh"), 0, 0, tiled=True).reshape(tokens.shape)

    act, grad = lax.optimization_barrier((to_owners(act), grad))
    grad = to_owners(grad)

    def unscaled(partial):
        factors = jnp.exp2(partial[..., None, -TILE:, :].astype(F32) - F32(TOP))
        partial = partial[..., :-TILE, :]
        tiles = partial.reshape(*partial.shape[:-2], -1, TILE, partial.shape[-1])
        return tiles.astype(F32) * factors

    place = jnp.stack([zl, y, c, x]).astype(jnp.int32)
    partial = rotate(0, place, lengths, act, *arrays).astype(F16)
    rot_act = unscaled(partial[0])
    for step in range(1, n_x):
        rot_act += unscaled(partner(partial[step], "x", step))
    rot_act = rot_act.astype(BF16).reshape(group, -1)

    partial = rotate(1, place, lengths, grad, *arrays).astype(F16)
    partial = unscaled(lax.all_to_all(partial, ("x", "c"), 0, 0, tiled=True))
    rot_grad = jnp.sum(partial.reshape(n_x, n_c, *partial.shape[1:]), axis=0)
    rot_grad = rot_grad.astype(BF16).reshape(n_c, group // 2, -1)
    wide_act = lax.all_gather(rot_act, "x", axis=0)
    wide_act, rot_grad = lax.optimization_barrier((wide_act, rot_grad))
    core_act = partner(wide_act, "c", 1)
    wide_grad = lax.all_gather(rot_grad, "zh", axis=0)
    share = share_of(place, wide_grad, wide_act, core_act).reshape(n_zl * n_y, -1, cols)
    received = lax.all_to_all(share, ("zl", "y"), 0, 0, tiled=True)
    received = received.astype(F32).reshape(SEQS, n_y, -1, cols)
    per_seq = jnp.sum(received, axis=1)
    scale = lengths.astype(F32)[:, None, None]
    return jnp.sum(per_seq * per_seq / scale, axis=0) / F32(SEQS)


def solution(mesh):
    split = Mesh(mesh.devices.reshape(2, 8, 4, 2, 4), ("zl", "y", "x", "c", "zh"))
    spec = P(("zl", "y", "x", "c"), "zh")
    return jax.shard_map(
        on_device, mesh=split, in_specs=(spec, spec, spec, spec, P()), out_specs=spec, check_vma=False
    )
```

```python
import jax
import jax.numpy as jnp
from jax import lax
from jax.experimental import pallas as pl
from jax.experimental.pallas import tpu as pltpu
from jax.sharding import Mesh
from jax.sharding import PartitionSpec as P

SEQS = 2
F32 = jnp.float32
BF16 = jnp.bfloat16
F16 = jnp.float16
TILE = 16
TOP = 15
VMEM = pl.BlockSpec(memory_space=pltpu.VMEM)
SMEM = pl.BlockSpec(memory_space=pltpu.SMEM)


def shift(value, axis, step):
    n = lax.axis_size(axis)
    return lax.ppermute(value, axis, [(i, (i + step) % n) for i in range(n)])


def sorting(width, outer, n_x, inner):
    run = width // (outer * n_x * inner)
    source = lax.broadcasted_iota(jnp.int32, (width, width), 0)
    target = lax.broadcasted_iota(jnp.int32, (width, width), 1)
    at_run, at_inner = source % run, source // run % inner
    at_x, at_outer = source // (run * inner) % n_x, source // (run * inner * n_x)
    moved = ((at_x * inner + at_inner) * outer + at_outer) * run + at_run
    return (moved == target).astype(F32).astype(BF16)


def spread(value, ones):
    return jnp.dot(value, ones, preferred_element_type=F32).astype(BF16)


def bases_kernel(y_lo, n_x, n_c, act, grad, out, held, sems):
    copies = [
        pltpu.make_async_copy(ref, held.at[i], sems.at[i]) for i, ref in enumerate((act, grad))
    ]
    for copy in copies:
        copy.start()
    by_owner = sorting(held.shape[2], y_lo, n_x, n_c)
    for copy in copies:
        copy.wait()
    out[0] = held[0]
    out[1] = spread(held[1], by_owner)


def arrange_bases(y_lo, n_x, n_c, act, grad):
    return pl.pallas_call(
        lambda *refs: bases_kernel(y_lo, n_x, n_c, *refs),
        out_shape=jax.ShapeDtypeStruct((2, *act.shape), BF16),
        in_specs=[pl.BlockSpec(memory_space=pl.ANY)] * 2,
        out_specs=VMEM,
        scratch_shapes=[pltpu.VMEM((2, *act.shape), BF16), pltpu.SemaphoreType.DMA((2,))],
        compiler_params=pltpu.CompilerParams(vmem_limit_bytes=60 * 2**20),
        cost_estimate=pl.CostEstimate(
            flops=2 * act.shape[0] * act.shape[1] ** 2, bytes_accessed=2**17, transcendentals=0
        ),
        name="arrange_bases",
    )(act, grad)


def tokens_kernel(y_lo, act, grad, tokens, held, in_sems, moved, out_sems):
    copies = [
        pltpu.make_async_copy(ref, held.at[i], in_sems.at[i]) for i, ref in enumerate((act, grad))
    ]
    for copy in copies:
        copy.start()
    n_x, n_zh, _, toks, width = tokens.shape
    run = width // y_lo
    for copy in copies:
        copy.wait()
    sent = []
    for x in range(n_x):
        for which in range(2):
            runs = [
                held[which, :, (y * n_x + x) * run : (y * n_x + x + 1) * run] for y in range(y_lo)
            ]
            moved[x, which] = jnp.concatenate(runs, axis=1)
        for zh in range(n_zh):
            sent.append(pltpu.make_async_copy(moved.at[x], tokens.at[x, zh], out_sems.at[x, zh]))
            sent[-1].start()
    for copy in sent:
        copy.wait()


def arrange_tokens(y_lo, n_x, n_zh, act, grad):
    toks, feats = act.shape
    return pl.pallas_call(
        lambda *refs: tokens_kernel(y_lo, *refs),
        out_shape=jax.ShapeDtypeStruct((n_x, n_zh, 2, toks, feats // n_x), BF16),
        in_specs=[pl.BlockSpec(memory_space=pl.ANY)] * 2,
        out_specs=pl.BlockSpec(memory_space=pl.ANY),
        scratch_shapes=[
            pltpu.VMEM((2, toks, feats), BF16),
            pltpu.SemaphoreType.DMA((2,)),
            pltpu.VMEM((n_x, 2, toks, feats // n_x), BF16),
            pltpu.SemaphoreType.DMA((n_x, n_zh)),
        ],
        compiler_params=pltpu.CompilerParams(vmem_limit_bytes=60 * 2**20),
        cost_estimate=pl.CostEstimate(
            flops=toks * feats, bytes_accessed=2**20, transcendentals=0
        ),
        name="arrange_tokens",
    )(act, grad)


def rotate_kernel(place, lengths, tokens, low, high, core_low, core_high, out, whole):
    n_x, n_zh, _, toks, width = tokens.shape
    rows, cols = low.shape[4], low.shape[5]
    group, part = n_x * toks, cols // n_x
    zl, y, c = place[0], place[1], place[2]
    sums = []
    for which in range(2):
        for one, pair in enumerate(((low, core_low), (high, core_high))):
            for two in range(2):
                for four in range(2):
                    from_y = y ^ (four * 4 + two * 2 + one)
                    for far in range(2):
                        owner = (zl ^ far) * 2 + from_y // 4
                        for ref, core in zip(pair, (c, 1 - c)):
                            at = pl.multiple_of((from_y % 4 * 2 + core) * rows, rows)
                            whole[which, owner, pl.ds(at, rows)] = ref[two, four, far, which]
        total = None
        for owner in range(n_zh):
            left = tokens[:, owner, which].reshape(group, width)
            product = jnp.dot(left, whole[which, owner], preferred_element_type=F32)
            total = product if total is None else total + product
        sums.append(total)
    index = lax.broadcasted_iota(jnp.int32, (group, 1), 0)
    position = ((y * n_x + index // toks) * 2 + c) * toks + index % toks
    sums[0] = jnp.where(position < lengths[zl], sums[0], 0.0)
    largest = jnp.max(jnp.maximum(jnp.abs(sums[0]), jnp.abs(sums[1])), axis=0, keepdims=True)
    largest = jnp.max(largest, axis=1, keepdims=True)
    level = jnp.clip(jnp.ceil(jnp.log2(jnp.maximum(largest, 1e-30))), -100.0, 100.0)
    act, grad = (total * jnp.exp2(F32(TOP) - level) for total in sums)
    half = group // 2
    for x in range(n_x):
        for core in range(2):
            piece = 2 * x + core
            out[piece, pl.ds(0, half)] = act[core * half : (core + 1) * half, x * part : (x + 1) * part]
            value = grad[:, piece * part // 2 : (piece + 1) * part // 2]
            out[piece, pl.ds(half, half)] = jnp.concatenate([value[:half], value[half:]], axis=1)
            out[piece, pl.ds(group, TILE)] = jnp.broadcast_to(level, (TILE, part))


def rotate(place, lengths, *arrays):
    n_x, n_zh, _, toks, width = arrays[0].shape
    cols = arrays[1].shape[5]
    return pl.pallas_call(
        rotate_kernel,
        out_shape=jax.ShapeDtypeStruct((2 * n_x, n_x * toks + TILE, cols // n_x), F32),
        in_specs=[SMEM] * 2 + [VMEM] * len(arrays),
        out_specs=VMEM,
        scratch_shapes=[pltpu.VMEM((2, n_zh, width, cols), BF16)],
        compiler_params=pltpu.CompilerParams(vmem_limit_bytes=40 * 2**20),
        cost_estimate=pl.CostEstimate(
            flops=4 * n_x * n_zh * toks * width * cols, bytes_accessed=8 * 2**20, transcendentals=0
        ),
        name="rotate",
    )(place, lengths, *arrays)


def share_kernel(grad, act, out):
    n_k, n_c, depth, part = grad.shape
    n_x, half = act.shape[0], part // 2
    total = None
    for core in range(n_c):
        turned = [grad[k, core].T for k in range(n_k)]
        for side in range(2):
            left = jnp.concatenate([t[side * half : (side + 1) * half] for t in turned], axis=0)
            right = jnp.concatenate([act[x, side, core] for x in range(n_x)], axis=1)
            product = jnp.dot(left, right, preferred_element_type=F32)
            total = product if total is None else total + product
    out[...] = total.astype(BF16)


def share_of(grad, act):
    n_k, n_c, depth, part = grad.shape
    rows, cols = n_k * part // 2, act.shape[0] * part
    return pl.pallas_call(
        share_kernel,
        out_shape=jax.ShapeDtypeStruct((rows, cols), BF16),
        in_specs=[VMEM, VMEM],
        out_specs=VMEM,
        compiler_params=pltpu.CompilerParams(vmem_limit_bytes=16 * 2**20),
        cost_estimate=pl.CostEstimate(
            flops=4 * n_c * rows * cols * depth, bytes_accessed=2 * 2**20, transcendentals=0
        ),
        name="share",
    )(grad, act)


def on_device(activations, gradients, basis_act, basis_grad, lengths):
    n_zl, n_y, n_x, n_c, n_zh = (lax.axis_size(a) for a in ("zl", "y", "x", "c", "zh"))
    zl, y, c = (lax.axis_index(a) for a in ("zl", "y", "c"))
    cols, group = basis_act.shape[1], n_x * activations.shape[0]

    def partner(value, step):
        return lax.ppermute(value, "y", [(i, i ^ step) for i in range(n_y)])

    bases = arrange_bases(n_y // 2, n_x, n_c, basis_act, basis_grad)
    tokens = arrange_tokens(n_y // 2, n_x, n_zh, activations, gradients)
    far_bases, tokens = lax.optimization_barrier((shift(bases, "zl", 1), tokens))
    low = jnp.stack([bases, far_bases])
    low = jnp.stack([low, partner(low, 4)])
    low = jnp.stack([low, partner(low, 2)])
    high = partner(low, 1)
    core_low, core_high = shift(low, "c", 1), shift(high, "c", 1)

    tokens = lax.all_to_all(
        tokens.reshape(n_x * n_zh, *tokens.shape[2:]), ("x", "zh"), 0, 0, tiled=True
    ).reshape(tokens.shape)

    place = jnp.stack([zl, y, c]).astype(jnp.int32)
    arrays = (lengths, tokens, low, high, core_low, core_high)
    partial = rotate(place, *arrays).astype(F16)
    partial = lax.all_to_all(partial, ("x", "c"), 0, 0, tiled=True)
    factors = jnp.exp2(partial[:, None, -TILE:].astype(F32) - F32(TOP))
    partial = partial[:, :-TILE].reshape(n_x * n_c, -1, TILE, partial.shape[2]).astype(F32)
    partial = (partial * factors).reshape(n_x, n_c, *partial.shape[1:])
    rotated = jnp.sum(partial, axis=0).astype(BF16).reshape(n_c, group, -1)
    rot_act, rot_grad = rotated[:, : group // 2], rotated[:, group // 2 :]

    wide_act = lax.all_to_all(
        jnp.broadcast_to(rot_act[None], (n_x * n_c, *rot_act.shape)), ("x", "c"), 0, 0, tiled=True
    ).reshape(n_x, n_c, *rot_act.shape)
    wide_grad = lax.all_gather(rot_grad, "zh", axis=0)
    share = share_of(wide_grad, wide_act).reshape(n_zl * n_y, -1, cols)
    received = lax.all_to_all(share, ("zl", "y"), 0, 0, tiled=True)
    received = received.astype(F32).reshape(SEQS, n_y, -1, cols)
    per_seq = jnp.sum(received, axis=1)
    scale = lengths.astype(F32)[:, None, None]
    return jnp.sum(per_seq * per_seq / scale, axis=0) / F32(SEQS)


def solution(mesh):
    split = Mesh(mesh.devices.reshape(2, 8, 4, 2, 4), ("zl", "y", "x", "c", "zh"))
    spec = P(("zl", "y", "x", "c"), "zh")
    return jax.shard_map(
        on_device, mesh=split, in_specs=(spec, spec, spec, spec, P()), out_specs=spec, check_vma=False
    )
```

```python
import jax
import jax.numpy as jnp
from jax import lax
from jax.experimental import pallas as pl
from jax.experimental.pallas import tpu as pltpu
from jax.sharding import Mesh
from jax.sharding import PartitionSpec as P

SEQS = 2
F32 = jnp.float32
BF16 = jnp.bfloat16
F16 = jnp.float16
TILE = 16
TOP = 15
VMEM = pl.BlockSpec(memory_space=pltpu.VMEM)
SMEM = pl.BlockSpec(memory_space=pltpu.SMEM)


def shift(value, axis, step):
    n = lax.axis_size(axis)
    return lax.ppermute(value, axis, [(i, (i + step) % n) for i in range(n)])


def sorting(width, outer, n_x, inner):
    run = width // (outer * n_x * inner)
    source = lax.broadcasted_iota(jnp.int32, (width, width), 0)
    target = lax.broadcasted_iota(jnp.int32, (width, width), 1)
    at_run, at_inner = source % run, source // run % inner
    at_x, at_outer = source // (run * inner) % n_x, source // (run * inner * n_x)
    moved = ((at_x * inner + at_inner) * outer + at_outer) * run + at_run
    return (moved == target).astype(F32).astype(BF16)


def spread(value, ones):
    return jnp.dot(value, ones, preferred_element_type=F32).astype(BF16)


def bases_kernel(y_lo, n_x, n_c, own, far, out):
    by_owner = sorting(own.shape[2], y_lo, n_x, n_c)
    for i, ref in enumerate((own, far)):
        out[i, 0] = ref[0]
        out[i, 1] = spread(ref[1], by_owner)


def arrange_bases(y_lo, n_x, n_c, own, far):
    return pl.pallas_call(
        lambda *refs: bases_kernel(y_lo, n_x, n_c, *refs),
        out_shape=jax.ShapeDtypeStruct((2, *own.shape), BF16),
        in_specs=[VMEM] * 2,
        out_specs=VMEM,
        compiler_params=pltpu.CompilerParams(vmem_limit_bytes=16 * 2**20),
        cost_estimate=pl.CostEstimate(
            flops=4 * own.shape[1] * own.shape[2] ** 2, bytes_accessed=2**18, transcendentals=0
        ),
        name="arrange_bases",
    )(own, far)


def tokens_kernel(y_lo, act, grad, tokens, held, in_sems, moved, out_sems):
    copies = [
        pltpu.make_async_copy(ref, held.at[i], in_sems.at[i]) for i, ref in enumerate((act, grad))
    ]
    for copy in copies:
        copy.start()
    n_x, n_zh, _, toks, width = tokens.shape
    run = width // y_lo
    sent = []
    for which in range(2):
        copies[which].wait()
        for x in range(n_x):
            runs = [
                held[which, :, (y * n_x + x) * run : (y * n_x + x + 1) * run] for y in range(y_lo)
            ]
            moved[which, x] = jnp.concatenate(runs, axis=1)
            for zh in range(n_zh):
                sent.append(
                    pltpu.make_async_copy(
                        moved.at[which, x], tokens.at[x, zh, which], out_sems.at[which, x, zh]
                    )
                )
                sent[-1].start()
    for copy in sent:
        copy.wait()


def arrange_tokens(y_lo, n_x, n_zh, act, grad):
    toks, feats = act.shape
    return pl.pallas_call(
        lambda *refs: tokens_kernel(y_lo, *refs),
        out_shape=jax.ShapeDtypeStruct((n_x, n_zh, 2, toks, feats // n_x), BF16),
        in_specs=[pl.BlockSpec(memory_space=pl.ANY)] * 2,
        out_specs=pl.BlockSpec(memory_space=pl.ANY),
        scratch_shapes=[
            pltpu.VMEM((2, toks, feats), BF16),
            pltpu.SemaphoreType.DMA((2,)),
            pltpu.VMEM((2, n_x, toks, feats // n_x), BF16),
            pltpu.SemaphoreType.DMA((2, n_x, n_zh)),
        ],
        compiler_params=pltpu.CompilerParams(vmem_limit_bytes=60 * 2**20),
        cost_estimate=pl.CostEstimate(
            flops=toks * feats, bytes_accessed=2**20, transcendentals=0
        ),
        name="arrange_tokens",
    )(act, grad)


def rotate_kernel(place, lengths, tokens, low, high, core_low, core_high, out, whole):
    n_x, n_zh, _, toks, width = tokens.shape
    rows, cols = low.shape[4], low.shape[5]
    group, part = n_x * toks, cols // n_x
    zl, y, c = place[0], place[1], place[2]
    sums = []
    for which in range(2):
        for one, pair in enumerate(((low, core_low), (high, core_high))):
            for two in range(2):
                for four in range(2):
                    from_y = y ^ (four * 4 + two * 2 + one)
                    for far in range(2):
                        owner = (zl ^ far) * 2 + from_y // 4
                        for ref, core in zip(pair, (c, 1 - c)):
                            at = pl.multiple_of((from_y % 4 * 2 + core) * rows, rows)
                            whole[which, owner, pl.ds(at, rows)] = ref[two, four, far, which]
        total = None
        for owner in range(n_zh):
            left = tokens[:, owner, which].reshape(group, width)
            product = jnp.dot(left, whole[which, owner], preferred_element_type=F32)
            total = product if total is None else total + product
        sums.append(total)
    index = lax.broadcasted_iota(jnp.int32, (group, 1), 0)
    position = ((y * n_x + index // toks) * 2 + c) * toks + index % toks
    sums[0] = jnp.where(position < lengths[zl], sums[0], 0.0)
    largest = jnp.max(jnp.maximum(jnp.abs(sums[0]), jnp.abs(sums[1])), axis=0, keepdims=True)
    largest = jnp.max(largest, axis=1, keepdims=True)
    level = jnp.clip(jnp.ceil(jnp.log2(jnp.maximum(largest, 1e-30))), -100.0, 100.0)
    act, grad = (total * jnp.exp2(F32(TOP) - level) for total in sums)
    half = group // 2
    for x in range(n_x):
        for core in range(2):
            piece = 2 * x + core
            out[piece, pl.ds(0, half)] = act[core * half : (core + 1) * half, x * part : (x + 1) * part]
            value = grad[:, piece * part // 2 : (piece + 1) * part // 2]
            out[piece, pl.ds(half, half)] = jnp.concatenate([value[:half], value[half:]], axis=1)
            out[piece, pl.ds(group, TILE)] = jnp.broadcast_to(level, (TILE, part))


def rotate(place, lengths, *arrays):
    n_x, n_zh, _, toks, width = arrays[0].shape
    cols = arrays[1].shape[5]
    return pl.pallas_call(
        rotate_kernel,
        out_shape=jax.ShapeDtypeStruct((2 * n_x, n_x * toks + TILE, cols // n_x), F32),
        in_specs=[SMEM] * 2 + [VMEM] * len(arrays),
        out_specs=VMEM,
        scratch_shapes=[pltpu.VMEM((2, n_zh, width, cols), BF16)],
        compiler_params=pltpu.CompilerParams(vmem_limit_bytes=40 * 2**20),
        cost_estimate=pl.CostEstimate(
            flops=4 * n_x * n_zh * toks * width * cols, bytes_accessed=8 * 2**20, transcendentals=0
        ),
        name="rotate",
    )(place, lengths, *arrays)


def share_kernel(grad, act, out):
    n_k, n_c, depth, part = grad.shape
    n_x, half = act.shape[0], part // 2
    total = None
    for core in range(n_c):
        turned = [grad[k, core].T for k in range(n_k)]
        for side in range(2):
            left = jnp.concatenate([t[side * half : (side + 1) * half] for t in turned], axis=0)
            right = jnp.concatenate([act[x, side, core] for x in range(n_x)], axis=1)
            product = jnp.dot(left, right, preferred_element_type=F32)
            total = product if total is None else total + product
    out[...] = total.astype(BF16)


def share_of(grad, act):
    n_k, n_c, depth, part = grad.shape
    rows, cols = n_k * part // 2, act.shape[0] * part
    return pl.pallas_call(
        share_kernel,
        out_shape=jax.ShapeDtypeStruct((rows, cols), BF16),
        in_specs=[VMEM, VMEM],
        out_specs=VMEM,
        compiler_params=pltpu.CompilerParams(vmem_limit_bytes=16 * 2**20),
        cost_estimate=pl.CostEstimate(
            flops=4 * n_c * rows * cols * depth, bytes_accessed=2 * 2**20, transcendentals=0
        ),
        name="share",
    )(grad, act)


def on_device(activations, gradients, basis_act, basis_grad, lengths):
    n_zl, n_y, n_x, n_c, n_zh = (lax.axis_size(a) for a in ("zl", "y", "x", "c", "zh"))
    zl, y, c = (lax.axis_index(a) for a in ("zl", "y", "c"))
    cols, group = basis_act.shape[1], n_x * activations.shape[0]

    def partner(value, step):
        return lax.ppermute(value, "y", [(i, i ^ step) for i in range(n_y)])

    raw = jnp.stack([basis_act, basis_grad])
    raw, activations = lax.optimization_barrier((raw, activations))
    far = shift(raw, "zl", 1)
    tokens = arrange_tokens(n_y // 2, n_x, n_zh, activations, gradients)
    far, tokens = lax.optimization_barrier((far, tokens))
    low = arrange_bases(n_y // 2, n_x, n_c, raw, far)
    low = jnp.stack([low, partner(low, 4)])
    low = jnp.stack([low, partner(low, 2)])
    high = partner(low, 1)
    core_low, core_high = shift(low, "c", 1), shift(high, "c", 1)

    tokens = lax.all_to_all(
        tokens.reshape(n_x * n_zh, *tokens.shape[2:]), ("x", "zh"), 0, 0, tiled=True
    ).reshape(tokens.shape)

    place = jnp.stack([zl, y, c]).astype(jnp.int32)
    arrays = (lengths, tokens, low, high, core_low, core_high)
    partial = rotate(place, *arrays).astype(F16)
    partial = lax.all_to_all(partial, ("x", "c"), 0, 0, tiled=True)
    factors = jnp.exp2(partial[:, None, -TILE:].astype(F32) - F32(TOP))
    partial = partial[:, :-TILE].reshape(n_x * n_c, -1, TILE, partial.shape[2]).astype(F32)
    partial = (partial * factors).reshape(n_x, n_c, *partial.shape[1:])
    rotated = jnp.sum(partial, axis=0).astype(BF16).reshape(n_c, group, -1)
    rot_act, rot_grad = rotated[:, : group // 2], rotated[:, group // 2 :]

    wide_act = lax.all_to_all(
        jnp.broadcast_to(rot_act[None], (n_x * n_c, *rot_act.shape)), ("x", "c"), 0, 0, tiled=True
    ).reshape(n_x, n_c, *rot_act.shape)
    wide_grad = lax.all_gather(rot_grad, "zh", axis=0)
    share = share_of(wide_grad, wide_act).reshape(n_zl * n_y, -1, cols)
    received = lax.all_to_all(share, ("zl", "y"), 0, 0, tiled=True)
    received = received.astype(F32).reshape(SEQS, n_y, -1, cols)
    per_seq = jnp.sum(received, axis=1)
    scale = lengths.astype(F32)[:, None, None]
    return jnp.sum(per_seq * per_seq / scale, axis=0) / F32(SEQS)


def solution(mesh):
    split = Mesh(mesh.devices.reshape(2, 8, 4, 2, 4), ("zl", "y", "x", "c", "zh"))
    spec = P(("zl", "y", "x", "c"), "zh")
    return jax.shard_map(
        on_device, mesh=split, in_specs=(spec, spec, spec, spec, P()), out_specs=spec, check_vma=False
    )
```

```python
import jax
import jax.numpy as jnp
from jax import lax
from jax.experimental import pallas as pl
from jax.experimental.pallas import tpu as pltpu
from jax.sharding import Mesh
from jax.sharding import PartitionSpec as P

SEQS = 2
F32 = jnp.float32
BF16 = jnp.bfloat16
F16 = jnp.float16
TILE = 16
TOP = 15
VMEM = pl.BlockSpec(memory_space=pltpu.VMEM)
SMEM = pl.BlockSpec(memory_space=pltpu.SMEM)


def shift(value, axis, step):
    n = lax.axis_size(axis)
    return lax.ppermute(value, axis, [(i, (i + step) % n) for i in range(n)])


def sorting(width, outer, n_x, inner):
    run = width // (outer * n_x * inner)
    source = lax.broadcasted_iota(jnp.int32, (width, width), 0)
    target = lax.broadcasted_iota(jnp.int32, (width, width), 1)
    at_run, at_inner = source % run, source // run % inner
    at_x, at_outer = source // (run * inner) % n_x, source // (run * inner * n_x)
    moved = ((at_x * inner + at_inner) * outer + at_outer) * run + at_run
    return (moved == target).astype(F32).astype(BF16)


def spread(value, ones):
    return jnp.dot(value, ones, preferred_element_type=F32).astype(BF16)


def bases_kernel(y_lo, n_x, n_c, own, far, out):
    by_owner = sorting(own.shape[2], y_lo, n_x, n_c)
    for i, ref in enumerate((own, far)):
        out[i, 0] = ref[0]
        out[i, 1] = spread(ref[1], by_owner)


def arrange_bases(y_lo, n_x, n_c, own, far):
    return pl.pallas_call(
        lambda *refs: bases_kernel(y_lo, n_x, n_c, *refs),
        out_shape=jax.ShapeDtypeStruct((2, *own.shape), BF16),
        in_specs=[VMEM] * 2,
        out_specs=VMEM,
        compiler_params=pltpu.CompilerParams(vmem_limit_bytes=16 * 2**20),
        cost_estimate=pl.CostEstimate(
            flops=4 * own.shape[1] * own.shape[2] ** 2, bytes_accessed=2**18, transcendentals=0
        ),
        name="arrange_bases",
    )(own, far)


def tokens_kernel(y_lo, act, grad, tokens, held, in_sems, moved, out_sems):
    copies = [
        pltpu.make_async_copy(ref, held.at[i], in_sems.at[i]) for i, ref in enumerate((act, grad))
    ]
    for copy in copies:
        copy.start()
    n_zh, n_x, _, toks, width = tokens.shape
    run = width // y_lo
    sent = []
    for which in range(2):
        copies[which].wait()
        for x in range(n_x):
            runs = [
                held[which, :, (y * n_x + x) * run : (y * n_x + x + 1) * run] for y in range(y_lo)
            ]
            moved[which, x] = jnp.concatenate(runs, axis=1)
            for zh in range(n_zh):
                sent.append(
                    pltpu.make_async_copy(
                        moved.at[which, x], tokens.at[zh, x, which], out_sems.at[which, x, zh]
                    )
                )
                sent[-1].start()
    for copy in sent:
        copy.wait()


def arrange_tokens(y_lo, n_x, n_zh, act, grad):
    toks, feats = act.shape
    return pl.pallas_call(
        lambda *refs: tokens_kernel(y_lo, *refs),
        out_shape=jax.ShapeDtypeStruct((n_zh, n_x, 2, toks, feats // n_x), BF16),
        in_specs=[pl.BlockSpec(memory_space=pl.ANY)] * 2,
        out_specs=pl.BlockSpec(memory_space=pl.ANY),
        scratch_shapes=[
            pltpu.VMEM((2, toks, feats), BF16),
            pltpu.SemaphoreType.DMA((2,)),
            pltpu.VMEM((2, n_x, toks, feats // n_x), BF16),
            pltpu.SemaphoreType.DMA((2, n_x, n_zh)),
        ],
        compiler_params=pltpu.CompilerParams(vmem_limit_bytes=60 * 2**20),
        cost_estimate=pl.CostEstimate(
            flops=toks * feats, bytes_accessed=2**20, transcendentals=0
        ),
        name="arrange_tokens",
    )(act, grad)


def rotate_kernel(place, lengths, tokens, low, high, core_low, core_high, out, whole):
    n_zh, n_x, _, toks, width = tokens.shape
    rows, cols = low.shape[4], low.shape[5]
    group, part = n_x * toks, cols // n_x
    zl, y, c = place[0], place[1], place[2]
    sums = []
    for which in range(2):
        for one, pair in enumerate(((low, core_low), (high, core_high))):
            for two in range(2):
                for four in range(2):
                    from_y = y ^ (four * 4 + two * 2 + one)
                    for far in range(2):
                        owner = (zl ^ far) * 2 + from_y // 4
                        for ref, core in zip(pair, (c, 1 - c)):
                            at = pl.multiple_of((from_y % 4 * 2 + core) * rows, rows)
                            whole[which, owner, pl.ds(at, rows)] = ref[two, four, far, which]
        total = None
        for owner in range(n_zh):
            left = tokens[owner, :, which].reshape(group, width)
            product = jnp.dot(left, whole[which, owner], preferred_element_type=F32)
            total = product if total is None else total + product
        sums.append(total)
    index = lax.broadcasted_iota(jnp.int32, (group, 1), 0)
    position = ((y * n_x + index // toks) * 2 + c) * toks + index % toks
    sums[0] = jnp.where(position < lengths[zl], sums[0], 0.0)
    largest = jnp.max(jnp.maximum(jnp.abs(sums[0]), jnp.abs(sums[1])), axis=0, keepdims=True)
    largest = jnp.max(largest, axis=1, keepdims=True)
    level = jnp.clip(jnp.ceil(jnp.log2(jnp.maximum(largest, 1e-30))), -100.0, 100.0)
    act, grad = (total * jnp.exp2(F32(TOP) - level) for total in sums)
    half = group // 2
    for x in range(n_x):
        for core in range(2):
            piece, to = 2 * x + core, core * n_x + x
            out[to, pl.ds(0, half)] = act[core * half : (core + 1) * half, x * part : (x + 1) * part]
            value = grad[:, piece * part // 2 : (piece + 1) * part // 2]
            out[to, pl.ds(half, half)] = jnp.concatenate([value[:half], value[half:]], axis=1)
            out[to, pl.ds(group, TILE)] = jnp.broadcast_to(level, (TILE, part))


def rotate(place, lengths, *arrays):
    n_zh, n_x, _, toks, width = arrays[0].shape
    cols = arrays[1].shape[5]
    return pl.pallas_call(
        rotate_kernel,
        out_shape=jax.ShapeDtypeStruct((2 * n_x, n_x * toks + TILE, cols // n_x), F32),
        in_specs=[SMEM] * 2 + [VMEM] * len(arrays),
        out_specs=VMEM,
        scratch_shapes=[pltpu.VMEM((2, n_zh, width, cols), BF16)],
        compiler_params=pltpu.CompilerParams(vmem_limit_bytes=40 * 2**20),
        cost_estimate=pl.CostEstimate(
            flops=4 * n_x * n_zh * toks * width * cols, bytes_accessed=8 * 2**20, transcendentals=0
        ),
        name="rotate",
    )(place, lengths, *arrays)


def share_kernel(grad, act, out):
    n_k, n_c, depth, part = grad.shape
    n_x, half = act.shape[1], part // 2
    total = None
    for core in range(n_c):
        turned = [grad[k, core].T for k in range(n_k)]
        for side in range(2):
            left = jnp.concatenate([t[side * half : (side + 1) * half] for t in turned], axis=0)
            right = jnp.concatenate([act[side, x, core] for x in range(n_x)], axis=1)
            product = jnp.dot(left, right, preferred_element_type=F32)
            total = product if total is None else total + product
    rows = out.shape[2]
    for z in range(2):
        for y in range(out.shape[0]):
            at = (z * out.shape[0] + y) * rows
            out[y, z] = total[at : at + rows].astype(BF16)


def share_of(n_y, grad, act):
    n_k, n_c, depth, part = grad.shape
    rows, cols = n_k * part // 2, act.shape[1] * part
    return pl.pallas_call(
        share_kernel,
        out_shape=jax.ShapeDtypeStruct((n_y, 2, rows // n_y // 2, cols), BF16),
        in_specs=[VMEM, VMEM],
        out_specs=VMEM,
        compiler_params=pltpu.CompilerParams(vmem_limit_bytes=16 * 2**20),
        cost_estimate=pl.CostEstimate(
            flops=4 * n_c * rows * cols * depth, bytes_accessed=2 * 2**20, transcendentals=0
        ),
        name="share",
    )(grad, act)


def on_device(activations, gradients, basis_act, basis_grad, lengths):
    n_zl, n_y, n_x, n_c, n_zh = (lax.axis_size(a) for a in ("zl", "y", "x", "c", "zh"))
    zl, y, c = (lax.axis_index(a) for a in ("zl", "y", "c"))
    cols, group = basis_act.shape[1], n_x * activations.shape[0]

    def partner(value, step):
        return lax.ppermute(value, "y", [(i, i ^ step) for i in range(n_y)])

    raw = jnp.stack([basis_act, basis_grad])
    raw, activations = lax.optimization_barrier((raw, activations))
    far = shift(raw, "zl", 1)
    tokens = arrange_tokens(n_y // 2, n_x, n_zh, activations, gradients)
    far, tokens = lax.optimization_barrier((far, tokens))
    low = arrange_bases(n_y // 2, n_x, n_c, raw, far)
    low = jnp.stack([low, partner(low, 4)])
    low = jnp.stack([low, partner(low, 2)])
    high = partner(low, 1)
    core_low, core_high = shift(low, "c", 1), shift(high, "c", 1)

    tokens = lax.all_to_all(
        tokens.reshape(n_x * n_zh, *tokens.shape[2:]), ("zh", "x"), 0, 0, tiled=True
    ).reshape(tokens.shape)

    place = jnp.stack([zl, y, c]).astype(jnp.int32)
    arrays = (lengths, tokens, low, high, core_low, core_high)
    partial = rotate(place, *arrays).astype(F16)
    partial = lax.all_to_all(partial, ("c", "x"), 0, 0, tiled=True)
    factors = jnp.exp2(partial[:, None, -TILE:].astype(F32) - F32(TOP))
    partial = partial[:, :-TILE].reshape(n_x * n_c, -1, TILE, partial.shape[2]).astype(F32)
    partial = (partial * factors).reshape(n_c, n_x, *partial.shape[1:])
    rotated = jnp.sum(partial, axis=1).astype(BF16).reshape(n_c, group, -1)
    rot_act, rot_grad = rotated[:, : group // 2], rotated[:, group // 2 :]

    wide_act = lax.all_to_all(
        jnp.broadcast_to(rot_act[None], (n_c * n_x, *rot_act.shape)), ("c", "x"), 0, 0, tiled=True
    ).reshape(n_c, n_x, *rot_act.shape)
    wide_grad = lax.all_gather(rot_grad, "zh", axis=0)
    share = share_of(n_y, wide_grad, wide_act).reshape(n_y * n_zl, -1, cols)
    received = lax.all_to_all(share, ("y", "zl"), 0, 0, tiled=True)
    received = received.astype(F32).reshape(n_y, SEQS, -1, cols)
    per_seq = jnp.sum(received, axis=0)
    scale = lengths.astype(F32)[:, None, None]
    return jnp.sum(per_seq * per_seq / scale, axis=0) / F32(SEQS)


def solution(mesh):
    split = Mesh(mesh.devices.reshape(2, 8, 4, 2, 4), ("zl", "y", "x", "c", "zh"))
    spec = P(("zl", "y", "x", "c"), "zh")
    return jax.shard_map(
        on_device, mesh=split, in_specs=(spec, spec, spec, spec, P()), out_specs=spec, check_vma=False
    )
```

```python
import jax
import jax.numpy as jnp
from jax import lax
from jax.experimental import pallas as pl
from jax.experimental.pallas import tpu as pltpu
from jax.sharding import Mesh
from jax.sharding import PartitionSpec as P

SEQS = 2
F32 = jnp.float32
BF16 = jnp.bfloat16
F16 = jnp.float16
TILE = 16
TOP = 15
VMEM = pl.BlockSpec(memory_space=pltpu.VMEM)
SMEM = pl.BlockSpec(memory_space=pltpu.SMEM)


def shift(value, axis, step):
    n = lax.axis_size(axis)
    return lax.ppermute(value, axis, [(i, (i + step) % n) for i in range(n)])


def sorting(width, outer, n_x, inner):
    run = width // (outer * n_x * inner)
    source = lax.broadcasted_iota(jnp.int32, (width, width), 0)
    target = lax.broadcasted_iota(jnp.int32, (width, width), 1)
    at_run, at_inner = source % run, source // run % inner
    at_x, at_outer = source // (run * inner) % n_x, source // (run * inner * n_x)
    moved = ((at_x * inner + at_inner) * outer + at_outer) * run + at_run
    return (moved == target).astype(F32).astype(BF16)


def spread(value, ones):
    return jnp.dot(value, ones, preferred_element_type=F32).astype(BF16)


def bases_kernel(y_lo, n_x, n_c, own, far, out):
    by_owner = sorting(own.shape[2], y_lo, n_x, n_c)
    for i, ref in enumerate((own, far)):
        out[i, 0] = ref[0]
        out[i, 1] = spread(ref[1], by_owner)


def arrange_bases(y_lo, n_x, n_c, own, far):
    return pl.pallas_call(
        lambda *refs: bases_kernel(y_lo, n_x, n_c, *refs),
        out_shape=jax.ShapeDtypeStruct((2, *own.shape), BF16),
        in_specs=[VMEM] * 2,
        out_specs=VMEM,
        compiler_params=pltpu.CompilerParams(vmem_limit_bytes=16 * 2**20),
        cost_estimate=pl.CostEstimate(
            flops=4 * own.shape[1] * own.shape[2] ** 2, bytes_accessed=2**18, transcendentals=0
        ),
        name="arrange_bases",
    )(own, far)


def tokens_kernel(y_lo, act, grad, tokens, held, in_sems, moved, out_sems):
    copies = [
        pltpu.make_async_copy(ref, held.at[i], in_sems.at[i]) for i, ref in enumerate((act, grad))
    ]
    for copy in copies:
        copy.start()
    n_zh, n_x, _, toks, width = tokens.shape
    run = width // y_lo
    sent = []
    for which in range(2):
        copies[which].wait()
        for x in range(n_x):
            runs = [
                held[which, :, (y * n_x + x) * run : (y * n_x + x + 1) * run] for y in range(y_lo)
            ]
            moved[which, x] = jnp.concatenate(runs, axis=1)
            for zh in range(n_zh):
                sent.append(
                    pltpu.make_async_copy(
                        moved.at[which, x], tokens.at[zh, x, which], out_sems.at[which, x, zh]
                    )
                )
                sent[-1].start()
    for copy in sent:
        copy.wait()


def arrange_tokens(y_lo, n_x, n_zh, act, grad):
    toks, feats = act.shape
    return pl.pallas_call(
        lambda *refs: tokens_kernel(y_lo, *refs),
        out_shape=jax.ShapeDtypeStruct((n_zh, n_x, 2, toks, feats // n_x), BF16),
        in_specs=[pl.BlockSpec(memory_space=pl.ANY)] * 2,
        out_specs=pl.BlockSpec(memory_space=pl.ANY),
        scratch_shapes=[
            pltpu.VMEM((2, toks, feats), BF16),
            pltpu.SemaphoreType.DMA((2,)),
            pltpu.VMEM((2, n_x, toks, feats // n_x), BF16),
            pltpu.SemaphoreType.DMA((2, n_x, n_zh)),
        ],
        compiler_params=pltpu.CompilerParams(vmem_limit_bytes=60 * 2**20),
        cost_estimate=pl.CostEstimate(
            flops=toks * feats, bytes_accessed=2**20, transcendentals=0
        ),
        name="arrange_tokens",
    )(act, grad)


def rotate_kernel(place, lengths, tokens, low, high, core_low, core_high, out, whole):
    n_zh, n_x, _, toks, width = tokens.shape
    rows, cols = low.shape[4], low.shape[5]
    group, part = n_x * toks, cols // n_x
    zl, y, c = place[0], place[1], place[2]
    sums = []
    for which in range(2):
        for one, pair in enumerate(((low, core_low), (high, core_high))):
            for two in range(2):
                for four in range(2):
                    from_y = y ^ (four * 4 + two * 2 + one)
                    for far in range(2):
                        owner = (zl ^ far) * 2 + from_y // 4
                        for ref, core in zip(pair, (c, 1 - c)):
                            at = pl.multiple_of((from_y % 4 * 2 + core) * rows, rows)
                            whole[which, owner, pl.ds(at, rows)] = ref[two, four, far, which]
        total = None
        for owner in range(n_zh):
            left = tokens[owner, :, which].reshape(group, width)
            product = jnp.dot(left, whole[which, owner], preferred_element_type=F32)
            total = product if total is None else total + product
        sums.append(total)
    index = lax.broadcasted_iota(jnp.int32, (group, 1), 0)
    position = ((y * n_x + index // toks) * 2 + c) * toks + index % toks
    sums[0] = jnp.where(position < lengths[zl], sums[0], 0.0)
    largest = jnp.max(jnp.maximum(jnp.abs(sums[0]), jnp.abs(sums[1])), axis=0, keepdims=True)
    largest = jnp.max(largest, axis=1, keepdims=True)
    level = jnp.clip(jnp.ceil(jnp.log2(jnp.maximum(largest, 1e-30))), -100.0, 100.0)
    act, grad = (total * jnp.exp2(F32(TOP) - level) for total in sums)
    half = group // 2
    for x in range(n_x):
        for core in range(2):
            piece, to = 2 * x + core, core * n_x + x
            out[to, pl.ds(0, half)] = act[core * half : (core + 1) * half, x * part : (x + 1) * part]
            value = grad[:, piece * part // 2 : (piece + 1) * part // 2]
            out[to, pl.ds(half, half)] = jnp.concatenate([value[:half], value[half:]], axis=1)
            out[to, pl.ds(group, TILE)] = jnp.broadcast_to(level, (TILE, part))


def rotate(place, lengths, *arrays):
    n_zh, n_x, _, toks, width = arrays[0].shape
    cols = arrays[1].shape[5]
    return pl.pallas_call(
        rotate_kernel,
        out_shape=jax.ShapeDtypeStruct((2 * n_x, n_x * toks + TILE, cols // n_x), F32),
        in_specs=[SMEM] * 2 + [VMEM] * len(arrays),
        out_specs=VMEM,
        scratch_shapes=[pltpu.VMEM((2, n_zh, width, cols), BF16)],
        compiler_params=pltpu.CompilerParams(vmem_limit_bytes=40 * 2**20),
        cost_estimate=pl.CostEstimate(
            flops=4 * n_x * n_zh * toks * width * cols, bytes_accessed=8 * 2**20, transcendentals=0
        ),
        name="rotate",
    )(place, lengths, *arrays)


def share_kernel(grad, act, out):
    n_k, n_c, depth, part = grad.shape
    n_x, half = act.shape[1], part // 2
    total = None
    for core in range(n_c):
        turned = [grad[k, core].T for k in range(n_k)]
        for side in range(2):
            left = jnp.concatenate([t[side * half : (side + 1) * half] for t in turned], axis=0)
            right = jnp.concatenate([act[side, x, core] for x in range(n_x)], axis=1)
            product = jnp.dot(left, right, preferred_element_type=F32)
            total = product if total is None else total + product
    out[...] = total.astype(BF16)


def share_of(grad, act):
    n_k, n_c, depth, part = grad.shape
    rows, cols = n_k * part // 2, act.shape[1] * part
    return pl.pallas_call(
        share_kernel,
        out_shape=jax.ShapeDtypeStruct((rows, cols), BF16),
        in_specs=[VMEM, VMEM],
        out_specs=VMEM,
        compiler_params=pltpu.CompilerParams(vmem_limit_bytes=16 * 2**20),
        cost_estimate=pl.CostEstimate(
            flops=4 * n_c * rows * cols * depth, bytes_accessed=2 * 2**20, transcendentals=0
        ),
        name="share",
    )(grad, act)


def on_device(activations, gradients, basis_act, basis_grad, lengths):
    n_zl, n_y, n_x, n_c, n_zh = (lax.axis_size(a) for a in ("zl", "y", "x", "c", "zh"))
    zl, y, c = (lax.axis_index(a) for a in ("zl", "y", "c"))
    cols, group = basis_act.shape[1], n_x * activations.shape[0]

    def partner(value, step):
        return lax.ppermute(value, "y", [(i, i ^ step) for i in range(n_y)])

    raw = jnp.stack([basis_act, basis_grad])
    raw, activations = lax.optimization_barrier((raw, activations))
    far = shift(raw, "zl", 1)
    tokens = arrange_tokens(n_y // 2, n_x, n_zh, activations, gradients)
    far, tokens = lax.optimization_barrier((far, tokens))
    low = arrange_bases(n_y // 2, n_x, n_c, raw, far)
    low = jnp.stack([low, partner(low, 4)])
    low = jnp.stack([low, partner(low, 2)])
    high = partner(low, 1)
    core_low, core_high = shift(low, "c", 1), shift(high, "c", 1)

    tokens = lax.all_to_all(
        tokens.reshape(n_x * n_zh, *tokens.shape[2:]), ("zh", "x"), 0, 0, tiled=True
    ).reshape(tokens.shape)

    place = jnp.stack([zl, y, c]).astype(jnp.int32)
    arrays = (lengths, tokens, low, high, core_low, core_high)
    partial = rotate(place, *arrays).astype(F16)
    partial = lax.all_to_all(partial, ("c", "x"), 0, 0, tiled=True)
    factors = jnp.exp2(partial[:, None, -TILE:].astype(F32) - F32(TOP))
    partial = partial[:, :-TILE].reshape(n_x * n_c, -1, TILE, partial.shape[2]).astype(F32)
    partial = (partial * factors).reshape(n_c, n_x, *partial.shape[1:])
    rotated = jnp.sum(partial, axis=1).astype(BF16).reshape(n_c, group, -1)
    rot_act, rot_grad = rotated[:, : group // 2], rotated[:, group // 2 :]

    wide_act = lax.all_to_all(
        jnp.broadcast_to(rot_act[None], (n_c * n_x, *rot_act.shape)), ("c", "x"), 0, 0, tiled=True
    ).reshape(n_c, n_x, *rot_act.shape)
    wide_grad = lax.all_gather(rot_grad, "zh", axis=0)
    share = share_of(wide_grad, wide_act).reshape(n_zl * n_y, -1, cols)
    received = lax.all_to_all(share, ("zl", "y"), 0, 0, tiled=True)
    received = received.astype(F32).reshape(SEQS, n_y, -1, cols)
    per_seq = jnp.sum(received, axis=1)
    scale = lengths.astype(F32)[:, None, None]
    return jnp.sum(per_seq * per_seq / scale, axis=0) / F32(SEQS)


def solution(mesh):
    split = Mesh(mesh.devices.reshape(2, 8, 4, 2, 4), ("zl", "y", "x", "c", "zh"))
    spec = P(("zl", "y", "x", "c"), "zh")
    return jax.shard_map(
        on_device, mesh=split, in_specs=(spec, spec, spec, spec, P()), out_specs=spec, check_vma=False
    )
```

```python
import jax
import jax.numpy as jnp
from jax import lax
from jax.experimental import pallas as pl
from jax.experimental.pallas import tpu as pltpu
from jax.sharding import Mesh
from jax.sharding import PartitionSpec as P

SEQS = 2
F32 = jnp.float32
BF16 = jnp.bfloat16
F16 = jnp.float16
TILE = 16
TOP = 15
VMEM = pl.BlockSpec(memory_space=pltpu.VMEM)
SMEM = pl.BlockSpec(memory_space=pltpu.SMEM)


def shift(value, axis, step):
    n = lax.axis_size(axis)
    return lax.ppermute(value, axis, [(i, (i + step) % n) for i in range(n)])


def sorting(width, outer, n_x, inner):
    run = width // (outer * n_x * inner)
    source = lax.broadcasted_iota(jnp.int32, (width, width), 0)
    target = lax.broadcasted_iota(jnp.int32, (width, width), 1)
    at_run, at_inner = source % run, source // run % inner
    at_x, at_outer = source // (run * inner) % n_x, source // (run * inner * n_x)
    moved = ((at_x * inner + at_inner) * outer + at_outer) * run + at_run
    return (moved == target).astype(F32).astype(BF16)


def spread(value, ones):
    return jnp.dot(value, ones, preferred_element_type=F32).astype(BF16)


def bases_kernel(y_lo, n_x, n_c, own, far, out):
    by_owner = sorting(own.shape[2], y_lo, n_x, n_c)
    for i, ref in enumerate((own, far)):
        out[i, 0] = ref[0]
        out[i, 1] = spread(ref[1], by_owner)


def arrange_bases(y_lo, n_x, n_c, own, far):
    return pl.pallas_call(
        lambda *refs: bases_kernel(y_lo, n_x, n_c, *refs),
        out_shape=jax.ShapeDtypeStruct((2, *own.shape), BF16),
        in_specs=[VMEM] * 2,
        out_specs=VMEM,
        compiler_params=pltpu.CompilerParams(vmem_limit_bytes=16 * 2**20),
        cost_estimate=pl.CostEstimate(
            flops=4 * own.shape[1] * own.shape[2] ** 2, bytes_accessed=2**18, transcendentals=0
        ),
        name="arrange_bases",
    )(own, far)


def tokens_kernel(y_lo, act, grad, tokens, held, in_sems, moved, out_sems):
    copies = [
        pltpu.make_async_copy(ref, held.at[i], in_sems.at[i]) for i, ref in enumerate((act, grad))
    ]
    for copy in copies:
        copy.start()
    n_x, n_zh, _, toks, width = tokens.shape
    run = width // y_lo
    sent = []
    for which in range(2):
        copies[which].wait()
        for x in range(n_x):
            runs = [
                held[which, :, (y * n_x + x) * run : (y * n_x + x + 1) * run] for y in range(y_lo)
            ]
            moved[which, x] = jnp.concatenate(runs, axis=1)
            for zh in range(n_zh):
                sent.append(
                    pltpu.make_async_copy(
                        moved.at[which, x], tokens.at[x, zh, which], out_sems.at[which, x, zh]
                    )
                )
                sent[-1].start()
    for copy in sent:
        copy.wait()


def arrange_tokens(y_lo, n_x, n_zh, act, grad):
    toks, feats = act.shape
    return pl.pallas_call(
        lambda *refs: tokens_kernel(y_lo, *refs),
        out_shape=jax.ShapeDtypeStruct((n_x, n_zh, 2, toks, feats // n_x), BF16),
        in_specs=[pl.BlockSpec(memory_space=pl.ANY)] * 2,
        out_specs=pl.BlockSpec(memory_space=pl.ANY),
        scratch_shapes=[
            pltpu.VMEM((2, toks, feats), BF16),
            pltpu.SemaphoreType.DMA((2,)),
            pltpu.VMEM((2, n_x, toks, feats // n_x), BF16),
            pltpu.SemaphoreType.DMA((2, n_x, n_zh)),
        ],
        compiler_params=pltpu.CompilerParams(vmem_limit_bytes=60 * 2**20),
        cost_estimate=pl.CostEstimate(
            flops=toks * feats, bytes_accessed=2**20, transcendentals=0
        ),
        name="arrange_tokens",
    )(act, grad)


def rotate_kernel(place, lengths, tokens, low, high, core_low, core_high, out, whole):
    n_x, n_zh, _, toks, width = tokens.shape
    rows, cols = low.shape[4], low.shape[5]
    group, part = n_x * toks, cols // n_x
    zl, y, c = place[0], place[1], place[2]
    sums = []
    for which in range(2):
        for one, pair in enumerate(((low, core_low), (high, core_high))):
            for two in range(2):
                for four in range(2):
                    from_y = y ^ (four * 4 + two * 2 + one)
                    for far in range(2):
                        owner = (zl ^ far) * 2 + from_y // 4
                        for ref, core in zip(pair, (c, 1 - c)):
                            at = pl.multiple_of((from_y % 4 * 2 + core) * rows, rows)
                            whole[which, owner, pl.ds(at, rows)] = ref[two, four, far, which]
        total = None
        for owner in range(n_zh):
            left = tokens[:, owner, which].reshape(group, width)
            product = jnp.dot(left, whole[which, owner], preferred_element_type=F32)
            total = product if total is None else total + product
        sums.append(total)
    index = lax.broadcasted_iota(jnp.int32, (group, 1), 0)
    position = ((y * n_x + index // toks) * 2 + c) * toks + index % toks
    sums[0] = jnp.where(position < lengths[zl], sums[0], 0.0)
    largest = jnp.max(jnp.maximum(jnp.abs(sums[0]), jnp.abs(sums[1])), axis=0, keepdims=True)
    largest = jnp.max(largest, axis=1, keepdims=True)
    level = jnp.clip(jnp.ceil(jnp.log2(jnp.maximum(largest, 1e-30))), -100.0, 100.0)
    act, grad = (total * jnp.exp2(F32(TOP) - level) for total in sums)
    half = group // 2
    for x in range(n_x):
        for core in range(2):
            piece, to = 2 * x + core, core * n_x + x
            out[to, pl.ds(0, half)] = act[core * half : (core + 1) * half, x * part : (x + 1) * part]
            value = grad[:, piece * part // 2 : (piece + 1) * part // 2]
            out[to, pl.ds(half, half)] = jnp.concatenate([value[:half], value[half:]], axis=1)
            out[to, pl.ds(group, TILE)] = jnp.broadcast_to(level, (TILE, part))


def rotate(place, lengths, *arrays):
    n_x, n_zh, _, toks, width = arrays[0].shape
    cols = arrays[1].shape[5]
    return pl.pallas_call(
        rotate_kernel,
        out_shape=jax.ShapeDtypeStruct((2 * n_x, n_x * toks + TILE, cols // n_x), F32),
        in_specs=[SMEM] * 2 + [VMEM] * len(arrays),
        out_specs=VMEM,
        scratch_shapes=[pltpu.VMEM((2, n_zh, width, cols), BF16)],
        compiler_params=pltpu.CompilerParams(vmem_limit_bytes=40 * 2**20),
        cost_estimate=pl.CostEstimate(
            flops=4 * n_x * n_zh * toks * width * cols, bytes_accessed=8 * 2**20, transcendentals=0
        ),
        name="rotate",
    )(place, lengths, *arrays)


def share_kernel(grad, act, out):
    n_k, n_c, depth, part = grad.shape
    n_x, half = act.shape[1], part // 2
    total = None
    for core in range(n_c):
        turned = [grad[k, core].T for k in range(n_k)]
        for side in range(2):
            left = jnp.concatenate([t[side * half : (side + 1) * half] for t in turned], axis=0)
            right = jnp.concatenate([act[side, x, core] for x in range(n_x)], axis=1)
            product = jnp.dot(left, right, preferred_element_type=F32)
            total = product if total is None else total + product
    out[...] = total.astype(BF16)


def share_of(grad, act):
    n_k, n_c, depth, part = grad.shape
    rows, cols = n_k * part // 2, act.shape[1] * part
    return pl.pallas_call(
        share_kernel,
        out_shape=jax.ShapeDtypeStruct((rows, cols), BF16),
        in_specs=[VMEM, VMEM],
        out_specs=VMEM,
        compiler_params=pltpu.CompilerParams(vmem_limit_bytes=16 * 2**20),
        cost_estimate=pl.CostEstimate(
            flops=4 * n_c * rows * cols * depth, bytes_accessed=2 * 2**20, transcendentals=0
        ),
        name="share",
    )(grad, act)


def on_device(activations, gradients, basis_act, basis_grad, lengths):
    n_zl, n_y, n_x, n_c, n_zh = (lax.axis_size(a) for a in ("zl", "y", "x", "c", "zh"))
    zl, y, c = (lax.axis_index(a) for a in ("zl", "y", "c"))
    cols, group = basis_act.shape[1], n_x * activations.shape[0]

    def partner(value, step):
        return lax.ppermute(value, "y", [(i, i ^ step) for i in range(n_y)])

    raw = jnp.stack([basis_act, basis_grad])
    raw, activations = lax.optimization_barrier((raw, activations))
    far = shift(raw, "zl", 1)
    tokens = arrange_tokens(n_y // 2, n_x, n_zh, activations, gradients)
    far, tokens = lax.optimization_barrier((far, tokens))
    low = arrange_bases(n_y // 2, n_x, n_c, raw, far)
    low = jnp.stack([low, partner(low, 4)])
    low = jnp.stack([low, partner(low, 2)])
    high = partner(low, 1)
    core_low, core_high = shift(low, "c", 1), shift(high, "c", 1)

    tokens = lax.all_to_all(
        tokens.reshape(n_x * n_zh, *tokens.shape[2:]), ("x", "zh"), 0, 0, tiled=True
    ).reshape(tokens.shape)

    place = jnp.stack([zl, y, c]).astype(jnp.int32)
    arrays = (lengths, tokens, low, high, core_low, core_high)
    partial = rotate(place, *arrays).astype(F16)
    partial = lax.all_to_all(partial, ("c", "x"), 0, 0, tiled=True)
    factors = jnp.exp2(partial[:, None, -TILE:].astype(F32) - F32(TOP))
    partial = partial[:, :-TILE].reshape(n_x * n_c, -1, TILE, partial.shape[2]).astype(F32)
    partial = (partial * factors).reshape(n_c, n_x, *partial.shape[1:])
    rotated = jnp.sum(partial, axis=1).astype(BF16).reshape(n_c, group, -1)
    rot_act, rot_grad = rotated[:, : group // 2], rotated[:, group // 2 :]

    wide_act = lax.all_to_all(
        jnp.broadcast_to(rot_act[None], (n_c * n_x, *rot_act.shape)), ("c", "x"), 0, 0, tiled=True
    ).reshape(n_c, n_x, *rot_act.shape)
    wide_grad = lax.all_gather(rot_grad, "zh", axis=0)
    share = share_of(wide_grad, wide_act).reshape(n_zl * n_y, -1, cols)
    received = lax.all_to_all(share, ("zl", "y"), 0, 0, tiled=True)
    received = received.astype(F32).reshape(SEQS, n_y, -1, cols)
    per_seq = jnp.sum(received, axis=1)
    scale = lengths.astype(F32)[:, None, None]
    return jnp.sum(per_seq * per_seq / scale, axis=0) / F32(SEQS)


def solution(mesh):
    split = Mesh(mesh.devices.reshape(2, 8, 4, 2, 4), ("zl", "y", "x", "c", "zh"))
    spec = P(("zl", "y", "x", "c"), "zh")
    return jax.shard_map(
        on_device, mesh=split, in_specs=(spec, spec, spec, spec, P()), out_specs=spec, check_vma=False
    )
```

```python
import jax
import jax.numpy as jnp
from jax import lax
from jax.experimental import pallas as pl
from jax.experimental.pallas import tpu as pltpu
from jax.sharding import Mesh
from jax.sharding import PartitionSpec as P

SEQS = 2
F32 = jnp.float32
BF16 = jnp.bfloat16
F16 = jnp.float16
TILE = 16
TOP = 15
VMEM = pl.BlockSpec(memory_space=pltpu.VMEM)
SMEM = pl.BlockSpec(memory_space=pltpu.SMEM)


def shift(value, axis, step):
    n = lax.axis_size(axis)
    return lax.ppermute(value, axis, [(i, (i + step) % n) for i in range(n)])


def sorting(width, outer, n_x, inner):
    run = width // (outer * n_x * inner)
    source = lax.broadcasted_iota(jnp.int32, (width, width), 0)
    target = lax.broadcasted_iota(jnp.int32, (width, width), 1)
    at_run, at_inner = source % run, source // run % inner
    at_x, at_outer = source // (run * inner) % n_x, source // (run * inner * n_x)
    moved = ((at_x * inner + at_inner) * outer + at_outer) * run + at_run
    return (moved == target).astype(F32).astype(BF16)


def spread(value, ones):
    return jnp.dot(value, ones, preferred_element_type=F32).astype(BF16)


def bases_kernel(y_lo, n_x, n_c, own, far, out):
    by_owner = sorting(own.shape[2], y_lo, n_x, n_c)
    for i, ref in enumerate((own, far)):
        out[i, 0] = ref[0]
        out[i, 1] = spread(ref[1], by_owner)


def arrange_bases(y_lo, n_x, n_c, own, far):
    return pl.pallas_call(
        lambda *refs: bases_kernel(y_lo, n_x, n_c, *refs),
        out_shape=jax.ShapeDtypeStruct((2, *own.shape), BF16),
        in_specs=[VMEM] * 2,
        out_specs=VMEM,
        compiler_params=pltpu.CompilerParams(vmem_limit_bytes=16 * 2**20),
        cost_estimate=pl.CostEstimate(
            flops=4 * own.shape[1] * own.shape[2] ** 2, bytes_accessed=2**18, transcendentals=0
        ),
        name="arrange_bases",
    )(own, far)


def tokens_kernel(y_lo, act, grad, tokens, held, in_sems, moved, out_sems):
    copies = [
        pltpu.make_async_copy(ref, held.at[i], in_sems.at[i]) for i, ref in enumerate((act, grad))
    ]
    for copy in copies:
        copy.start()
    n_x, n_zh, _, toks, width = tokens.shape
    run = width // y_lo
    sent = []
    for which in range(2):
        copies[which].wait()
        for x in range(n_x):
            runs = [
                held[which, :, (y * n_x + x) * run : (y * n_x + x + 1) * run] for y in range(y_lo)
            ]
            moved[which, x] = jnp.concatenate(runs, axis=1)
            for zh in range(n_zh):
                sent.append(
                    pltpu.make_async_copy(
                        moved.at[which, x], tokens.at[x, zh, which], out_sems.at[which, x, zh]
                    )
                )
                sent[-1].start()
    for copy in sent:
        copy.wait()


def arrange_tokens(y_lo, n_x, n_zh, act, grad):
    toks, feats = act.shape
    return pl.pallas_call(
        lambda *refs: tokens_kernel(y_lo, *refs),
        out_shape=jax.ShapeDtypeStruct((n_x, n_zh, 2, toks, feats // n_x), BF16),
        in_specs=[pl.BlockSpec(memory_space=pl.ANY)] * 2,
        out_specs=pl.BlockSpec(memory_space=pl.ANY),
        scratch_shapes=[
            pltpu.VMEM((2, toks, feats), BF16),
            pltpu.SemaphoreType.DMA((2,)),
            pltpu.VMEM((2, n_x, toks, feats // n_x), BF16),
            pltpu.SemaphoreType.DMA((2, n_x, n_zh)),
        ],
        compiler_params=pltpu.CompilerParams(vmem_limit_bytes=60 * 2**20),
        cost_estimate=pl.CostEstimate(
            flops=toks * feats, bytes_accessed=2**20, transcendentals=0
        ),
        name="arrange_tokens",
    )(act, grad)


def rotate_kernel(place, lengths, tokens, low, high, core_low, core_high, out, *wholes):
    n_x, n_zh, _, toks, width = tokens.shape
    rows, cols = low.shape[4], low.shape[5]
    group, part = n_x * toks, cols // n_x
    zl, y, c = place[0], place[1], place[2]
    for which, whole in enumerate(wholes):
        for one, pair in enumerate(((low, core_low), (high, core_high))):
            for two in range(2):
                for four in range(2):
                    from_y = y ^ (four * 4 + two * 2 + one)
                    for far in range(2):
                        owner = (zl ^ far) * 2 + from_y // 4
                        for ref, core in zip(pair, (c, 1 - c)):
                            at = pl.multiple_of((from_y % 4 * 2 + core) * rows, rows)
                            whole[owner, pl.ds(at, rows)] = ref[two, four, far, which]
    sums = []
    for which, whole in enumerate(wholes):
        total = None
        for owner in range(n_zh):
            left = tokens[:, owner, which].reshape(group, width)
            product = jnp.dot(left, whole[owner], preferred_element_type=F32)
            total = product if total is None else total + product
        sums.append(total)
    index = lax.broadcasted_iota(jnp.int32, (group, 1), 0)
    position = ((y * n_x + index // toks) * 2 + c) * toks + index % toks
    sums[0] = jnp.where(position < lengths[zl], sums[0], 0.0)
    largest = jnp.max(jnp.maximum(jnp.abs(sums[0]), jnp.abs(sums[1])), axis=0, keepdims=True)
    largest = jnp.max(largest, axis=1, keepdims=True)
    level = jnp.clip(jnp.ceil(jnp.log2(jnp.maximum(largest, 1e-30))), -100.0, 100.0)
    act, grad = (total * jnp.exp2(F32(TOP) - level) for total in sums)
    half = group // 2
    for x in range(n_x):
        for core in range(2):
            piece, to = 2 * x + core, core * n_x + x
            out[to, pl.ds(0, half)] = act[core * half : (core + 1) * half, x * part : (x + 1) * part]
            value = grad[:, piece * part // 2 : (piece + 1) * part // 2]
            out[to, pl.ds(half, half)] = jnp.concatenate([value[:half], value[half:]], axis=1)
            out[to, pl.ds(group, TILE)] = jnp.broadcast_to(level, (TILE, part))


def rotate(place, lengths, *arrays):
    n_x, n_zh, _, toks, width = arrays[0].shape
    cols = arrays[1].shape[5]
    return pl.pallas_call(
        rotate_kernel,
        out_shape=jax.ShapeDtypeStruct((2 * n_x, n_x * toks + TILE, cols // n_x), F32),
        in_specs=[SMEM] * 2 + [VMEM] * len(arrays),
        out_specs=VMEM,
        scratch_shapes=[pltpu.VMEM((n_zh, width, cols), BF16)] * 2,
        compiler_params=pltpu.CompilerParams(vmem_limit_bytes=40 * 2**20),
        cost_estimate=pl.CostEstimate(
            flops=4 * n_x * n_zh * toks * width * cols, bytes_accessed=8 * 2**20, transcendentals=0
        ),
        name="rotate",
    )(place, lengths, *arrays)


def share_kernel(grad, act, out):
    n_k, n_c, depth, part = grad.shape
    n_x, half = act.shape[1], part // 2
    total = None
    for core in range(n_c):
        turned = [grad[k, core].T for k in range(n_k)]
        for side in range(2):
            left = jnp.concatenate([t[side * half : (side + 1) * half] for t in turned], axis=0)
            right = jnp.concatenate([act[side, x, core] for x in range(n_x)], axis=1)
            product = jnp.dot(left, right, preferred_element_type=F32)
            total = product if total is None else total + product
    out[...] = total.astype(BF16)


def share_of(grad, act):
    n_k, n_c, depth, part = grad.shape
    rows, cols = n_k * part // 2, act.shape[1] * part
    return pl.pallas_call(
        share_kernel,
        out_shape=jax.ShapeDtypeStruct((rows, cols), BF16),
        in_specs=[VMEM, VMEM],
        out_specs=VMEM,
        compiler_params=pltpu.CompilerParams(vmem_limit_bytes=16 * 2**20),
        cost_estimate=pl.CostEstimate(
            flops=4 * n_c * rows * cols * depth, bytes_accessed=2 * 2**20, transcendentals=0
        ),
        name="share",
    )(grad, act)


def on_device(activations, gradients, basis_act, basis_grad, lengths):
    n_zl, n_y, n_x, n_c, n_zh = (lax.axis_size(a) for a in ("zl", "y", "x", "c", "zh"))
    zl, y, c = (lax.axis_index(a) for a in ("zl", "y", "c"))
    cols, group = basis_act.shape[1], n_x * activations.shape[0]

    def partner(value, step):
        return lax.ppermute(value, "y", [(i, i ^ step) for i in range(n_y)])

    raw = jnp.stack([basis_act, basis_grad])
    raw, activations = lax.optimization_barrier((raw, activations))
    far = shift(raw, "zl", 1)
    tokens = arrange_tokens(n_y // 2, n_x, n_zh, activations, gradients)
    far, tokens = lax.optimization_barrier((far, tokens))
    low = arrange_bases(n_y // 2, n_x, n_c, raw, far)
    low = jnp.stack([low, partner(low, 4)])
    low = jnp.stack([low, partner(low, 2)])
    high = partner(low, 1)
    core_low, core_high = shift(low, "c", 1), shift(high, "c", 1)

    tokens = lax.all_to_all(
        tokens.reshape(n_x * n_zh, *tokens.shape[2:]), ("x", "zh"), 0, 0, tiled=True
    ).reshape(tokens.shape)

    place = jnp.stack([zl, y, c]).astype(jnp.int32)
    arrays = (lengths, tokens, low, high, core_low, core_high)
    partial = rotate(place, *arrays).astype(F16)
    partial = lax.all_to_all(partial, ("c", "x"), 0, 0, tiled=True)
    factors = jnp.exp2(partial[:, None, -TILE:].astype(F32) - F32(TOP))
    partial = partial[:, :-TILE].reshape(n_x * n_c, -1, TILE, partial.shape[2]).astype(F32)
    partial = (partial * factors).reshape(n_c, n_x, *partial.shape[1:])
    rotated = jnp.sum(partial, axis=1).astype(BF16).reshape(n_c, group, -1)
    rot_act, rot_grad = rotated[:, : group // 2], rotated[:, group // 2 :]

    wide_act = lax.all_to_all(
        jnp.broadcast_to(rot_act[None], (n_c * n_x, *rot_act.shape)), ("c", "x"), 0, 0, tiled=True
    ).reshape(n_c, n_x, *rot_act.shape)
    wide_grad = lax.all_gather(rot_grad, "zh", axis=0)
    share = share_of(wide_grad, wide_act).reshape(n_zl * n_y, -1, cols)
    received = lax.all_to_all(share, ("zl", "y"), 0, 0, tiled=True)
    received = received.astype(F32).reshape(SEQS, n_y, -1, cols)
    per_seq = jnp.sum(received, axis=1)
    scale = lengths.astype(F32)[:, None, None]
    return jnp.sum(per_seq * per_seq / scale, axis=0) / F32(SEQS)


def solution(mesh):
    split = Mesh(mesh.devices.reshape(2, 8, 4, 2, 4), ("zl", "y", "x", "c", "zh"))
    spec = P(("zl", "y", "x", "c"), "zh")
    return jax.shard_map(
        on_device, mesh=split, in_specs=(spec, spec, spec, spec, P()), out_specs=spec, check_vma=False
    )
```

```python
import jax
import jax.numpy as jnp
from jax import lax
from jax.experimental import pallas as pl
from jax.experimental.pallas import tpu as pltpu
from jax.sharding import Mesh
from jax.sharding import PartitionSpec as P

SEQS = 2
F32 = jnp.float32
BF16 = jnp.bfloat16
F16 = jnp.float16
TILE = 16
TOP = 15
VMEM = pl.BlockSpec(memory_space=pltpu.VMEM)
SMEM = pl.BlockSpec(memory_space=pltpu.SMEM)


def shift(value, axis, step):
    n = lax.axis_size(axis)
    return lax.ppermute(value, axis, [(i, (i + step) % n) for i in range(n)])


def sorting(width, outer, n_x, inner):
    run = width // (outer * n_x * inner)
    source = lax.broadcasted_iota(jnp.int32, (width, width), 0)
    target = lax.broadcasted_iota(jnp.int32, (width, width), 1)
    at_run, at_inner = source % run, source // run % inner
    at_x, at_outer = source // (run * inner) % n_x, source // (run * inner * n_x)
    moved = ((at_x * inner + at_inner) * outer + at_outer) * run + at_run
    return (moved == target).astype(F32).astype(BF16)


def spread(value, ones):
    return jnp.dot(value, ones, preferred_element_type=F32).astype(BF16)


def bases_kernel(y_lo, n_x, n_c, own, far, out):
    by_owner = sorting(own.shape[2], y_lo, n_x, n_c)
    for i, ref in enumerate((own, far)):
        out[i, 0] = ref[0]
        out[i, 1] = spread(ref[1], by_owner)


def arrange_bases(y_lo, n_x, n_c, own, far):
    return pl.pallas_call(
        lambda *refs: bases_kernel(y_lo, n_x, n_c, *refs),
        out_shape=jax.ShapeDtypeStruct((2, *own.shape), BF16),
        in_specs=[VMEM] * 2,
        out_specs=VMEM,
        compiler_params=pltpu.CompilerParams(vmem_limit_bytes=16 * 2**20),
        cost_estimate=pl.CostEstimate(
            flops=4 * own.shape[1] * own.shape[2] ** 2, bytes_accessed=2**18, transcendentals=0
        ),
        name="arrange_bases",
    )(own, far)


def tokens_kernel(y_lo, act, grad, tokens, held, in_sems, moved, out_sems):
    copies = [
        pltpu.make_async_copy(ref, held.at[i], in_sems.at[i]) for i, ref in enumerate((act, grad))
    ]
    for copy in copies:
        copy.start()
    n_x, n_zh, _, toks, width = tokens.shape
    run = width // y_lo
    sent = []
    for which in range(2):
        copies[which].wait()
        for x in range(n_x):
            runs = [
                held[which, :, (y * n_x + x) * run : (y * n_x + x + 1) * run] for y in range(y_lo)
            ]
            moved[which, x] = jnp.concatenate(runs, axis=1)
            for zh in range(n_zh):
                sent.append(
                    pltpu.make_async_copy(
                        moved.at[which, x], tokens.at[x, zh, which], out_sems.at[which, x, zh]
                    )
                )
                sent[-1].start()
    for copy in sent:
        copy.wait()


def arrange_tokens(y_lo, n_x, n_zh, act, grad):
    toks, feats = act.shape
    return pl.pallas_call(
        lambda *refs: tokens_kernel(y_lo, *refs),
        out_shape=jax.ShapeDtypeStruct((n_x, n_zh, 2, toks, feats // n_x), BF16),
        in_specs=[pl.BlockSpec(memory_space=pl.ANY)] * 2,
        out_specs=pl.BlockSpec(memory_space=pl.ANY),
        scratch_shapes=[
            pltpu.VMEM((2, toks, feats), BF16),
            pltpu.SemaphoreType.DMA((2,)),
            pltpu.VMEM((2, n_x, toks, feats // n_x), BF16),
            pltpu.SemaphoreType.DMA((2, n_x, n_zh)),
        ],
        compiler_params=pltpu.CompilerParams(vmem_limit_bytes=60 * 2**20),
        cost_estimate=pl.CostEstimate(
            flops=toks * feats, bytes_accessed=2**20, transcendentals=0
        ),
        name="arrange_tokens",
    )(act, grad)


def rotate_kernel(place, lengths, tokens, low, high, core_low, core_high, out, *wholes):
    n_x, n_zh, _, toks, width = tokens.shape
    rows, cols = low.shape[4], low.shape[5]
    group, part = n_x * toks, cols // n_x
    zl, y, c = place[0], place[1], place[2]
    for which, whole in enumerate(wholes):
        for one, pair in enumerate(((low, core_low), (high, core_high))):
            for two in range(2):
                for four in range(2):
                    from_y = y ^ (four * 4 + two * 2 + one)
                    for far in range(2):
                        owner = (zl ^ far) * 2 + from_y // 4
                        for ref, core in zip(pair, (c, 1 - c)):
                            at = pl.multiple_of((from_y % 4 * 2 + core) * rows, rows)
                            whole[owner, pl.ds(at, rows)] = ref[two, four, far, which]
    sums = []
    for which, whole in enumerate(wholes):
        total = None
        for owner in range(n_zh):
            left = tokens[:, owner, which].reshape(group, width)
            product = jnp.dot(left, whole[owner], preferred_element_type=F32)
            total = product if total is None else total + product
        sums.append(total)
    index = lax.broadcasted_iota(jnp.int32, (group, 1), 0)
    position = ((y * n_x + index // toks) * 2 + c) * toks + index % toks
    sums[0] = jnp.where(position < lengths[zl], sums[0], 0.0)
    largest = jnp.max(jnp.maximum(jnp.abs(sums[0]), jnp.abs(sums[1])), axis=0, keepdims=True)
    largest = jnp.max(largest, axis=1, keepdims=True)
    level = jnp.clip(jnp.ceil(jnp.log2(jnp.maximum(largest, 1e-30))), -100.0, 100.0)
    act, grad = (total * jnp.exp2(F32(TOP) - level) for total in sums)
    half = group // 2
    for x in range(n_x):
        for core in range(2):
            piece, to = 2 * x + core, core * n_x + x
            out[to, pl.ds(0, half)] = act[core * half : (core + 1) * half, x * part : (x + 1) * part]
            value = grad[:, piece * part // 2 : (piece + 1) * part // 2]
            out[to, pl.ds(half, half)] = jnp.concatenate([value[:half], value[half:]], axis=1)
            out[to, pl.ds(group, TILE)] = jnp.broadcast_to(level, (TILE, part))


def rotate(place, lengths, *arrays):
    n_x, n_zh, _, toks, width = arrays[0].shape
    cols = arrays[1].shape[5]
    return pl.pallas_call(
        rotate_kernel,
        out_shape=jax.ShapeDtypeStruct((2 * n_x, n_x * toks + TILE, cols // n_x), F32),
        in_specs=[SMEM] * 2 + [VMEM] * len(arrays),
        out_specs=VMEM,
        scratch_shapes=[pltpu.VMEM((n_zh, width, cols), BF16)] * 2,
        compiler_params=pltpu.CompilerParams(vmem_limit_bytes=40 * 2**20),
        cost_estimate=pl.CostEstimate(
            flops=4 * n_x * n_zh * toks * width * cols, bytes_accessed=8 * 2**20, transcendentals=0
        ),
        name="rotate",
    )(place, lengths, *arrays)


def share_kernel(grad, act, out):
    n_k, n_c, depth, part = grad.shape
    n_x, half = act.shape[1], part // 2
    total = None
    for core in range(n_c):
        turned = [grad[k, core].T for k in range(n_k)]
        for side in range(2):
            left = jnp.concatenate([t[side * half : (side + 1) * half] for t in turned], axis=0)
            right = jnp.concatenate([act[side, x, core] for x in range(n_x)], axis=1)
            product = jnp.dot(left, right, preferred_element_type=F32)
            total = product if total is None else total + product
    out[...] = total.astype(BF16)


def share_of(grad, act):
    n_k, n_c, depth, part = grad.shape
    rows, cols = n_k * part // 2, act.shape[1] * part
    return pl.pallas_call(
        share_kernel,
        out_shape=jax.ShapeDtypeStruct((rows, cols), BF16),
        in_specs=[VMEM, VMEM],
        out_specs=VMEM,
        compiler_params=pltpu.CompilerParams(vmem_limit_bytes=16 * 2**20),
        cost_estimate=pl.CostEstimate(
            flops=4 * n_c * rows * cols * depth, bytes_accessed=2 * 2**20, transcendentals=0
        ),
        name="share",
    )(grad, act)


def copies_kernel(value, out, sems):
    copies = [pltpu.make_async_copy(value, out.at[i], sems.at[i]) for i in range(out.shape[0])]
    for copy in copies:
        copy.start()
    for copy in copies:
        copy.wait()


def copies_of(value, count):
    return pl.pallas_call(
        copies_kernel,
        out_shape=jax.ShapeDtypeStruct((count, *value.shape), value.dtype),
        in_specs=[VMEM],
        out_specs=pl.BlockSpec(memory_space=pl.ANY),
        scratch_shapes=[pltpu.SemaphoreType.DMA((count,))],
        compiler_params=pltpu.CompilerParams(vmem_limit_bytes=16 * 2**20),
        cost_estimate=pl.CostEstimate(flops=0, bytes_accessed=2**20, transcendentals=0),
        name="copies",
    )(value)


def on_device(activations, gradients, basis_act, basis_grad, lengths):
    n_zl, n_y, n_x, n_c, n_zh = (lax.axis_size(a) for a in ("zl", "y", "x", "c", "zh"))
    zl, y, c = (lax.axis_index(a) for a in ("zl", "y", "c"))
    cols, group = basis_act.shape[1], n_x * activations.shape[0]

    def partner(value, step):
        return lax.ppermute(value, "y", [(i, i ^ step) for i in range(n_y)])

    raw = jnp.stack([basis_act, basis_grad])
    raw, activations = lax.optimization_barrier((raw, activations))
    far = shift(raw, "zl", 1)
    tokens = arrange_tokens(n_y // 2, n_x, n_zh, activations, gradients)
    far, tokens = lax.optimization_barrier((far, tokens))
    low = arrange_bases(n_y // 2, n_x, n_c, raw, far)
    low = jnp.stack([low, partner(low, 4)])
    low = jnp.stack([low, partner(low, 2)])
    high = partner(low, 1)
    core_low, core_high = shift(low, "c", 1), shift(high, "c", 1)

    tokens = lax.all_to_all(
        tokens.reshape(n_x * n_zh, *tokens.shape[2:]), ("x", "zh"), 0, 0, tiled=True
    ).reshape(tokens.shape)

    place = jnp.stack([zl, y, c]).astype(jnp.int32)
    arrays = (lengths, tokens, low, high, core_low, core_high)
    partial = rotate(place, *arrays).astype(F16)
    partial = lax.all_to_all(partial, ("c", "x"), 0, 0, tiled=True)
    factors = jnp.exp2(partial[:, None, -TILE:].astype(F32) - F32(TOP))
    partial = partial[:, :-TILE].reshape(n_x * n_c, -1, TILE, partial.shape[2]).astype(F32)
    partial = (partial * factors).reshape(n_c, n_x, *partial.shape[1:])
    rotated = jnp.sum(partial, axis=1).astype(BF16).reshape(n_c, group, -1)
    rot_act, rot_grad = rotated[:, : group // 2], rotated[:, group // 2 :]

    wide_act = lax.all_to_all(
        copies_of(rot_act, n_c * n_x), ("c", "x"), 0, 0, tiled=True
    ).reshape(n_c, n_x, *rot_act.shape)
    wide_grad = lax.all_gather(rot_grad, "zh", axis=0)
    share = share_of(wide_grad, wide_act).reshape(n_zl * n_y, -1, cols)
    received = lax.all_to_all(share, ("zl", "y"), 0, 0, tiled=True)
    received = received.astype(F32).reshape(SEQS, n_y, -1, cols)
    per_seq = jnp.sum(received, axis=1)
    scale = lengths.astype(F32)[:, None, None]
    return jnp.sum(per_seq * per_seq / scale, axis=0) / F32(SEQS)


def solution(mesh):
    split = Mesh(mesh.devices.reshape(2, 8, 4, 2, 4), ("zl", "y", "x", "c", "zh"))
    spec = P(("zl", "y", "x", "c"), "zh")
    return jax.shard_map(
        on_device, mesh=split, in_specs=(spec, spec, spec, spec, P()), out_specs=spec, check_vma=False
    )
```
